32 devices in a mesh: grp: 2 (over y), gx: 16 (over z, x, core).
Axes of the slice: x: 2, y: 2, z: 4, core: 2. Of those that a mesh axis runs over, the one named last changes fastest.
Arguments:
- features: bfloat16 [128, 32, 64, 128], P('grp', 'gx'), parts along dimension 0, may hold values from -6 to 6
- cotangent: bfloat16 [128, 32, 64, 128], P('grp', 'gx'), parts along dimension 0, may hold values from -6 to 6
- spectral_weight: bfloat16 [16384, 64, 128], P('gx'), may hold values from -0.5 to 0.5
- channel_weight: bfloat16 [64, 64], replicated, may hold values from -0.75 to 0.75
- channel_bias: float32 [64], replicated, may hold values from -3 to 3
Outputs:
- activated: bfloat16 [128, 32, 64, 128], P('grp', 'gx'), parts along dimension 0
- feature_grad: bfloat16 [128, 32, 64, 128], P('grp', 'gx'), parts along dimension 0
- spectral_grad: bfloat16 [32768, 64, 128], P(('grp', 'gx')), parts along dimension 0
The draws below stay inside these ranges and needn't reach their ends.
There are 2 independent parts, one for each index of `grp`. The reference program is written for one: setup_inputs(seed, part) draws one part's arguments, and reference() takes and returns one part's arrays. A program takes and returns all parts, laid end to end along the dimension named above; an argument that names none is the same for every part. Nothing has to cross between parts.
All inputs are finite; a program needn't handle non-finite values.
Results may differ from the reference program's by a relative error of at most 0.018.
Values may be sent and summed in bfloat16 or wider, within the bound.
A program may use at most 192 MiB of HBM per device.

```python
import math
import jax
import jax.numpy as jnp

C = 64
MX = 32
MY = 32
MZ = 16
NZ = 128
NY = 64
NX = 32
MODES = 16384


def level_of(stream_key, extent, shards, low, largest):
    def one(axis_at, shards_of):
        heights = jax.random.uniform(jax.random.fold_in(jax.random.fold_in(stream_key, 6), axis_at), (shards_of,), jnp.float32, low / len(shards), largest / len(shards))
        return jnp.repeat(jnp.exp(heights), extent[axis_at] // shards_of).reshape((-1,) + (1,) * (len(extent) - axis_at - 1))

    factor_of = one(*shards[0])
    for cut in shards[1:]:
        factor_of = factor_of * one(*cut)
    return factor_of


def noise(own_key, dims, scale, most, split=(), held_as=jnp.bfloat16):
    result = scale * jax.random.normal(own_key, dims, jnp.float32)
    if split:
        result = result * level_of(own_key, dims, split, -0.22, 0.18)
    return jnp.clip(result, -most, most).astype(held_as)


def setup_inputs(seed: int = 0, part: int = 0) -> dict:
    streams_of = jax.random.split(jax.random.key(seed), 6)
    own_keys = jax.random.split(jax.random.fold_in(streams_of[5], part), 6)
    return {
        "features": noise(own_keys[0], (C, NX, NY, NZ), 1.0, 6.0, ((1, 16),)),
        "cotangent": noise(own_keys[1], (C, NX, NY, NZ), 1.0, 6.0, ((1, 16),)),
        "spectral_weight": noise(streams_of[2], (MODES, C, 2 * C), (2 * C) ** -0.5, 0.5, ((0, 16),)),
        "channel_weight": noise(streams_of[3], (C, C), C ** -0.5, 0.75),
        "channel_bias": noise(streams_of[4], (C,), 0.5, 3.0, (), jnp.float32),
    }


SQRT_TWO_PI = math.sqrt(2.0 / math.pi)
CUBIC_COEF = 0.044715

def freq_index(retained, length):
    ladder = jnp.arange(retained, dtype=jnp.int32)
    return jnp.where(ladder < retained // 2, ladder, length - retained + ladder).astype(jnp.int32)

def cos_sin(wavenum, length):
    points = jnp.arange(length, dtype=jnp.int32)
    angles = (wavenum[:, None] * points[None, :] % length).astype(jnp.float32) * (2.0 * math.pi / length)
    return (jnp.cos(angles), jnp.sin(angles))

def analysis_pair(wavenum, length):
    cosine, sine_wave = cos_sin(wavenum, length)
    cosine, sine_wave = (cosine.T, sine_wave.T)
    return jnp.stack([jnp.stack([cosine, -sine_wave], 1), jnp.stack([sine_wave, cosine], 1)], 1).astype(jnp.bfloat16)

def synthesis_pair(wavenum, length):
    cosine, sine_wave = cos_sin(wavenum, length)
    return jnp.stack([jnp.stack([cosine, sine_wave], 1), jnp.stack([-sine_wave, cosine], 1)], 1).astype(jnp.bfloat16)

def depth_table(retained, length):
    cosine, sine_wave = cos_sin(jnp.arange(retained, dtype=jnp.int32), length)
    return jnp.concatenate([cosine, -sine_wave], 0).astype(jnp.bfloat16)

def gelu_parts(inputs):
    cubed_in = inputs * inputs * inputs
    tangent = jnp.tanh(SQRT_TWO_PI * (inputs + CUBIC_COEF * cubed_in))
    output = 0.5 * inputs * (1.0 + tangent)
    derivative = 0.5 * (1.0 + tangent) + 0.5 * inputs * (1.0 - tangent * tangent) * SQRT_TWO_PI * (1.0 + 3.0 * CUBIC_COEF * inputs * inputs)
    return (output, derivative)

def mode_product(coeffs, weights, channels):
    stacked = coeffs.reshape(coeffs.shape[0], 2, channels).astype(jnp.float32)
    halves = jnp.einsum('mac,mcj->amj', stacked, weights.astype(jnp.float32))
    real_out = halves[0, :, :channels] - halves[1, :, channels:]
    imag_out = halves[0, :, channels:] + halves[1, :, :channels]
    return jnp.concatenate([real_out, imag_out], 1).astype(jnp.bfloat16)

def mode_grads(coeffs, weights, grad_modes, channels, weight_scale, input_scale):
    number = coeffs.shape[0]
    stacked = coeffs.reshape(number, 2, channels).astype(jnp.float32)
    grad_pairs = grad_modes.reshape(number, 2, channels).astype(jnp.float32)
    real_w = jnp.einsum('mac,mao->mco', stacked, grad_pairs)
    imag_w = jnp.einsum('mc,mo->mco', stacked[:, 0], grad_pairs[:, 1]) - jnp.einsum('mc,mo->mco', stacked[:, 1], grad_pairs[:, 0])
    weight_grad = (jnp.concatenate([real_w, imag_w], 2) * weight_scale).astype(jnp.bfloat16)
    straight = jnp.concatenate([grad_pairs[:, 0], grad_pairs[:, 1]], 1)
    rotated = jnp.concatenate([grad_pairs[:, 1], -grad_pairs[:, 0]], 1)
    wide_weights = weights.astype(jnp.float32)
    real_x = jnp.einsum('mcj,mj->mc', wide_weights, straight)
    imag_x = jnp.einsum('mcj,mj->mc', wide_weights, rotated)
    input_grad = (jnp.concatenate([real_x, imag_x], 1) * input_scale).astype(jnp.bfloat16)
    return (weight_grad, input_grad)

def reference(features, cotangent, spectral_weight, channel_weight, channel_bias):
    wave_pairs = MY * MZ
    forward_scale = 1.0 / math.sqrt(NX * NY * NZ)
    inverse_scale = 1.0 / math.sqrt(MODES)
    weight_scale = math.sqrt(MODES / (NX * NY * NZ))
    depth_basis = depth_table(MZ, NZ)
    across_y = analysis_pair(freq_index(MY, NY), NY).astype(jnp.float32)
    across_x = analysis_pair(freq_index(MX, NX), NX).astype(jnp.float32)
    back_y = synthesis_pair(freq_index(MY, NY), NY).astype(jnp.float32)
    back_x = synthesis_pair(freq_index(MX, NX), NX).astype(jnp.float32)
    depth_part = jnp.dot(features, depth_basis.T, preferred_element_type=jnp.float32).astype(jnp.bfloat16)
    depth_five = depth_part.reshape(C, NX, NY, 2, MZ).astype(jnp.float32)
    plane_part = jnp.einsum('cxyaz,yabk->cxbkz', depth_five, across_y).astype(jnp.bfloat16).reshape(C, NX, 2, wave_pairs)
    mode_sums = jnp.einsum('cxaq,xabk->qkbc', plane_part.astype(jnp.float32), across_x).reshape(MODES, 2 * C)
    coeffs = (mode_sums * forward_scale).astype(jnp.bfloat16)
    mode_block = math.gcd(MODES, 1024)
    spectral_list = []
    for offset in range(0, MODES, mode_block):
        spectral_list.append(mode_product(coeffs[offset:offset + mode_block], spectral_weight[offset:offset + mode_block], C))
    spectral = jnp.concatenate(spectral_list, 0)
    planes_back = jnp.einsum('qkao,kabx->oxbq', spectral.reshape(wave_pairs, MX, 2, C).astype(jnp.float32), back_x).astype(jnp.bfloat16)
    slab_size = math.gcd(NX, 16)
    act_list = []
    upstream_list = []
    rows_list = []
    for offset in range(0, NX, slab_size):
        rows_back = planes_back[:, offset:offset + slab_size].reshape(C, slab_size, 2, MY, MZ).astype(jnp.float32)
        lines_back = jnp.einsum('oxakz,kaby->oxybz', rows_back, back_y).astype(jnp.bfloat16).reshape(C, slab_size, NY, 2 * MZ)
        spectral_term = jnp.dot(lines_back, depth_basis, preferred_element_type=jnp.float32) * inverse_scale
        local_in = features[:, offset:offset + slab_size]
        pointwise = jnp.dot(channel_weight, local_in.reshape(C, -1), preferred_element_type=jnp.float32).reshape(C, slab_size, NY, NZ)
        hidden = spectral_term + pointwise + channel_bias.astype(jnp.float32)[:, None, None, None]
        activated, derivative = gelu_parts(hidden)
        act_list.append(activated.astype(jnp.bfloat16))
        upstream = (cotangent[:, offset:offset + slab_size].astype(jnp.float32) * derivative).astype(jnp.bfloat16)
        upstream_list.append(upstream)
        lines_grad = (jnp.dot(upstream, depth_basis.T, preferred_element_type=jnp.float32) * inverse_scale).astype(jnp.bfloat16)
        lines_five = lines_grad.reshape(C, slab_size, NY, 2, MZ).astype(jnp.float32)
        rows_grad = jnp.einsum('oxybz,kaby->oxakz', lines_five, back_y).astype(jnp.bfloat16).reshape(C, slab_size, 2, wave_pairs)
        rows_list.append(rows_grad)
    activated_all = jnp.concatenate(act_list, 1)
    rows_all = jnp.concatenate(rows_list, 1)
    grad_sums = jnp.einsum('oxbq,kabx->qkao', rows_all.astype(jnp.float32), back_x).reshape(MODES, 2 * C)
    grad_modes = grad_sums.astype(jnp.bfloat16)
    weight_list = []
    coeff_list = []
    for offset in range(0, MODES, mode_block):
        weight_grad, input_grad = mode_grads(coeffs[offset:offset + mode_block], spectral_weight[offset:offset + mode_block], grad_modes[offset:offset + mode_block], C, weight_scale, forward_scale)
        weight_list.append(weight_grad)
        coeff_list.append(input_grad)
    spectral_grad = jnp.concatenate(weight_list, 0)
    coeff_grad = jnp.concatenate(coeff_list, 0)
    plane_grad = jnp.einsum('qkbc,xabk->cxaq', coeff_grad.reshape(wave_pairs, MX, 2, C).astype(jnp.float32), across_x).astype(jnp.bfloat16)
    grad_list = []
    for index_slab, offset in enumerate(range(0, NX, slab_size)):
        block_grad = plane_grad[:, offset:offset + slab_size].reshape(C, slab_size, 2, MY, MZ).astype(jnp.float32)
        depth_grad = jnp.einsum('cxbkz,yabk->cxyaz', block_grad, across_y).astype(jnp.bfloat16).reshape(C, slab_size, NY, 2 * MZ)
        upstream = upstream_list[index_slab]
        channel_back = jnp.dot(channel_weight.T, upstream.reshape(C, -1), preferred_element_type=jnp.float32).reshape(C, slab_size, NY, NZ)
        total_grad = jnp.dot(depth_grad, depth_basis, preferred_element_type=jnp.float32) + channel_back
        grad_list.append(total_grad.astype(jnp.bfloat16))
    feature_grad = jnp.concatenate(grad_list, 1)
    return (activated_all, feature_grad, spectral_grad)
```

```python
import functools
import math

import jax
import jax.numpy as jnp
import numpy as np
from jax import lax
from jax.experimental import pallas as pl
from jax.experimental.pallas import tpu as pltpu
from jax.sharding import PartitionSpec as P

MX = 32
MY = 32
MZ = 16


SQRT_TWO_PI = math.sqrt(2.0 / math.pi)
CUBIC_COEF = 0.044715


def freq_index(retained, length):
    ladder = jnp.arange(retained, dtype=jnp.int32)
    return jnp.where(ladder < retained // 2, ladder, length - retained + ladder)


def cos_sin(wavenum, length):
    points = jnp.arange(length, dtype=jnp.int32)
    angles = (wavenum[:, None] * points[None, :] % length).astype(jnp.float32) * (
        2.0 * math.pi / length
    )
    return (jnp.cos(angles), jnp.sin(angles))


def analysis_pair(wavenum, length):
    cosine, sine_wave = cos_sin(wavenum, length)
    cosine, sine_wave = (cosine.T, sine_wave.T)
    return jnp.stack(
        [jnp.stack([cosine, -sine_wave], 1), jnp.stack([sine_wave, cosine], 1)], 1
    ).astype(jnp.bfloat16)


def synthesis_pair(wavenum, length):
    cosine, sine_wave = cos_sin(wavenum, length)
    return jnp.stack(
        [jnp.stack([cosine, sine_wave], 1), jnp.stack([-sine_wave, cosine], 1)], 1
    ).astype(jnp.bfloat16)


def depth_table(retained, length):
    cosine, sine_wave = cos_sin(jnp.arange(retained, dtype=jnp.int32), length)
    return jnp.concatenate([cosine, -sine_wave], 0).astype(jnp.bfloat16)


def gelu_parts(inputs):
    squared = inputs * inputs
    slope = SQRT_TWO_PI * CUBIC_COEF
    tangent = jnp.tanh(inputs * (SQRT_TWO_PI + slope * squared))
    half = 0.5 + 0.5 * tangent
    output = inputs * half
    derivative = half + output * (1.0 - tangent) * (SQRT_TWO_PI + 3.0 * slope * squared)
    return (output, derivative)


def mode_product(coeffs, weights):
    channels = weights.shape[1]
    halves = jnp.einsum("mac,mcj->amj", coeffs, weights, preferred_element_type=jnp.float32)
    real_out = halves[0, :, :channels] - halves[1, :, channels:]
    imag_out = halves[0, :, channels:] + halves[1, :, :channels]
    return jnp.stack([real_out, imag_out], 1).astype(jnp.bfloat16)


def exchange(blocks):
    return lax.all_to_all(blocks, "gx", 0, 0, tiled=True)


def middle_kernel(
    scale, feat_ref, cot_ref, lines_ref, weight_ref, bias_ref, basis_ref, act_ref, up_ref, grad_ref
):
    channels, _, rows, depth_len = feat_ref.shape
    spectral = jnp.dot(
        lines_ref[0].reshape(rows * channels, lines_ref.shape[3]),
        basis_ref[...],
        preferred_element_type=jnp.float32,
    ).reshape(rows, channels, depth_len)
    feats = jnp.swapaxes(feat_ref[:, 0].astype(jnp.float32), 0, 1).astype(jnp.bfloat16)
    cots = jnp.swapaxes(cot_ref[:, 0].astype(jnp.float32), 0, 1)
    acts = []
    for row in range(rows):
        pointwise = jnp.dot(weight_ref[...], feats[row], preferred_element_type=jnp.float32)
        hidden = spectral[row] * scale + pointwise + bias_ref[...]
        activated, derivative = gelu_parts(hidden)
        acts.append(activated)
        up_ref[0, row] = (cots[row] * derivative).astype(jnp.bfloat16)
    act_ref[:, 0] = jnp.swapaxes(jnp.stack(acts, 0), 0, 1).astype(jnp.bfloat16)
    grad = lax.dot_general(
        up_ref[0].reshape(rows * channels, depth_len),
        basis_ref[...],
        (((1,), (1,)), ((), ())),
        preferred_element_type=jnp.float32,
    )
    grad_ref[0] = (grad * scale).astype(jnp.bfloat16).reshape(rows, channels, lines_ref.shape[3])


def final_kernel(up_ref, depth_ref, weight_ref, basis_ref, out_ref):
    _, rows, channels, depth_len = up_ref.shape
    spectral = jnp.dot(
        depth_ref[0].reshape(rows * channels, depth_ref.shape[3]),
        basis_ref[...],
        preferred_element_type=jnp.float32,
    ).reshape(rows, channels, depth_len)
    totals = []
    for row in range(rows):
        back = jnp.dot(weight_ref[...], up_ref[0, row], preferred_element_type=jnp.float32)
        totals.append(spectral[row] + back)
    out_ref[:, 0] = jnp.swapaxes(jnp.stack(totals, 0), 0, 1).astype(jnp.bfloat16)


ROWS = 16


def middle(features, cotangent, lines_back, channel_weight, channel_bias, depth_basis, scale):
    channels, planes, lines, depth_len = features.shape
    parts = lines_back.shape[3]
    field = pl.BlockSpec((channels, 1, ROWS, depth_len), lambda x, y: (0, x, y, 0))
    turned = pl.BlockSpec((1, ROWS, channels, depth_len), lambda x, y: (x, y, 0, 0))
    narrow = pl.BlockSpec((1, ROWS, channels, parts), lambda x, y: (x, y, 0, 0))
    count = features.size
    return pl.pallas_call(
        functools.partial(middle_kernel, scale),
        grid=(planes, lines // ROWS),
        in_specs=[
            field,
            field,
            narrow,
            pl.BlockSpec((channels, channels), lambda x, y: (0, 0)),
            pl.BlockSpec((channels, 1), lambda x, y: (0, 0)),
            pl.BlockSpec((parts, depth_len), lambda x, y: (0, 0)),
        ],
        out_specs=[field, turned, narrow],
        out_shape=[
            jax.ShapeDtypeStruct(features.shape, jnp.bfloat16),
            jax.ShapeDtypeStruct((planes, lines, channels, depth_len), jnp.bfloat16),
            jax.ShapeDtypeStruct((planes, lines, channels, parts), jnp.bfloat16),
        ],
        compiler_params=pltpu.CompilerParams(vmem_limit_bytes=56 * 1024 * 1024),
        cost_estimate=pl.CostEstimate(
            flops=count * 2 * (channels + 2 * parts), bytes_accessed=count * 8, transcendentals=count
        ),
    )(features, cotangent, lines_back, channel_weight, channel_bias[:, None], depth_basis)


def final(upstream, depth_grad, weight_back, depth_basis):
    planes, lines, channels, depth_len = upstream.shape
    parts = depth_grad.shape[3]
    count = upstream.size
    return pl.pallas_call(
        final_kernel,
        grid=(planes, lines // ROWS),
        in_specs=[
            pl.BlockSpec((1, ROWS, channels, depth_len), lambda x, y: (x, y, 0, 0)),
            pl.BlockSpec((1, ROWS, channels, parts), lambda x, y: (x, y, 0, 0)),
            pl.BlockSpec((channels, channels), lambda x, y: (0, 0)),
            pl.BlockSpec((parts, depth_len), lambda x, y: (0, 0)),
        ],
        out_specs=pl.BlockSpec((channels, 1, ROWS, depth_len), lambda x, y: (0, x, y, 0)),
        out_shape=jax.ShapeDtypeStruct((channels, planes, lines, depth_len), jnp.bfloat16),
        compiler_params=pltpu.CompilerParams(vmem_limit_bytes=32 * 1024 * 1024),
        cost_estimate=pl.CostEstimate(
            flops=count * 2 * (channels + parts), bytes_accessed=count * 4, transcendentals=0
        ),
    )(upstream, depth_grad, weight_back, depth_basis)


def plain_body(features, cotangent, spectral_weight, channel_weight, channel_bias):
    channels, planes, lines, depth_len = features.shape
    devices = lax.axis_size("gx")
    all_planes = planes * devices
    owned_modes = spectral_weight.shape[0]
    wave_pairs = MY * MZ
    owned_pairs = owned_modes // MX
    wide = 2 * channels
    forward_scale = 1.0 / math.sqrt(all_planes * lines * depth_len)
    inverse_scale = 1.0 / math.sqrt(MX * wave_pairs)
    weight_scale = math.sqrt(MX * wave_pairs / (all_planes * lines * depth_len))
    depth_basis = depth_table(MZ, depth_len)
    across_y = analysis_pair(freq_index(MY, lines), lines)
    back_y = synthesis_pair(freq_index(MY, lines), lines)
    across_x = analysis_pair(freq_index(MX, all_planes), all_planes)
    back_x = synthesis_pair(freq_index(MX, all_planes), all_planes)

    def to_owners(rows):
        blocks = rows.reshape(devices, owned_pairs * planes, wide)
        return exchange(blocks).reshape(devices, owned_pairs, planes, 2, channels)

    def to_planes(rows):
        blocks = rows.reshape(devices, planes * owned_pairs, wide)
        got = exchange(blocks).reshape(devices, planes, owned_pairs, 2, channels)
        return got.transpose(1, 0, 2, 3, 4).reshape(planes, MY, MZ, 2, channels)

    depth_part = jnp.dot(features, depth_basis.T, preferred_element_type=jnp.float32).astype(
        jnp.bfloat16
    )
    plane_part = jnp.einsum(
        "cxyaz,yabk->kzxbc",
        depth_part.reshape(channels, planes, lines, 2, MZ),
        across_y,
        preferred_element_type=jnp.float32,
    ).astype(jnp.bfloat16)
    gathered = to_owners(plane_part)
    mode_sums = jnp.einsum(
        "sqpac,spabk->qkbc",
        gathered,
        across_x.reshape(devices, planes, 2, 2, MX),
        preferred_element_type=jnp.float32,
    )
    coeffs = (mode_sums * forward_scale).astype(jnp.bfloat16).reshape(owned_modes, 2, channels)
    spectral = mode_product(coeffs, spectral_weight)
    planes_back = jnp.einsum(
        "qkao,kabx->xqbo",
        spectral.reshape(owned_pairs, MX, 2, channels),
        back_x,
        preferred_element_type=jnp.float32,
    ).astype(jnp.bfloat16)
    planes_here = to_planes(planes_back)
    lines_back = (
        jnp.einsum("xkzao,kaby->xyobz", planes_here, back_y, preferred_element_type=jnp.float32)
        .astype(jnp.bfloat16)
        .reshape(planes, lines, channels, 2 * MZ)
    )
    activated, upstream, lines_grad = middle(
        features, cotangent, lines_back, channel_weight, channel_bias, depth_basis, inverse_scale
    )
    rows_grad = jnp.einsum(
        "xyobz,kaby->kzxao",
        lines_grad.reshape(planes, lines, channels, 2, MZ),
        back_y,
        preferred_element_type=jnp.float32,
    ).astype(jnp.bfloat16)
    gathered_grad = to_owners(rows_grad)
    grad_modes = (
        jnp.einsum(
            "sqpbo,kabsp->qkao",
            gathered_grad,
            back_x.reshape(MX, 2, 2, devices, planes),
            preferred_element_type=jnp.float32,
        )
        .astype(jnp.bfloat16)
        .reshape(owned_modes, 2, channels)
    )
    straight = grad_modes.reshape(owned_modes, wide)
    rotated = jnp.concatenate([grad_modes[:, 1], -grad_modes[:, 0]], 1)
    pairs = jnp.stack([straight, rotated], 1)
    coeff_grad = (
        jnp.einsum("mcj,mbj->mbc", spectral_weight, pairs, preferred_element_type=jnp.float32)
        * forward_scale
    ).astype(jnp.bfloat16)
    plane_grad = jnp.einsum(
        "qkbc,xabk->xqac",
        coeff_grad.reshape(owned_pairs, MX, 2, channels),
        across_x,
        preferred_element_type=jnp.float32,
    ).astype(jnp.bfloat16)
    grad_here = to_planes(plane_grad)
    spectral_grad = (
        jnp.einsum("mac,maj->mcj", coeffs, pairs, preferred_element_type=jnp.float32)
        * weight_scale
    ).astype(jnp.bfloat16)
    depth_grad = (
        jnp.einsum("xkzbc,yabk->xycaz", grad_here, across_y, preferred_element_type=jnp.float32)
        .astype(jnp.bfloat16)
        .reshape(planes, lines, channels, 2 * MZ)
    )
    feature_grad = final(upstream, depth_grad, channel_weight.T, depth_basis)
    return (activated, feature_grad, spectral_grad)


MESH = pl.DeviceIdType.MESH
F32 = jnp.float32
BF16 = jnp.bfloat16
MB = 1024 * 1024


def host_cos_sin(wavenum, length):
    angles = (np.outer(wavenum, np.arange(length)) % length).astype(np.float32) * np.float32(
        2.0 * math.pi / length
    )
    return np.cos(angles), np.sin(angles)


def host_freq(retained, length):
    ladder = np.arange(retained)
    return np.where(ladder < retained // 2, ladder, length - retained + ladder)


def host_minus(retained, length):
    cosine, sine = host_cos_sin(host_freq(retained, length), length)
    cosine, sine = cosine.T, sine.T
    return np.stack([np.stack([cosine, -sine], 1), np.stack([sine, cosine], 1)], 1)


def host_plus(retained, length):
    cosine, sine = host_cos_sin(host_freq(retained, length), length)
    return np.stack([np.stack([cosine, sine], 1), np.stack([-sine, cosine], 1)], 1)


def host_tables(devices, lines, depth_len, channels):
    all_planes = 2 * devices
    two = np.eye(2)
    eight = np.eye(8)
    cosine, sine = host_cos_sin(np.arange(MZ), depth_len)
    depth = np.stack([cosine, -sine], 0)
    z_in = np.einsum("akz,cd->czakd", depth, eight).reshape(8 * depth_len, 16 * MZ)
    minus_y = host_minus(MY, lines).reshape(lines, 2, 2, devices, 2)
    y_in = np.einsum("yabdk,xw->dkbwxay", minus_y, two).reshape(8 * devices, 4 * lines)
    groups = channels // 8
    source = np.arange(MZ * channels).reshape(groups, MZ, 8)
    target = source.transpose(1, 0, 2).reshape(-1)
    order = np.zeros((MZ * channels, MZ * channels))
    order[target, np.arange(MZ * channels)] = 1.0
    minus_x = host_minus(MX, all_planes).reshape(devices, 2, 2, 2, MX)
    x_in = np.einsum("sxabk,hg,jl,p->hkjpbsglax", minus_x, two, two, np.ones(2)).reshape(
        16 * MX, 16 * devices
    )
    swapped = np.stack([minus_x[:, :, :, 1], -minus_x[:, :, :, 0]], 3)
    x_turn = np.einsum("sxabk,hg,jl,p->hkjpbsglax", swapped, two, two, np.ones(2)).reshape(
        16 * MX, 16 * devices
    )
    plus_x = host_plus(MX, all_planes).reshape(MX, 2, 2, devices, 2)
    crossed = np.stack([-plus_x[:, :, 1], plus_x[:, :, 0]], 2)
    both = np.stack([plus_x, crossed], 0)
    x_out = np.einsum("rkabsx,pq,jl->prsjbxklqa", both, two, two).reshape(32 * devices, 8 * MX)
    x_back = np.einsum("kabsx,jl,q->sjbxklqa", plus_x, two, np.ones(2)).reshape(
        8 * devices, 8 * MX
    )
    plus_y = host_plus(MY, lines).reshape(devices, 2, 2, 2, lines)
    y_out = np.einsum("skaby,hg,xw->xbhysgkaw", plus_y, two, two).reshape(8 * lines, 16 * devices)
    tables = dict(
        z_in=z_in, z_out=z_in.T, y_in=y_in, order=order, unorder=order.T, x_in=x_in,
        x_turn=x_turn, x_out=x_out, x_back=x_back, y_out=y_out,
    )
    return {name: jnp.asarray(np.ascontiguousarray(t), BF16) for name, t in tables.items()}


def fdot(left, right):
    return jnp.dot(left, right, preferred_element_type=F32)


def greet(devices):
    me, group = lax.axis_index("gx"), lax.axis_index("grp")
    barrier = pltpu.get_barrier_semaphore()

    @pl.loop(1, devices)
    def _(step):
        pl.semaphore_signal(
            barrier, inc=1, device_id=(group, lax.rem(me + step, devices)), device_id_type=MESH
        )

    def arrived():
        pl.semaphore_wait(barrier, devices - 1)

    return arrived


def swap_start(devices, sent, got, send_sem, recv_sem, stage):
    me, group = lax.axis_index("gx"), lax.axis_index("grp")

    def copy(step):
        target = lax.rem(me + step, devices)
        return pltpu.make_async_remote_copy(
            src_ref=sent.at[target],
            dst_ref=got.at[me],
            send_sem=send_sem.at[stage, step],
            recv_sem=recv_sem.at[stage, step],
            device_id=(group, target),
            device_id_type=MESH,
        )

    @pl.loop(1, devices)
    def _(step):
        copy(step).start()

    got[me] = sent[me]

    def finish():
        @pl.loop(1, devices)
        def _(step):
            copy(step).wait_recv()

    def drained():
        @pl.loop(1, devices)
        def _(step):
            copy(step).wait_send()

    return finish, drained


def to_chunks(devices, lines_ref, y_in, order, sent):
    rows = fdot(y_in[...], lines_ref[...]).astype(BF16)
    rows = fdot(rows, order[...])
    lanes = rows.shape[1]
    halves = [
        rows[:, h * lanes // 2 : (h + 1) * lanes // 2].reshape(devices, 8, lanes // 2)
        for h in range(2)
    ]
    chunk = jnp.concatenate(halves, 1).astype(BF16)
    for u in range(2):
        sent[u] = chunk[:, :, u * lanes // 4 : (u + 1) * lanes // 4]


def mode_block(weights, k_pair, half, pair):
    def one(kx):
        return jnp.concatenate(
            [weights[k2, half * 8 + pair * 2 + parity, kx] for k2 in range(2) for parity in range(2)],
            0,
        )

    return jnp.concatenate([one(2 * k_pair), one(2 * k_pair + 1)], 1)


def iotas():
    row = lax.broadcasted_iota(jnp.int32, (8, 128), 0)
    lane = lax.broadcasted_iota(jnp.int32, (8, 128), 1)
    return row, lane


def weight_copies(weights_hbm, weights, sem):
    def copy(half, pair):
        kz = pl.ds(half * 8 + pair * 2, 2)
        return pltpu.make_async_copy(
            weights_hbm.at[:, kz], weights.at[:, kz], sem.at[half, pair]
        )

    return copy


def fill_kron(channel_weight, out, contract):
    size = out.shape[0]
    channels = channel_weight.shape[0]

    def spread(rows, first, axis):
        shape = (rows, channels) if axis == 0 else (channels, rows)
        long = lax.broadcasted_iota(jnp.int32, shape, axis)
        short = lax.broadcasted_iota(jnp.int32, shape, 1 - axis)
        return jnp.where(long // 16 + first == short, 1.0, 0.0).astype(BF16)

    columns = spread(size, 0, 1)
    line = lax.broadcasted_iota(jnp.int32, (128, size), 0) % 16
    same = line == lax.broadcasted_iota(jnp.int32, (128, size), 1) % 16

    @pl.loop(0, size // 128)
    def _(block):
        rows = lax.dot_general(
            spread(128, block * 8, 0),
            channel_weight[...],
            (((1,), (1 - contract,)), ((), ())),
            preferred_element_type=F32,
        ).astype(BF16)
        out[pl.ds(pl.multiple_of(block * 128, 128), 128), :] = jnp.where(
            same, fdot(rows, columns), 0.0
        ).astype(BF16)


def enter_kernel(
    devices, forward_scale,
    feat_hbm, weights_hbm, channel_weight, z_in, y_in, order, x_in, x_out,
    got_out, back_out, kron_hbm, kron_back_hbm,
    feat, weights, lines_part, sent, got, modes, mixed, sent_back, got_back, krons,
    feat_sem, weight_sem, kron_sem, send_sem, recv_sem,
):
    channels, planes, lines, depth_len = feat.shape
    groups = channels // 8
    arrived = greet(devices)
    load = pltpu.make_async_copy(feat_hbm, feat, feat_sem)
    load.start()
    load.wait()
    weight_copy = weight_copies(weights_hbm, weights, weight_sem)
    for pair in range(4):
        for half in range(2):
            weight_copy(half, pair).start()

    @pl.loop(0, groups)
    def _(group):
        for plane in range(planes):
            wide = jnp.concatenate([feat[group * 8 + i, plane] for i in range(8)], 1)
            part = fdot(wide, z_in[...]).astype(BF16)
            for a in range(2):
                lines_part[
                    pl.ds((plane * 2 + a) * lines, lines),
                    pl.ds(pl.multiple_of(group * 128, 128), 128),
                ] = part[:, a * 128 : (a + 1) * 128]

    to_chunks(devices, lines_part, y_in, order, sent)
    arrived()
    ends = [
        swap_start(devices, sent.at[u], got.at[u], send_sem, recv_sem, u) for u in range(2)
    ]
    kron_copies = []
    for back in range(2):
        fill_kron(channel_weight, krons.at[back], 1 - back)
        kron_copies.append(
            pltpu.make_async_copy(
                krons.at[back], [kron_hbm, kron_back_hbm][back], kron_sem.at[back]
            )
        )
        kron_copies[back].start()
    row, lane = iotas()
    own = [(row // 2) == (lane // 64 + 2 * k2) for k2 in range(2)]
    low = lax.broadcasted_iota(jnp.int32, (8 * devices, 128), 1) < 64
    for u in range(2):
        ends[u][0]()
        source = got[u].reshape(16 * devices, 256)
        modes[...] = (fdot(x_in[...], source) * forward_scale).reshape(2, MX, 8, 256)

        @pl.loop(0, 4)
        def _(part):
            half, local = part // 2, part % 2
            weight_copy(half, 2 * u + local).wait()
            span = pl.ds(pl.multiple_of(local * 128, 128), 128)

            def step(k_pair, carry):
                left = []
                for i in range(2):
                    block = modes[half, 2 * k_pair + i, :, span]
                    left.append(
                        jnp.concatenate([jnp.where(own[0], block, 0.0), jnp.where(own[1], block, 0.0)], 1)
                    )
                left = jnp.concatenate(left, 0).astype(BF16)
                out = fdot(left, mode_block(weights, k_pair, half, 2 * u + local))
                out = jnp.concatenate([out[:8, :128], out[8:, 128:]], 0).astype(BF16)
                mixed[half, pl.ds(pl.multiple_of(k_pair * 16, 16), 16), span] = out
                return carry

            lax.fori_loop(0, MX // 2, step, 0, unroll=8)

        halves = []
        for half in range(2):
            every = fdot(x_out[...], mixed[half])
            size = 8 * devices
            tiles = []
            for local in range(2):
                even, even_x, odd, odd_x = [
                    every[i * size : (i + 1) * size, local * 128 : (local + 1) * 128]
                    for i in range(4)
                ]
                tiles.append(
                    jnp.where(low, even, odd_x) + pltpu.roll(jnp.where(low, odd, even_x), 64, 1)
                )
            halves.append(jnp.concatenate(tiles, 1).reshape(devices, 8, 256))
        sent_back[u] = jnp.concatenate(halves, 1).astype(BF16)
        ends.append(swap_start(devices, sent_back.at[u], got_back.at[u], send_sem, recv_sem, 2 + u))
    got_out[...] = got[...]
    for copy in kron_copies:
        copy.wait()
    ends[2][0]()
    ends[3][0]()
    for end in ends:
        end[1]()
    back_out[...] = got_back[...]


def middle_transform(devices, back, y_out, unorder, blocks):
    lines_u = [fdot(y_out[...], back[u].reshape(16 * devices, 256)).astype(BF16) for u in range(2)]
    lines = lines_u[0].shape[0] // 8
    for plane in range(2):
        for part in range(2):
            pieces = []
            for half in range(2):
                first = ((plane * 2 + part) * 2 + half) * lines
                pieces += [lines_u[u][first : first + lines] for u in range(2)]
            rows = fdot(jnp.concatenate(pieces, 1), unorder[...]).astype(BF16)
            groups = rows.shape[1] // 128
            for block in range(lines // 16):
                for group in range(groups):
                    blocks[
                        block,
                        (plane * groups + group) * 16 : (plane * groups + group + 1) * 16,
                        part * 128 : (part + 1) * 128,
                    ] = rows[block * 16 : (block + 1) * 16, group * 128 : (group + 1) * 128]


def new_middle_kernel(
    devices, scale,
    feat, cot, back, kron, bias, z_in, z_out, y_in, y_out, order, unorder,
    act, up, chunks,
    blocks, lines_part, pointwise, spectral, up_wide,
):
    channels, planes, rows, depth_len = feat.shape
    groups = channels // 8
    step = pl.program_id(0)

    @pl.when(step == 0)
    def _():
        middle_transform(devices, back, y_out, unorder, blocks)

    spectral[...] = fdot(blocks[step], z_out[...])
    both = jnp.concatenate(
        [feat[:, x].reshape(channels * rows, depth_len) for x in range(planes)], 1
    )
    pointwise[...] = fdot(kron[...], both)

    @pl.loop(0, groups)
    def _(group):
        for plane in range(planes):
            here = pl.ds(pl.multiple_of((plane * groups + group) * rows, 16), rows)
            for i in range(8):
                o = group * 8 + i
                hidden = (
                    spectral[here, i * 128 : (i + 1) * 128] * scale
                    + pointwise[pl.ds(pl.multiple_of(o * rows, 16), rows), plane * 128 : (plane + 1) * 128]
                    + bias[o]
                )
                activated, derivative = gelu_parts(hidden)
                act[o, plane] = activated.astype(BF16)
                upstream = (cot[o, plane].astype(F32) * derivative).astype(BF16)
                up[o, plane] = upstream
                up_wide[here, i * 128 : (i + 1) * 128] = upstream

    grad = (fdot(up_wide[...], z_in[...]) * scale).astype(BF16)
    for plane in range(planes):
        for a in range(2):
            first = (plane * 2 + a) * 64
            for group in range(groups):
                lines_part[
                    pl.ds(pl.multiple_of(first + step * rows, 16), rows),
                    group * 128 : (group + 1) * 128,
                ] = grad[
                    (plane * groups + group) * rows : (plane * groups + group + 1) * rows,
                    a * 128 : (a + 1) * 128,
                ]

    @pl.when(step == pl.num_programs(0) - 1)
    def _():
        to_chunks(devices, lines_part, y_in, order, chunks)


def return_kernel(
    devices, forward_scale,
    sent_in, weights_hbm, x_in, x_turn, x_back,
    got_out, back_out,
    weights, sent, got, modes, turned, mixed, sent_back, got_back,
    weight_sem, send_sem, recv_sem,
):
    arrived = greet(devices)
    weight_copy = weight_copies(weights_hbm, weights, weight_sem)
    for pair in range(4):
        for half in range(2):
            weight_copy(half, pair).start()
    sent[...] = sent_in[...]
    arrived()
    ends = [
        swap_start(devices, sent.at[u], got.at[u], send_sem, recv_sem, u) for u in range(2)
    ]
    row, lane = iotas()
    low = lane < 64
    direct = low == ((row // 2) % 2 == 0)
    first_line = row < 4
    zero = jnp.zeros((8, 128), F32)
    for u in range(2):
        ends[u][0]()
        source = got[u].reshape(16 * devices, 256)
        modes[...] = fdot(x_in[...], source).reshape(2, MX, 8, 256)
        turned[...] = fdot(x_turn[...], source).reshape(2, MX, 8, 256)

        @pl.loop(0, 4)
        def _(part):
            half, local = part // 2, part % 2
            weight_copy(half, 2 * u + local).wait()
            span = pl.ds(pl.multiple_of(local * 128, 128), 128)

            def step(k_pair, carry):
                pairs = []
                for i in range(2):
                    straight = modes[half, 2 * k_pair + i, :, span]
                    other = turned[half, 2 * k_pair + i, :, span]
                    pairs.append(pair_tile(straight, other, low, direct))
                left = jnp.concatenate(
                    [jnp.concatenate([pairs[0], zero], 1), jnp.concatenate([zero, pairs[1]], 1)], 0
                ).astype(BF16)
                out = lax.dot_general(
                    left,
                    mode_block(weights, k_pair, half, 2 * u + local),
                    (((1,), (1,)), ((), ())),
                    preferred_element_type=F32,
                )
                tiles = []
                for i in range(2):
                    rows = out[8 * i : 8 * i + 8]
                    tiles.append(
                        jnp.where(direct, jnp.where(first_line, rows[:, :128], rows[:, 128:]), 0.0)
                    )
                mixed[half, pl.ds(pl.multiple_of(k_pair * 16, 16), 16), span] = (
                    jnp.concatenate(tiles, 0) * forward_scale
                ).astype(BF16)
                return carry

            lax.fori_loop(0, MX // 2, step, 0, unroll=8)

        sent_back[u] = jnp.concatenate(
            [fdot(x_back[...], mixed[half]).reshape(devices, 8, 256) for half in range(2)], 1
        ).astype(BF16)
        ends.append(swap_start(devices, sent_back.at[u], got_back.at[u], send_sem, recv_sem, 2 + u))
    got_out[...] = got[...]
    ends[2][0]()
    ends[3][0]()
    for end in ends:
        end[1]()
    back_out[...] = got_back[...]


def pair_tile(straight, other, low, direct):
    return jnp.where(
        direct,
        jnp.where(low, straight, other),
        pltpu.roll(jnp.where(low, other, straight), 64, 1),
    )


def weight_grad_kernel(
    devices, forward_scale, weight_scale,
    got, got_grad, x_in, x_turn,
    out_hbm,
    coeffs, modes, turned, buffer, sem,
):
    row, lane = iotas()
    low = lane < 64
    direct = low == ((row // 2) % 2 == 0)
    own = [(row // 2) == (lane // 64 + 2 * k2) for k2 in range(2)]
    for u in range(2):
        coeffs[u] = (fdot(x_in[...], got[u].reshape(16 * devices, 256)) * forward_scale).reshape(
            2, MX, 8, 256
        )
        source = got_grad[u].reshape(16 * devices, 256)
        modes[u] = fdot(x_in[...], source).reshape(2, MX, 8, 256)
        turned[u] = fdot(x_turn[...], source).reshape(2, MX, 8, 256)
    block = lax.broadcasted_iota(jnp.int32, (128, 256), 0) // 8
    side = lax.broadcasted_iota(jnp.int32, (128, 256), 1) // 128

    def copy(index, slot):
        return pltpu.make_async_copy(
            buffer.at[slot], out_hbm.at[:, pl.ds(2 * index, 2)], sem.at[slot]
        )

    @pl.loop(0, 8)
    def _(index):
        slot = lax.rem(index, 2)
        half, u, local = index // 4, (index % 4) // 2, index % 2
        span = pl.ds(pl.multiple_of(local * 128, 128), 128)

        @pl.when(index >= 2)
        def _():
            copy(index - 2, slot).wait()

        @pl.loop(0, 2)
        def _(k_half):
            here = pl.ds(k_half * (MX // 2), MX // 2)
            values = coeffs[u, half, here, :, span]
            wide = jnp.concatenate(
                [jnp.where(own[k2][None], values, 0.0).reshape(128, 128) for k2 in range(2)], 1
            )
            left = wide.T.astype(BF16)
            pairs = []
            for k in range(MX // 2):
                pairs.append(
                    pair_tile(
                        modes[u, half, k_half * (MX // 2) + k, :, span],
                        turned[u, half, k_half * (MX // 2) + k, :, span],
                        low,
                        direct,
                    )
                )
            pairs = jnp.concatenate(pairs, 0).astype(BF16).astype(F32) * weight_scale
            pairs = jnp.concatenate([pairs, pairs], 1)
            for i in range(MX // 4):
                right = jnp.where(block == 2 * i + side, pairs, 0.0).astype(BF16)
                out = fdot(left, right).astype(BF16)
                for s in range(2):
                    for k2 in range(2):
                        for parity in range(2):
                            first = (k2 * 2 + parity) * 64
                            buffer[slot, k2, parity, k_half * (MX // 2) + 2 * i + s] = out[
                                first : first + 64, s * 128 : (s + 1) * 128
                            ]

        copy(index, slot).start()

    copy(6, 0).wait()
    copy(7, 1).wait()


def new_final_kernel(devices, up, back, kron, z_out, y_out, unorder, out, blocks, pointwise, spectral):
    channels, planes, rows, depth_len = up.shape
    groups = channels // 8
    step = pl.program_id(0)

    @pl.when(step == 0)
    def _():
        middle_transform(devices, back, y_out, unorder, blocks)

    spectral[...] = fdot(blocks[step], z_out[...])
    both = jnp.concatenate(
        [up[:, x].reshape(channels * rows, depth_len) for x in range(planes)], 1
    )
    pointwise[...] = fdot(kron[...], both)

    @pl.loop(0, groups)
    def _(group):
        for plane in range(planes):
            here = pl.ds(pl.multiple_of((plane * groups + group) * rows, 16), rows)
            for i in range(8):
                o = group * 8 + i
                total = (
                    spectral[here, i * 128 : (i + 1) * 128]
                    + pointwise[pl.ds(pl.multiple_of(o * rows, 16), rows), plane * 128 : (plane + 1) * 128]
                )
                out[o, plane] = total.astype(BF16)


def vmem(*shape, dtype=BF16):
    return pltpu.VMEM(shape, dtype)


WHOLE = pl.BlockSpec(memory_space=pltpu.VMEM)
ANYWHERE = pl.BlockSpec(memory_space=pl.ANY)


def block_body(features, cotangent, spectral_weight, channel_weight, channel_bias):
    channels, planes, lines, depth_len = features.shape
    devices = lax.axis_size("gx")
    all_planes = planes * devices
    number = MX * MY * MZ
    forward_scale = 1.0 / math.sqrt(all_planes * lines * depth_len)
    inverse_scale = 1.0 / math.sqrt(number)
    weight_scale = math.sqrt(number / (all_planes * lines * depth_len))
    tables = host_tables(devices, lines, depth_len, channels)
    weights = spectral_weight.reshape(2, MZ, MX, channels, 2 * channels)
    wide = MZ * channels
    chunk = jax.ShapeDtypeStruct((2, devices, 16, 256), BF16)
    dma = pltpu.SemaphoreType.DMA
    square = jax.ShapeDtypeStruct((16 * channels, 16 * channels), BF16)
    got, back, kron, kron_back = pl.pallas_call(
        functools.partial(enter_kernel, devices, forward_scale),
        out_shape=[chunk, chunk, square, square],
        in_specs=[ANYWHERE, ANYWHERE] + [WHOLE] * 6,
        out_specs=[WHOLE, WHOLE, ANYWHERE, ANYWHERE],
        scratch_shapes=[
            vmem(*features.shape),
            vmem(*weights.shape),
            vmem(4 * lines, wide),
            vmem(*chunk.shape),
            vmem(*chunk.shape),
            vmem(2, MX, 8, 256, dtype=F32),
            vmem(2, 8 * MX, 256),
            vmem(*chunk.shape),
            vmem(*chunk.shape),
            vmem(2, *square.shape),
            dma(()),
            dma((2, 4)),
            dma((2,)),
            dma((4, devices)),
            dma((4, devices)),
        ],
        compiler_params=pltpu.CompilerParams(
            collective_id=0, has_side_effects=True, vmem_limit_bytes=48 * MB
        ),
        name="enter",
    )(
        features, weights, channel_weight, tables["z_in"], tables["y_in"], tables["order"],
        tables["x_in"], tables["x_out"],
    )
    rows = 16
    field = pl.BlockSpec((channels, planes, rows, depth_len), lambda y: (0, 0, y, 0))

    def full(array):
        return pl.BlockSpec(array.shape, lambda y: (0,) * len(array.shape))

    like = jax.ShapeDtypeStruct(features.shape, BF16)
    activated, upstream, sent = pl.pallas_call(
        functools.partial(new_middle_kernel, devices, inverse_scale),
        grid=(lines // rows,),
        in_specs=[
            field, field, full(chunk), full(kron), pl.BlockSpec(memory_space=pltpu.SMEM),
            full(tables["z_in"]), full(tables["z_out"]), full(tables["y_in"]),
            full(tables["y_out"]), full(tables["order"]), full(tables["unorder"]),
        ],
        out_specs=[field, field, full(chunk)],
        out_shape=[like, like, chunk],
        scratch_shapes=[
            vmem(lines // rows, 2 * wide // 8, 256),
            vmem(4 * lines, wide),
            vmem(channels * rows, planes * depth_len, dtype=F32),
            vmem(planes * channels * 2, 8 * depth_len, dtype=F32),
            vmem(planes * channels * 2, 8 * depth_len),
        ],
        compiler_params=pltpu.CompilerParams(vmem_limit_bytes=48 * MB),
        name="middle",
    )(
        features, cotangent, back, kron, channel_bias, tables["z_in"], tables["z_out"],
        tables["y_in"], tables["y_out"], tables["order"], tables["unorder"],
    )
    got_grad, back_grad = pl.pallas_call(
        functools.partial(return_kernel, devices, forward_scale),
        out_shape=[chunk, chunk],
        in_specs=[WHOLE, ANYWHERE] + [WHOLE] * 3,
        out_specs=[WHOLE, WHOLE],
        scratch_shapes=[
            vmem(*weights.shape),
            vmem(*chunk.shape),
            vmem(*chunk.shape),
            vmem(2, MX, 8, 256, dtype=F32),
            vmem(2, MX, 8, 256, dtype=F32),
            vmem(2, 8 * MX, 256),
            vmem(*chunk.shape),
            vmem(*chunk.shape),
            dma((2, 4)),
            dma((4, devices)),
            dma((4, devices)),
        ],
        compiler_params=pltpu.CompilerParams(
            collective_id=1, has_side_effects=True, vmem_limit_bytes=48 * MB
        ),
        name="backward",
    )(sent, weights, tables["x_in"], tables["x_turn"], tables["x_back"])
    spectral_grad = pl.pallas_call(
        functools.partial(weight_grad_kernel, devices, forward_scale, weight_scale),
        out_shape=jax.ShapeDtypeStruct(weights.shape, BF16),
        in_specs=[WHOLE] * 4,
        out_specs=ANYWHERE,
        scratch_shapes=[
            vmem(2, 2, MX, 8, 256, dtype=F32),
            vmem(2, 2, MX, 8, 256, dtype=F32),
            vmem(2, 2, MX, 8, 256, dtype=F32),
            vmem(2, 2, 2, MX, channels, 2 * channels),
            dma((2,)),
        ],
        compiler_params=pltpu.CompilerParams(vmem_limit_bytes=40 * MB),
        name="weight_grad",
    )(got, got_grad, tables["x_in"], tables["x_turn"])
    feature_grad = pl.pallas_call(
        functools.partial(new_final_kernel, devices),
        grid=(lines // rows,),
        in_specs=[
            field, full(chunk), full(kron), full(tables["z_out"]), full(tables["y_out"]),
            full(tables["unorder"]),
        ],
        out_specs=field,
        out_shape=like,
        scratch_shapes=[
            vmem(lines // rows, 2 * wide // 8, 256),
            vmem(channels * rows, planes * depth_len, dtype=F32),
            vmem(planes * channels * 2, 8 * depth_len, dtype=F32),
        ],
        compiler_params=pltpu.CompilerParams(vmem_limit_bytes=40 * MB),
        name="final",
    )(upstream, back_grad, kron_back, tables["z_out"], tables["y_out"], tables["unorder"])
    return (activated, feature_grad, spectral_grad.reshape(spectral_weight.shape))


def body(features, cotangent, spectral_weight, channel_weight, channel_bias):
    channels, planes, lines, depth_len = features.shape
    devices = lax.axis_size("gx")
    fits = (
        2 * devices == MY
        and planes == 2
        and channels == 64
        and lines == 64
        and depth_len == 128
        and spectral_weight.shape[0] == 2 * MZ * MX
    )
    chosen = block_body if fits else plain_body
    return chosen(features, cotangent, spectral_weight, channel_weight, channel_bias)


def solution(mesh):
    in_specs = (
        P("grp", "gx", None, None),
        P("grp", "gx", None, None),
        P("gx", None, None),
        P(),
        P(),
    )
    out_specs = (
        P("grp", "gx", None, None),
        P("grp", "gx", None, None),
        P(("grp", "gx"), None, None),
    )
    return jax.shard_map(body, mesh=mesh, in_specs=in_specs, out_specs=out_specs, check_vma=False)
```

```python
import functools
import math

import jax
import jax.numpy as jnp
import numpy as np
from jax import lax
from jax.experimental import pallas as pl
from jax.experimental.pallas import tpu as pltpu
from jax.sharding import PartitionSpec as P

MX = 32
MY = 32
MZ = 16


SQRT_TWO_PI = math.sqrt(2.0 / math.pi)
CUBIC_COEF = 0.044715


def freq_index(retained, length):
    ladder = jnp.arange(retained, dtype=jnp.int32)
    return jnp.where(ladder < retained // 2, ladder, length - retained + ladder)


def cos_sin(wavenum, length):
    points = jnp.arange(length, dtype=jnp.int32)
    angles = (wavenum[:, None] * points[None, :] % length).astype(jnp.float32) * (
        2.0 * math.pi / length
    )
    return (jnp.cos(angles), jnp.sin(angles))


def analysis_pair(wavenum, length):
    cosine, sine_wave = cos_sin(wavenum, length)
    cosine, sine_wave = (cosine.T, sine_wave.T)
    return jnp.stack(
        [jnp.stack([cosine, -sine_wave], 1), jnp.stack([sine_wave, cosine], 1)], 1
    ).astype(jnp.bfloat16)


def synthesis_pair(wavenum, length):
    cosine, sine_wave = cos_sin(wavenum, length)
    return jnp.stack(
        [jnp.stack([cosine, sine_wave], 1), jnp.stack([-sine_wave, cosine], 1)], 1
    ).astype(jnp.bfloat16)


def depth_table(retained, length):
    cosine, sine_wave = cos_sin(jnp.arange(retained, dtype=jnp.int32), length)
    return jnp.concatenate([cosine, -sine_wave], 0).astype(jnp.bfloat16)


def gelu_parts(inputs):
    squared = inputs * inputs
    slope = SQRT_TWO_PI * CUBIC_COEF
    tangent = jnp.tanh(inputs * (SQRT_TWO_PI + slope * squared))
    half = 0.5 + 0.5 * tangent
    output = inputs * half
    derivative = half + output * (1.0 - tangent) * (SQRT_TWO_PI + 3.0 * slope * squared)
    return (output, derivative)


def mode_product(coeffs, weights):
    channels = weights.shape[1]
    halves = jnp.einsum("mac,mcj->amj", coeffs, weights, preferred_element_type=jnp.float32)
    real_out = halves[0, :, :channels] - halves[1, :, channels:]
    imag_out = halves[0, :, channels:] + halves[1, :, :channels]
    return jnp.stack([real_out, imag_out], 1).astype(jnp.bfloat16)


def exchange(blocks):
    return lax.all_to_all(blocks, "gx", 0, 0, tiled=True)


def middle_kernel(
    scale, feat_ref, cot_ref, lines_ref, weight_ref, bias_ref, basis_ref, act_ref, up_ref, grad_ref
):
    channels, _, rows, depth_len = feat_ref.shape
    spectral = jnp.dot(
        lines_ref[0].reshape(rows * channels, lines_ref.shape[3]),
        basis_ref[...],
        preferred_element_type=jnp.float32,
    ).reshape(rows, channels, depth_len)
    feats = jnp.swapaxes(feat_ref[:, 0].astype(jnp.float32), 0, 1).astype(jnp.bfloat16)
    cots = jnp.swapaxes(cot_ref[:, 0].astype(jnp.float32), 0, 1)
    acts = []
    for row in range(rows):
        pointwise = jnp.dot(weight_ref[...], feats[row], preferred_element_type=jnp.float32)
        hidden = spectral[row] * scale + pointwise + bias_ref[...]
        activated, derivative = gelu_parts(hidden)
        acts.append(activated)
        up_ref[0, row] = (cots[row] * derivative).astype(jnp.bfloat16)
    act_ref[:, 0] = jnp.swapaxes(jnp.stack(acts, 0), 0, 1).astype(jnp.bfloat16)
    grad = lax.dot_general(
        up_ref[0].reshape(rows * channels, depth_len),
        basis_ref[...],
        (((1,), (1,)), ((), ())),
        preferred_element_type=jnp.float32,
    )
    grad_ref[0] = (grad * scale).astype(jnp.bfloat16).reshape(rows, channels, lines_ref.shape[3])


def final_kernel(up_ref, depth_ref, weight_ref, basis_ref, out_ref):
    _, rows, channels, depth_len = up_ref.shape
    spectral = jnp.dot(
        depth_ref[0].reshape(rows * channels, depth_ref.shape[3]),
        basis_ref[...],
        preferred_element_type=jnp.float32,
    ).reshape(rows, channels, depth_len)
    totals = []
    for row in range(rows):
        back = jnp.dot(weight_ref[...], up_ref[0, row], preferred_element_type=jnp.float32)
        totals.append(spectral[row] + back)
    out_ref[:, 0] = jnp.swapaxes(jnp.stack(totals, 0), 0, 1).astype(jnp.bfloat16)


ROWS = 16


def middle(features, cotangent, lines_back, channel_weight, channel_bias, depth_basis, scale):
    channels, planes, lines, depth_len = features.shape
    parts = lines_back.shape[3]
    field = pl.BlockSpec((channels, 1, ROWS, depth_len), lambda x, y: (0, x, y, 0))
    turned = pl.BlockSpec((1, ROWS, channels, depth_len), lambda x, y: (x, y, 0, 0))
    narrow = pl.BlockSpec((1, ROWS, channels, parts), lambda x, y: (x, y, 0, 0))
    count = features.size
    return pl.pallas_call(
        functools.partial(middle_kernel, scale),
        grid=(planes, lines // ROWS),
        in_specs=[
            field,
            field,
            narrow,
            pl.BlockSpec((channels, channels), lambda x, y: (0, 0)),
            pl.BlockSpec((channels, 1), lambda x, y: (0, 0)),
            pl.BlockSpec((parts, depth_len), lambda x, y: (0, 0)),
        ],
        out_specs=[field, turned, narrow],
        out_shape=[
            jax.ShapeDtypeStruct(features.shape, jnp.bfloat16),
            jax.ShapeDtypeStruct((planes, lines, channels, depth_len), jnp.bfloat16),
            jax.ShapeDtypeStruct((planes, lines, channels, parts), jnp.bfloat16),
        ],
        compiler_params=pltpu.CompilerParams(vmem_limit_bytes=56 * 1024 * 1024),
        cost_estimate=pl.CostEstimate(
            flops=count * 2 * (channels + 2 * parts), bytes_accessed=count * 8, transcendentals=count
        ),
    )(features, cotangent, lines_back, channel_weight, channel_bias[:, None], depth_basis)


def final(upstream, depth_grad, weight_back, depth_basis):
    planes, lines, channels, depth_len = upstream.shape
    parts = depth_grad.shape[3]
    count = upstream.size
    return pl.pallas_call(
        final_kernel,
        grid=(planes, lines // ROWS),
        in_specs=[
            pl.BlockSpec((1, ROWS, channels, depth_len), lambda x, y: (x, y, 0, 0)),
            pl.BlockSpec((1, ROWS, channels, parts), lambda x, y: (x, y, 0, 0)),
            pl.BlockSpec((channels, channels), lambda x, y: (0, 0)),
            pl.BlockSpec((parts, depth_len), lambda x, y: (0, 0)),
        ],
        out_specs=pl.BlockSpec((channels, 1, ROWS, depth_len), lambda x, y: (0, x, y, 0)),
        out_shape=jax.ShapeDtypeStruct((channels, planes, lines, depth_len), jnp.bfloat16),
        compiler_params=pltpu.CompilerParams(vmem_limit_bytes=32 * 1024 * 1024),
        cost_estimate=pl.CostEstimate(
            flops=count * 2 * (channels + parts), bytes_accessed=count * 4, transcendentals=0
        ),
    )(upstream, depth_grad, weight_back, depth_basis)


def plain_body(features, cotangent, spectral_weight, channel_weight, channel_bias):
    channels, planes, lines, depth_len = features.shape
    devices = lax.axis_size("gx")
    all_planes = planes * devices
    owned_modes = spectral_weight.shape[0]
    wave_pairs = MY * MZ
    owned_pairs = owned_modes // MX
    wide = 2 * channels
    forward_scale = 1.0 / math.sqrt(all_planes * lines * depth_len)
    inverse_scale = 1.0 / math.sqrt(MX * wave_pairs)
    weight_scale = math.sqrt(MX * wave_pairs / (all_planes * lines * depth_len))
    depth_basis = depth_table(MZ, depth_len)
    across_y = analysis_pair(freq_index(MY, lines), lines)
    back_y = synthesis_pair(freq_index(MY, lines), lines)
    across_x = analysis_pair(freq_index(MX, all_planes), all_planes)
    back_x = synthesis_pair(freq_index(MX, all_planes), all_planes)

    def to_owners(rows):
        blocks = rows.reshape(devices, owned_pairs * planes, wide)
        return exchange(blocks).reshape(devices, owned_pairs, planes, 2, channels)

    def to_planes(rows):
        blocks = rows.reshape(devices, planes * owned_pairs, wide)
        got = exchange(blocks).reshape(devices, planes, owned_pairs, 2, channels)
        return got.transpose(1, 0, 2, 3, 4).reshape(planes, MY, MZ, 2, channels)

    depth_part = jnp.dot(features, depth_basis.T, preferred_element_type=jnp.float32).astype(
        jnp.bfloat16
    )
    plane_part = jnp.einsum(
        "cxyaz,yabk->kzxbc",
        depth_part.reshape(channels, planes, lines, 2, MZ),
        across_y,
        preferred_element_type=jnp.float32,
    ).astype(jnp.bfloat16)
    gathered = to_owners(plane_part)
    mode_sums = jnp.einsum(
        "sqpac,spabk->qkbc",
        gathered,
        across_x.reshape(devices, planes, 2, 2, MX),
        preferred_element_type=jnp.float32,
    )
    coeffs = (mode_sums * forward_scale).astype(jnp.bfloat16).reshape(owned_modes, 2, channels)
    spectral = mode_product(coeffs, spectral_weight)
    planes_back = jnp.einsum(
        "qkao,kabx->xqbo",
        spectral.reshape(owned_pairs, MX, 2, channels),
        back_x,
        preferred_element_type=jnp.float32,
    ).astype(jnp.bfloat16)
    planes_here = to_planes(planes_back)
    lines_back = (
        jnp.einsum("xkzao,kaby->xyobz", planes_here, back_y, preferred_element_type=jnp.float32)
        .astype(jnp.bfloat16)
        .reshape(planes, lines, channels, 2 * MZ)
    )
    activated, upstream, lines_grad = middle(
        features, cotangent, lines_back, channel_weight, channel_bias, depth_basis, inverse_scale
    )
    rows_grad = jnp.einsum(
        "xyobz,kaby->kzxao",
        lines_grad.reshape(planes, lines, channels, 2, MZ),
        back_y,
        preferred_element_type=jnp.float32,
    ).astype(jnp.bfloat16)
    gathered_grad = to_owners(rows_grad)
    grad_modes = (
        jnp.einsum(
            "sqpbo,kabsp->qkao",
            gathered_grad,
            back_x.reshape(MX, 2, 2, devices, planes),
            preferred_element_type=jnp.float32,
        )
        .astype(jnp.bfloat16)
        .reshape(owned_modes, 2, channels)
    )
    straight = grad_modes.reshape(owned_modes, wide)
    rotated = jnp.concatenate([grad_modes[:, 1], -grad_modes[:, 0]], 1)
    pairs = jnp.stack([straight, rotated], 1)
    coeff_grad = (
        jnp.einsum("mcj,mbj->mbc", spectral_weight, pairs, preferred_element_type=jnp.float32)
        * forward_scale
    ).astype(jnp.bfloat16)
    plane_grad = jnp.einsum(
        "qkbc,xabk->xqac",
        coeff_grad.reshape(owned_pairs, MX, 2, channels),
        across_x,
        preferred_element_type=jnp.float32,
    ).astype(jnp.bfloat16)
    grad_here = to_planes(plane_grad)
    spectral_grad = (
        jnp.einsum("mac,maj->mcj", coeffs, pairs, preferred_element_type=jnp.float32)
        * weight_scale
    ).astype(jnp.bfloat16)
    depth_grad = (
        jnp.einsum("xkzbc,yabk->xycaz", grad_here, across_y, preferred_element_type=jnp.float32)
        .astype(jnp.bfloat16)
        .reshape(planes, lines, channels, 2 * MZ)
    )
    feature_grad = final(upstream, depth_grad, channel_weight.T, depth_basis)
    return (activated, feature_grad, spectral_grad)


MESH = pl.DeviceIdType.MESH
F32 = jnp.float32
BF16 = jnp.bfloat16
MB = 1024 * 1024


def host_cos_sin(wavenum, length):
    angles = (np.outer(wavenum, np.arange(length)) % length).astype(np.float32) * np.float32(
        2.0 * math.pi / length
    )
    return np.cos(angles), np.sin(angles)


def host_freq(retained, length):
    ladder = np.arange(retained)
    return np.where(ladder < retained // 2, ladder, length - retained + ladder)


def host_minus(retained, length):
    cosine, sine = host_cos_sin(host_freq(retained, length), length)
    cosine, sine = cosine.T, sine.T
    return np.stack([np.stack([cosine, -sine], 1), np.stack([sine, cosine], 1)], 1)


def host_plus(retained, length):
    cosine, sine = host_cos_sin(host_freq(retained, length), length)
    return np.stack([np.stack([cosine, sine], 1), np.stack([-sine, cosine], 1)], 1)


def host_tables(devices, lines, depth_len, channels):
    all_planes = 2 * devices
    two = np.eye(2)
    eight = np.eye(8)
    cosine, sine = host_cos_sin(np.arange(MZ), depth_len)
    depth = np.stack([cosine, -sine], 0)
    z_in = np.einsum("akz,cd->czakd", depth, eight).reshape(8 * depth_len, 16 * MZ)
    minus_y = host_minus(MY, lines).reshape(lines, 2, 2, devices, 2)
    y_in = np.einsum("yabdk,xw->dkbwxay", minus_y, two).reshape(8 * devices, 4 * lines)
    groups = channels // 8
    source = np.arange(MZ * channels).reshape(groups, MZ, 8)
    target = source.transpose(1, 0, 2).reshape(-1)
    order = np.zeros((MZ * channels, MZ * channels))
    order[target, np.arange(MZ * channels)] = 1.0
    minus_x = host_minus(MX, all_planes).reshape(devices, 2, 2, 2, MX)
    x_in = np.einsum("sxabk,hg,jl,p->hkjpbsglax", minus_x, two, two, np.ones(2)).reshape(
        16 * MX, 16 * devices
    )
    swapped = np.stack([minus_x[:, :, :, 1], -minus_x[:, :, :, 0]], 3)
    x_turn = np.einsum("sxabk,hg,jl,p->hkjpbsglax", swapped, two, two, np.ones(2)).reshape(
        16 * MX, 16 * devices
    )
    plus_x = host_plus(MX, all_planes).reshape(MX, 2, 2, devices, 2)
    crossed = np.stack([-plus_x[:, :, 1], plus_x[:, :, 0]], 2)
    both = np.stack([plus_x, crossed], 0)
    x_out = np.einsum("rkabsx,pq,jl->prsjbxklqa", both, two, two).reshape(32 * devices, 8 * MX)
    x_back = np.einsum("kabsx,jl,q->sjbxklqa", plus_x, two, np.ones(2)).reshape(
        8 * devices, 8 * MX
    )
    plus_y = host_plus(MY, lines).reshape(devices, 2, 2, 2, lines)
    y_out = np.einsum("skaby,hg,xw->xbhysgkaw", plus_y, two, two).reshape(8 * lines, 16 * devices)
    tables = dict(
        z_in=z_in, z_out=z_in.T, y_in=y_in, order=order, unorder=order.T, x_in=x_in,
        x_turn=x_turn, x_out=x_out, x_back=x_back, y_out=y_out,
    )
    return {name: jnp.asarray(np.ascontiguousarray(t), BF16) for name, t in tables.items()}


def fdot(left, right):
    return jnp.dot(left, right, preferred_element_type=F32)


def greet(devices):
    me, group = lax.axis_index("gx"), lax.axis_index("grp")
    barrier = pltpu.get_barrier_semaphore()

    @pl.loop(1, devices)
    def _(step):
        pl.semaphore_signal(
            barrier, inc=1, device_id=(group, lax.rem(me + step, devices)), device_id_type=MESH
        )

    def arrived():
        pl.semaphore_wait(barrier, devices - 1)

    return arrived


def swap_start(devices, sent, got, send_sem, recv_sem, stage):
    me, group = lax.axis_index("gx"), lax.axis_index("grp")

    def copy(step):
        target = lax.rem(me + step, devices)
        return pltpu.make_async_remote_copy(
            src_ref=sent.at[target],
            dst_ref=got.at[me],
            send_sem=send_sem.at[stage, step],
            recv_sem=recv_sem.at[stage, step],
            device_id=(group, target),
            device_id_type=MESH,
        )

    @pl.loop(1, devices)
    def _(step):
        copy(step).start()

    got[me] = sent[me]

    def finish():
        @pl.loop(1, devices)
        def _(step):
            copy(step).wait_recv()

    def drained():
        @pl.loop(1, devices)
        def _(step):
            copy(step).wait_send()

    return finish, drained


def to_chunks(devices, lines_ref, y_in, order, sent):
    rows = fdot(y_in[...], lines_ref[...]).astype(BF16)
    rows = fdot(rows, order[...])
    lanes = rows.shape[1]
    halves = [
        rows[:, h * lanes // 2 : (h + 1) * lanes // 2].reshape(devices, 8, lanes // 2)
        for h in range(2)
    ]
    chunk = jnp.concatenate(halves, 1).astype(BF16)
    for u in range(2):
        sent[u] = chunk[:, :, u * lanes // 4 : (u + 1) * lanes // 4]


def mode_block(weights, k_pair, half, pair):
    def one(kx):
        return jnp.concatenate(
            [weights[k2, half * 8 + pair * 2 + parity, kx] for k2 in range(2) for parity in range(2)],
            0,
        )

    return jnp.concatenate([one(2 * k_pair), one(2 * k_pair + 1)], 1)


def iotas():
    row = lax.broadcasted_iota(jnp.int32, (8, 128), 0)
    lane = lax.broadcasted_iota(jnp.int32, (8, 128), 1)
    return row, lane


def weight_copies(weights_hbm, weights, sem):
    def copy(half, pair):
        kz = pl.ds(half * 8 + pair * 2, 2)
        return pltpu.make_async_copy(
            weights_hbm.at[:, kz], weights.at[:, kz], sem.at[half, pair]
        )

    return copy


def fill_kron(channel_weight, out, contract):
    size = out.shape[0]
    channels = channel_weight.shape[0]

    def spread(rows, first, axis):
        shape = (rows, channels) if axis == 0 else (channels, rows)
        long = lax.broadcasted_iota(jnp.int32, shape, axis)
        short = lax.broadcasted_iota(jnp.int32, shape, 1 - axis)
        return jnp.where(long // 16 + first == short, 1.0, 0.0).astype(BF16)

    columns = spread(size, 0, 1)
    line = lax.broadcasted_iota(jnp.int32, (128, size), 0) % 16
    same = line == lax.broadcasted_iota(jnp.int32, (128, size), 1) % 16

    @pl.loop(0, size // 128)
    def _(block):
        rows = lax.dot_general(
            spread(128, block * 8, 0),
            channel_weight[...],
            (((1,), (1 - contract,)), ((), ())),
            preferred_element_type=F32,
        ).astype(BF16)
        out[pl.ds(pl.multiple_of(block * 128, 128), 128), :] = jnp.where(
            same, fdot(rows, columns), 0.0
        ).astype(BF16)


TABLES = (
    "z_in", "y_in", "order", "x_in", "x_out", "y_out", "unorder", "z_out", "x_turn", "x_back",
)
EARLY = 3


def layer_kernel(
    devices, forward_scale, inverse_scale,
    feat_hbm, cot_hbm, weights_hbm, channel_weight, bias, *refs,
):
    number = len(TABLES)
    tables_hbm = dict(zip(TABLES, refs[:number]))
    act, grad, lefts, pairs = refs[number : number + 4]
    tables = dict(zip(TABLES, refs[number + 4 : 2 * number + 4]))
    (
        feat, cot, weights, kron, kron_back, pointwise, lines_part, blocks, spectral,
        up_wide, sent, got, coeffs, modes, turned, mixed,
        feat_sem, load_sem, weight_sem, send_sem, recv_sem,
    ) = refs[2 * number + 4 :]
    channels, planes, lines, depth_len = feat.shape
    groups = channels // 8
    rows = 16
    arrived = greet(devices)
    pieces = feat_sem.shape[0]
    share = channels // pieces

    def load_feat(piece):
        here = pl.ds(piece * share, share)
        return pltpu.make_async_copy(feat_hbm.at[here], feat.at[here], feat_sem.at[piece])

    loads = {
        name: pltpu.make_async_copy(tables_hbm[name], tables[name], load_sem.at[i])
        for i, name in enumerate(TABLES)
    }
    load_cot = pltpu.make_async_copy(cot_hbm, cot, load_sem.at[number])
    loads["z_in"].start()
    for piece in range(pieces):
        load_feat(piece).start()
    for name in TABLES[1:EARLY]:
        loads[name].start()
    weight_copy = weight_copies(weights_hbm, weights, weight_sem)
    loads["z_in"].wait()

    @pl.loop(0, pieces)
    def _(piece):
        load_feat(piece).wait()
        for local in range(share // 8):
            group = piece * (share // 8) + local
            for plane in range(planes):
                wide = jnp.concatenate([feat[group * 8 + i, plane] for i in range(8)], 1)
                part = fdot(wide, tables["z_in"][...]).astype(BF16)
                for a in range(2):
                    lines_part[
                        pl.ds((plane * 2 + a) * lines, lines),
                        pl.ds(pl.multiple_of(group * 128, 128), 128),
                    ] = part[:, a * 128 : (a + 1) * 128]

    loads["x_in"].start()
    for pair in range(2):
        for half in range(2):
            weight_copy(half, pair).start()
    for name in TABLES[EARLY + 1 :]:
        loads[name].start()
    for pair in range(2, 4):
        for half in range(2):
            weight_copy(half, pair).start()
    load_cot.start()
    for name in TABLES[1:EARLY]:
        loads[name].wait()
    to_chunks(devices, lines_part, tables["y_in"], tables["order"], sent.at[0])
    arrived()

    def swap(stage, u):
        return swap_start(
            devices, sent.at[stage, u], got.at[stage, u], send_sem, recv_sem, 2 * stage + u
        )

    ends = [swap(0, u) for u in range(2)]

    def point(block):
        here = pl.ds(pl.multiple_of(block * rows, rows), rows)
        both = jnp.concatenate(
            [feat[:, x, here].reshape(channels * rows, depth_len) for x in range(planes)], 1
        )
        pointwise[block] = fdot(kron[...], both)

    fill_kron(channel_weight, kron, 1)

    @pl.loop(0, 2)
    def _(block):
        point(block)

    for name in TABLES[EARLY:]:
        loads[name].wait()
    row, lane = iotas()
    own = [(row // 2) == (lane // 64 + 2 * k2) for k2 in range(2)]
    low_tall = lax.broadcasted_iota(jnp.int32, (8 * devices, 128), 1) < 64
    low = lane < 64
    direct = low == ((row // 2) % 2 == 0)
    first_line = row < 4
    zero = jnp.zeros((8, 128), F32)

    for u in range(2):
        ends[u][0]()
        source = got[0, u].reshape(16 * devices, 256)
        coeffs[u] = (fdot(tables["x_in"][...], source) * forward_scale).reshape(2, MX, 8, 256)

        @pl.loop(0, 4)
        def _(part):
            half, local = part // 2, part % 2
            weight_copy(half, 2 * u + local).wait()
            span = pl.ds(pl.multiple_of(local * 128, 128), 128)

            def step(k_pair, carry):
                left = []
                for i in range(2):
                    block = coeffs[u, half, 2 * k_pair + i, :, span]
                    left.append(
                        jnp.concatenate([jnp.where(own[k2], block, 0.0) for k2 in range(2)], 1)
                    )
                left = jnp.concatenate(left, 0).astype(BF16)
                out = fdot(left, mode_block(weights, k_pair, half, 2 * u + local))
                out = jnp.concatenate([out[:8, :128], out[8:, 128:]], 0).astype(BF16)
                mixed[half, pl.ds(pl.multiple_of(k_pair * 16, 16), 16), span] = out
                return carry

            lax.fori_loop(0, MX // 2, step, 0, unroll=8)

        halves = []
        for half in range(2):
            every = fdot(tables["x_out"][...], mixed[half])
            size = 8 * devices
            tiles = []
            for local in range(2):
                even, even_x, odd, odd_x = [
                    every[i * size : (i + 1) * size, local * 128 : (local + 1) * 128]
                    for i in range(4)
                ]
                tiles.append(
                    jnp.where(low_tall, even, odd_x)
                    + pltpu.roll(jnp.where(low_tall, odd, even_x), 64, 1)
                )
            halves.append(jnp.concatenate(tiles, 1).reshape(devices, 8, 256))
        sent[1, u] = jnp.concatenate(halves, 1).astype(BF16)
        ends.append(swap(1, u))

    @pl.loop(2, lines // rows)
    def _(block):
        point(block)

    fill_kron(channel_weight, kron_back, 0)

    @pl.loop(0, 2)
    def _(k_half):
        here = pl.ds(k_half * (MX // 2), MX // 2)
        for index in range(8):
            half, u, local = index // 4, (index % 4) // 2, index % 2
            values = coeffs[u, half, here, :, local * 128 : (local + 1) * 128]
            wide = jnp.concatenate(
                [jnp.where(own[k2][None], values, 0.0).reshape(128, 128) for k2 in range(2)], 1
            )
            lefts[index, k_half] = wide.T.astype(BF16)

    load_cot.wait()
    ends[2][0]()
    ends[3][0]()
    to_lines(devices, got.at[1], tables["y_out"], tables["unorder"], blocks)

    @pl.loop(0, lines // rows)
    def _(block):
        line = pl.ds(pl.multiple_of(block * rows, rows), rows)
        spectral[...] = fdot(blocks[block], tables["z_out"][...])

        @pl.loop(0, groups)
        def _(group):
            for plane in range(planes):
                here = pl.ds(pl.multiple_of((plane * groups + group) * rows, rows), rows)
                for i in range(8):
                    o = group * 8 + i
                    hidden = (
                        spectral[here, i * 128 : (i + 1) * 128] * inverse_scale
                        + pointwise[
                            block,
                            pl.ds(pl.multiple_of(o * rows, rows), rows),
                            plane * 128 : (plane + 1) * 128,
                        ]
                        + bias[o]
                    )
                    activated, derivative = gelu_parts(hidden)
                    act[o, plane, line] = activated.astype(BF16)
                    up_wide[block, here, i * 128 : (i + 1) * 128] = (
                        cot[o, plane, line].astype(F32) * derivative
                    ).astype(BF16)

        part = (fdot(up_wide[block], tables["z_in"][...]) * inverse_scale).astype(BF16)
        for plane in range(planes):
            for a in range(2):
                for group in range(groups):
                    first = (plane * groups + group) * rows
                    lines_part[
                        pl.ds(
                            pl.multiple_of((plane * 2 + a) * lines + block * rows, rows), rows
                        ),
                        group * 128 : (group + 1) * 128,
                    ] = part[first : first + rows, a * 128 : (a + 1) * 128]

    to_chunks(devices, lines_part, tables["y_in"], tables["order"], sent.at[2])
    ends += [swap(2, u) for u in range(2)]

    @pl.loop(0, lines // rows)
    def _(block):
        both = []
        for plane in range(planes):
            tiles = []
            for o in range(channels):
                first = (plane * groups + o // 8) * rows
                tiles.append(
                    up_wide[block, first : first + rows, (o % 8) * 128 : (o % 8 + 1) * 128]
                )
            both.append(jnp.concatenate(tiles, 0))
        pointwise[block] = fdot(kron_back[...], jnp.concatenate(both, 1))

    for u in range(2):
        ends[4 + u][0]()
        source = got[2, u].reshape(16 * devices, 256)
        modes[...] = fdot(tables["x_in"][...], source).reshape(2, MX, 8, 256)
        turned[...] = fdot(tables["x_turn"][...], source).reshape(2, MX, 8, 256)

        @pl.loop(0, 4)
        def _(part):
            half, local = part // 2, part % 2
            span = pl.ds(pl.multiple_of(local * 128, 128), 128)

            def step(k_pair, carry):
                here = pl.ds(pl.multiple_of(k_pair * 16, 16), 16)
                tiles = [
                    pair_tile(
                        modes[half, 2 * k_pair + i, :, span],
                        turned[half, 2 * k_pair + i, :, span],
                        low,
                        direct,
                    )
                    for i in range(2)
                ]
                pairs[half * 4 + 2 * u + local, here] = jnp.concatenate(tiles, 0).astype(BF16)
                left = jnp.concatenate(
                    [jnp.concatenate([tiles[0], zero], 1), jnp.concatenate([zero, tiles[1]], 1)], 0
                ).astype(BF16)
                out = lax.dot_general(
                    left,
                    mode_block(weights, k_pair, half, 2 * u + local),
                    (((1,), (1,)), ((), ())),
                    preferred_element_type=F32,
                )
                kept = []
                for i in range(2):
                    here_rows = out[8 * i : 8 * i + 8]
                    kept.append(
                        jnp.where(
                            direct,
                            jnp.where(first_line, here_rows[:, :128], here_rows[:, 128:]),
                            0.0,
                        )
                    )
                mixed[half, here, span] = (jnp.concatenate(kept, 0) * forward_scale).astype(BF16)
                return carry

            lax.fori_loop(0, MX // 2, step, 0, unroll=8)

        sent[3, u] = jnp.concatenate(
            [fdot(tables["x_back"][...], mixed[half]).reshape(devices, 8, 256) for half in range(2)],
            1,
        ).astype(BF16)
        ends.append(swap(3, u))

    ends[6][0]()
    ends[7][0]()
    to_lines(devices, got.at[3], tables["y_out"], tables["unorder"], blocks)

    @pl.loop(0, lines // rows)
    def _(block):
        line = pl.ds(pl.multiple_of(block * rows, rows), rows)
        spectral[...] = fdot(blocks[block], tables["z_out"][...])

        @pl.loop(0, groups)
        def _(group):
            for plane in range(planes):
                here = pl.ds(pl.multiple_of((plane * groups + group) * rows, rows), rows)
                for i in range(8):
                    o = group * 8 + i
                    total = (
                        spectral[here, i * 128 : (i + 1) * 128]
                        + pointwise[
                            block,
                            pl.ds(pl.multiple_of(o * rows, rows), rows),
                            plane * 128 : (plane + 1) * 128,
                        ]
                    )
                    grad[o, plane, line] = total.astype(BF16)

    for end in ends:
        end[1]()


def to_lines(devices, back, y_out, unorder, blocks):
    lines_u = [fdot(y_out[...], back[u].reshape(16 * devices, 256)).astype(BF16) for u in range(2)]
    lines = lines_u[0].shape[0] // 8
    for plane in range(2):
        for part in range(2):
            pieces = []
            for half in range(2):
                first = ((plane * 2 + part) * 2 + half) * lines
                pieces += [lines_u[u][first : first + lines] for u in range(2)]
            rows = fdot(jnp.concatenate(pieces, 1), unorder[...]).astype(BF16)
            groups = rows.shape[1] // 128
            for block in range(lines // 16):
                for group in range(groups):
                    blocks[
                        block,
                        (plane * groups + group) * 16 : (plane * groups + group + 1) * 16,
                        part * 128 : (part + 1) * 128,
                    ] = rows[block * 16 : (block + 1) * 16, group * 128 : (group + 1) * 128]


def pair_tile(straight, other, low, direct):
    return jnp.where(
        direct,
        jnp.where(low, straight, other),
        pltpu.roll(jnp.where(low, other, straight), 64, 1),
    )


def weight_grad_kernel(
    weight_scale, act_in, grad_in, lefts, pairs, act_out, grad_out, out_hbm, buffer, sem, field_sem,
):
    fields = [
        pltpu.make_async_copy(act_in, act_out, field_sem.at[0]),
        pltpu.make_async_copy(grad_in, grad_out, field_sem.at[1]),
    ]
    for copy in fields:
        copy.start()
    block = lax.broadcasted_iota(jnp.int32, (128, 256), 0) // 8
    side = lax.broadcasted_iota(jnp.int32, (128, 256), 1) // 128

    def copy(index, slot):
        return pltpu.make_async_copy(
            buffer.at[slot], out_hbm.at[:, pl.ds(2 * index, 2)], sem.at[slot]
        )

    @pl.loop(0, 8)
    def _(index):
        slot = lax.rem(index, 2)

        @pl.when(index >= 2)
        def _():
            copy(index - 2, slot).wait()

        @pl.loop(0, 2)
        def _(k_half):
            here = pl.ds(pl.multiple_of(k_half * 128, 128), 128)
            right = pairs[index, here].astype(F32) * weight_scale
            right = jnp.concatenate([right, right], 1)
            for i in range(MX // 4):
                kept = jnp.where(block == 2 * i + side, right, 0.0).astype(BF16)
                out = fdot(lefts[index, k_half], kept).astype(BF16)
                for s in range(2):
                    for k2 in range(2):
                        for parity in range(2):
                            first = (k2 * 2 + parity) * 64
                            buffer[slot, k2, parity, k_half * (MX // 2) + 2 * i + s] = out[
                                first : first + 64, s * 128 : (s + 1) * 128
                            ]

        copy(index, slot).start()

    copy(6, 0).wait()
    copy(7, 1).wait()
    for one in fields:
        one.wait()


def vmem(*shape, dtype=BF16):
    return pltpu.VMEM(shape, dtype)


WHOLE = pl.BlockSpec(memory_space=pltpu.VMEM)
ANYWHERE = pl.BlockSpec(memory_space=pl.ANY)


def block_body(features, cotangent, spectral_weight, channel_weight, channel_bias):
    channels, planes, lines, depth_len = features.shape
    devices = lax.axis_size("gx")
    all_planes = planes * devices
    number = MX * MY * MZ
    forward_scale = 1.0 / math.sqrt(all_planes * lines * depth_len)
    inverse_scale = 1.0 / math.sqrt(number)
    weight_scale = math.sqrt(number / (all_planes * lines * depth_len))
    tables = host_tables(devices, lines, depth_len, channels)
    tables = [tables[name] for name in TABLES]
    weights = spectral_weight.reshape(2, MZ, MX, channels, 2 * channels)
    wide = MZ * channels
    rows = 16
    steps = lines // rows
    dma = pltpu.SemaphoreType.DMA
    like = jax.ShapeDtypeStruct(features.shape, BF16)
    lefts = (8, 2, 256, 128)
    pairs = (8, 8 * MX, 128)
    activated, feature_grad, left, pair = pl.pallas_call(
        functools.partial(layer_kernel, devices, forward_scale, inverse_scale),
        out_shape=[
            vmem(*features.shape), vmem(*features.shape), vmem(*lefts), vmem(*pairs)
        ],
        in_specs=[ANYWHERE] * 3
        + [WHOLE, pl.BlockSpec(memory_space=pltpu.SMEM)]
        + [ANYWHERE] * len(tables),
        out_specs=[WHOLE] * 4,
        scratch_shapes=[vmem(*table.shape) for table in tables]
        + [
            vmem(*features.shape),
            vmem(*features.shape),
            vmem(*weights.shape),
            vmem(channels * rows, channels * rows),
            vmem(channels * rows, channels * rows),
            vmem(steps, channels * rows, planes * depth_len, dtype=F32),
            vmem(4 * lines, wide),
            vmem(steps, 2 * wide // 8, 256),
            vmem(planes * channels * 2, 8 * depth_len, dtype=F32),
            vmem(steps, planes * channels * 2, 8 * depth_len),
            vmem(4, 2, devices, 16, 256),
            vmem(4, 2, devices, 16, 256),
            vmem(2, 2, MX, 8, 256, dtype=F32),
            vmem(2, MX, 8, 256, dtype=F32),
            vmem(2, MX, 8, 256, dtype=F32),
            vmem(2, 8 * MX, 256),
            dma((4,)),
            dma((len(tables) + 1,)),
            dma((2, 4)),
            dma((8, devices)),
            dma((8, devices)),
        ],
        compiler_params=pltpu.CompilerParams(
            collective_id=0, has_side_effects=True, vmem_limit_bytes=56 * MB
        ),
        name="layer",
    )(features, cotangent, weights, channel_weight, channel_bias, *tables)
    activated, feature_grad, spectral_grad = pl.pallas_call(
        functools.partial(weight_grad_kernel, weight_scale),
        out_shape=[like, like, jax.ShapeDtypeStruct(weights.shape, BF16)],
        in_specs=[WHOLE] * 4,
        out_specs=[ANYWHERE] * 3,
        scratch_shapes=[
            vmem(2, 2, 2, MX, channels, 2 * channels),
            dma((2,)),
            dma((2,)),
        ],
        compiler_params=pltpu.CompilerParams(vmem_limit_bytes=40 * MB),
        name="weight_grad",
    )(activated, feature_grad, left, pair)
    return (activated, feature_grad, spectral_grad.reshape(spectral_weight.shape))


def body(features, cotangent, spectral_weight, channel_weight, channel_bias):
    channels, planes, lines, depth_len = features.shape
    devices = lax.axis_size("gx")
    fits = (
        2 * devices == MY
        and planes == 2
        and channels == 64
        and lines == 64
        and depth_len == 128
        and spectral_weight.shape[0] == 2 * MZ * MX
    )
    chosen = block_body if fits else plain_body
    return chosen(features, cotangent, spectral_weight, channel_weight, channel_bias)


def solution(mesh):
    in_specs = (
        P("grp", "gx", None, None),
        P("grp", "gx", None, None),
        P("gx", None, None),
        P(),
        P(),
    )
    out_specs = (
        P("grp", "gx", None, None),
        P("grp", "gx", None, None),
        P(("grp", "gx"), None, None),
    )
    return jax.shard_map(body, mesh=mesh, in_specs=in_specs, out_specs=out_specs, check_vma=False)
```

```python
import functools
import math

import jax
import jax.numpy as jnp
import numpy as np
from jax import lax
from jax.experimental import pallas as pl
from jax.experimental.pallas import tpu as pltpu
from jax.sharding import PartitionSpec as P

MX = 32
MY = 32
MZ = 16


SQRT_TWO_PI = math.sqrt(2.0 / math.pi)
CUBIC_COEF = 0.044715


def freq_index(retained, length):
    ladder = jnp.arange(retained, dtype=jnp.int32)
    return jnp.where(ladder < retained // 2, ladder, length - retained + ladder)


def cos_sin(wavenum, length):
    points = jnp.arange(length, dtype=jnp.int32)
    angles = (wavenum[:, None] * points[None, :] % length).astype(jnp.float32) * (
        2.0 * math.pi / length
    )
    return (jnp.cos(angles), jnp.sin(angles))


def analysis_pair(wavenum, length):
    cosine, sine_wave = cos_sin(wavenum, length)
    cosine, sine_wave = (cosine.T, sine_wave.T)
    return jnp.stack(
        [jnp.stack([cosine, -sine_wave], 1), jnp.stack([sine_wave, cosine], 1)], 1
    ).astype(jnp.bfloat16)


def synthesis_pair(wavenum, length):
    cosine, sine_wave = cos_sin(wavenum, length)
    return jnp.stack(
        [jnp.stack([cosine, sine_wave], 1), jnp.stack([-sine_wave, cosine], 1)], 1
    ).astype(jnp.bfloat16)


def depth_table(retained, length):
    cosine, sine_wave = cos_sin(jnp.arange(retained, dtype=jnp.int32), length)
    return jnp.concatenate([cosine, -sine_wave], 0).astype(jnp.bfloat16)


def gelu_parts(inputs):
    squared = inputs * inputs
    slope = SQRT_TWO_PI * CUBIC_COEF
    tangent = jnp.tanh(inputs * (SQRT_TWO_PI + slope * squared))
    half = 0.5 + 0.5 * tangent
    output = inputs * half
    derivative = half + output * (1.0 - tangent) * (SQRT_TWO_PI + 3.0 * slope * squared)
    return (output, derivative)


def mode_product(coeffs, weights):
    channels = weights.shape[1]
    halves = jnp.einsum("mac,mcj->amj", coeffs, weights, preferred_element_type=jnp.float32)
    real_out = halves[0, :, :channels] - halves[1, :, channels:]
    imag_out = halves[0, :, channels:] + halves[1, :, :channels]
    return jnp.stack([real_out, imag_out], 1).astype(jnp.bfloat16)


def exchange(blocks):
    return lax.all_to_all(blocks, "gx", 0, 0, tiled=True)


def middle_kernel(
    scale, feat_ref, cot_ref, lines_ref, weight_ref, bias_ref, basis_ref, act_ref, up_ref, grad_ref
):
    channels, _, rows, depth_len = feat_ref.shape
    spectral = jnp.dot(
        lines_ref[0].reshape(rows * channels, lines_ref.shape[3]),
        basis_ref[...],
        preferred_element_type=jnp.float32,
    ).reshape(rows, channels, depth_len)
    feats = jnp.swapaxes(feat_ref[:, 0].astype(jnp.float32), 0, 1).astype(jnp.bfloat16)
    cots = jnp.swapaxes(cot_ref[:, 0].astype(jnp.float32), 0, 1)
    acts = []
    for row in range(rows):
        pointwise = jnp.dot(weight_ref[...], feats[row], preferred_element_type=jnp.float32)
        hidden = spectral[row] * scale + pointwise + bias_ref[...]
        activated, derivative = gelu_parts(hidden)
        acts.append(activated)
        up_ref[0, row] = (cots[row] * derivative).astype(jnp.bfloat16)
    act_ref[:, 0] = jnp.swapaxes(jnp.stack(acts, 0), 0, 1).astype(jnp.bfloat16)
    grad = lax.dot_general(
        up_ref[0].reshape(rows * channels, depth_len),
        basis_ref[...],
        (((1,), (1,)), ((), ())),
        preferred_element_type=jnp.float32,
    )
    grad_ref[0] = (grad * scale).astype(jnp.bfloat16).reshape(rows, channels, lines_ref.shape[3])


def final_kernel(up_ref, depth_ref, weight_ref, basis_ref, out_ref):
    _, rows, channels, depth_len = up_ref.shape
    spectral = jnp.dot(
        depth_ref[0].reshape(rows * channels, depth_ref.shape[3]),
        basis_ref[...],
        preferred_element_type=jnp.float32,
    ).reshape(rows, channels, depth_len)
    totals = []
    for row in range(rows):
        back = jnp.dot(weight_ref[...], up_ref[0, row], preferred_element_type=jnp.float32)
        totals.append(spectral[row] + back)
    out_ref[:, 0] = jnp.swapaxes(jnp.stack(totals, 0), 0, 1).astype(jnp.bfloat16)


ROWS = 16


def middle(features, cotangent, lines_back, channel_weight, channel_bias, depth_basis, scale):
    channels, planes, lines, depth_len = features.shape
    parts = lines_back.shape[3]
    field = pl.BlockSpec((channels, 1, ROWS, depth_len), lambda x, y: (0, x, y, 0))
    turned = pl.BlockSpec((1, ROWS, channels, depth_len), lambda x, y: (x, y, 0, 0))
    narrow = pl.BlockSpec((1, ROWS, channels, parts), lambda x, y: (x, y, 0, 0))
    count = features.size
    return pl.pallas_call(
        functools.partial(middle_kernel, scale),
        grid=(planes, lines // ROWS),
        in_specs=[
            field,
            field,
            narrow,
            pl.BlockSpec((channels, channels), lambda x, y: (0, 0)),
            pl.BlockSpec((channels, 1), lambda x, y: (0, 0)),
            pl.BlockSpec((parts, depth_len), lambda x, y: (0, 0)),
        ],
        out_specs=[field, turned, narrow],
        out_shape=[
            jax.ShapeDtypeStruct(features.shape, jnp.bfloat16),
            jax.ShapeDtypeStruct((planes, lines, channels, depth_len), jnp.bfloat16),
            jax.ShapeDtypeStruct((planes, lines, channels, parts), jnp.bfloat16),
        ],
        compiler_params=pltpu.CompilerParams(vmem_limit_bytes=56 * 1024 * 1024),
        cost_estimate=pl.CostEstimate(
            flops=count * 2 * (channels + 2 * parts), bytes_accessed=count * 8, transcendentals=count
        ),
    )(features, cotangent, lines_back, channel_weight, channel_bias[:, None], depth_basis)


def final(upstream, depth_grad, weight_back, depth_basis):
    planes, lines, channels, depth_len = upstream.shape
    parts = depth_grad.shape[3]
    count = upstream.size
    return pl.pallas_call(
        final_kernel,
        grid=(planes, lines // ROWS),
        in_specs=[
            pl.BlockSpec((1, ROWS, channels, depth_len), lambda x, y: (x, y, 0, 0)),
            pl.BlockSpec((1, ROWS, channels, parts), lambda x, y: (x, y, 0, 0)),
            pl.BlockSpec((channels, channels), lambda x, y: (0, 0)),
            pl.BlockSpec((parts, depth_len), lambda x, y: (0, 0)),
        ],
        out_specs=pl.BlockSpec((channels, 1, ROWS, depth_len), lambda x, y: (0, x, y, 0)),
        out_shape=jax.ShapeDtypeStruct((channels, planes, lines, depth_len), jnp.bfloat16),
        compiler_params=pltpu.CompilerParams(vmem_limit_bytes=32 * 1024 * 1024),
        cost_estimate=pl.CostEstimate(
            flops=count * 2 * (channels + parts), bytes_accessed=count * 4, transcendentals=0
        ),
    )(upstream, depth_grad, weight_back, depth_basis)


def plain_body(features, cotangent, spectral_weight, channel_weight, channel_bias):
    channels, planes, lines, depth_len = features.shape
    devices = lax.axis_size("gx")
    all_planes = planes * devices
    owned_modes = spectral_weight.shape[0]
    wave_pairs = MY * MZ
    owned_pairs = owned_modes // MX
    wide = 2 * channels
    forward_scale = 1.0 / math.sqrt(all_planes * lines * depth_len)
    inverse_scale = 1.0 / math.sqrt(MX * wave_pairs)
    weight_scale = math.sqrt(MX * wave_pairs / (all_planes * lines * depth_len))
    depth_basis = depth_table(MZ, depth_len)
    across_y = analysis_pair(freq_index(MY, lines), lines)
    back_y = synthesis_pair(freq_index(MY, lines), lines)
    across_x = analysis_pair(freq_index(MX, all_planes), all_planes)
    back_x = synthesis_pair(freq_index(MX, all_planes), all_planes)

    def to_owners(rows):
        blocks = rows.reshape(devices, owned_pairs * planes, wide)
        return exchange(blocks).reshape(devices, owned_pairs, planes, 2, channels)

    def to_planes(rows):
        blocks = rows.reshape(devices, planes * owned_pairs, wide)
        got = exchange(blocks).reshape(devices, planes, owned_pairs, 2, channels)
        return got.transpose(1, 0, 2, 3, 4).reshape(planes, MY, MZ, 2, channels)

    depth_part = jnp.dot(features, depth_basis.T, preferred_element_type=jnp.float32).astype(
        jnp.bfloat16
    )
    plane_part = jnp.einsum(
        "cxyaz,yabk->kzxbc",
        depth_part.reshape(channels, planes, lines, 2, MZ),
        across_y,
        preferred_element_type=jnp.float32,
    ).astype(jnp.bfloat16)
    gathered = to_owners(plane_part)
    mode_sums = jnp.einsum(
        "sqpac,spabk->qkbc",
        gathered,
        across_x.reshape(devices, planes, 2, 2, MX),
        preferred_element_type=jnp.float32,
    )
    coeffs = (mode_sums * forward_scale).astype(jnp.bfloat16).reshape(owned_modes, 2, channels)
    spectral = mode_product(coeffs, spectral_weight)
    planes_back = jnp.einsum(
        "qkao,kabx->xqbo",
        spectral.reshape(owned_pairs, MX, 2, channels),
        back_x,
        preferred_element_type=jnp.float32,
    ).astype(jnp.bfloat16)
    planes_here = to_planes(planes_back)
    lines_back = (
        jnp.einsum("xkzao,kaby->xyobz", planes_here, back_y, preferred_element_type=jnp.float32)
        .astype(jnp.bfloat16)
        .reshape(planes, lines, channels, 2 * MZ)
    )
    activated, upstream, lines_grad = middle(
        features, cotangent, lines_back, channel_weight, channel_bias, depth_basis, inverse_scale
    )
    rows_grad = jnp.einsum(
        "xyobz,kaby->kzxao",
        lines_grad.reshape(planes, lines, channels, 2, MZ),
        back_y,
        preferred_element_type=jnp.float32,
    ).astype(jnp.bfloat16)
    gathered_grad = to_owners(rows_grad)
    grad_modes = (
        jnp.einsum(
            "sqpbo,kabsp->qkao",
            gathered_grad,
            back_x.reshape(MX, 2, 2, devices, planes),
            preferred_element_type=jnp.float32,
        )
        .astype(jnp.bfloat16)
        .reshape(owned_modes, 2, channels)
    )
    straight = grad_modes.reshape(owned_modes, wide)
    rotated = jnp.concatenate([grad_modes[:, 1], -grad_modes[:, 0]], 1)
    pairs = jnp.stack([straight, rotated], 1)
    coeff_grad = (
        jnp.einsum("mcj,mbj->mbc", spectral_weight, pairs, preferred_element_type=jnp.float32)
        * forward_scale
    ).astype(jnp.bfloat16)
    plane_grad = jnp.einsum(
        "qkbc,xabk->xqac",
        coeff_grad.reshape(owned_pairs, MX, 2, channels),
        across_x,
        preferred_element_type=jnp.float32,
    ).astype(jnp.bfloat16)
    grad_here = to_planes(plane_grad)
    spectral_grad = (
        jnp.einsum("mac,maj->mcj", coeffs, pairs, preferred_element_type=jnp.float32)
        * weight_scale
    ).astype(jnp.bfloat16)
    depth_grad = (
        jnp.einsum("xkzbc,yabk->xycaz", grad_here, across_y, preferred_element_type=jnp.float32)
        .astype(jnp.bfloat16)
        .reshape(planes, lines, channels, 2 * MZ)
    )
    feature_grad = final(upstream, depth_grad, channel_weight.T, depth_basis)
    return (activated, feature_grad, spectral_grad)


MESH = pl.DeviceIdType.MESH
F32 = jnp.float32
BF16 = jnp.bfloat16
MB = 1024 * 1024


def host_cos_sin(wavenum, length):
    angles = (np.outer(wavenum, np.arange(length)) % length).astype(np.float32) * np.float32(
        2.0 * math.pi / length
    )
    return np.cos(angles), np.sin(angles)


def host_freq(retained, length):
    ladder = np.arange(retained)
    return np.where(ladder < retained // 2, ladder, length - retained + ladder)


def host_minus(retained, length):
    cosine, sine = host_cos_sin(host_freq(retained, length), length)
    cosine, sine = cosine.T, sine.T
    return np.stack([np.stack([cosine, -sine], 1), np.stack([sine, cosine], 1)], 1)


def host_plus(retained, length):
    cosine, sine = host_cos_sin(host_freq(retained, length), length)
    return np.stack([np.stack([cosine, sine], 1), np.stack([-sine, cosine], 1)], 1)


def host_tables(devices, lines, depth_len, channels):
    all_planes = 2 * devices
    two = np.eye(2)
    eight = np.eye(8)
    cosine, sine = host_cos_sin(np.arange(MZ), depth_len)
    depth = np.stack([cosine, -sine], 0)
    z_in = np.einsum("akz,cd->czakd", depth, eight).reshape(8 * depth_len, 16 * MZ)
    minus_y = host_minus(MY, lines).reshape(lines, 2, 2, devices, 2)
    y_in = np.einsum("yabdk,xw->dkbwxay", minus_y, two).reshape(8 * devices, 4 * lines)
    groups = channels // 8
    source = np.arange(MZ * channels).reshape(groups, MZ, 8)
    target = source.transpose(1, 0, 2).reshape(-1)
    order = np.zeros((MZ * channels, MZ * channels))
    order[target, np.arange(MZ * channels)] = 1.0
    minus_x = host_minus(MX, all_planes).reshape(devices, 2, 2, 2, MX)
    x_in = np.einsum("sxabk,hg,jl,p->hkjpbsglax", minus_x, two, two, np.ones(2)).reshape(
        16 * MX, 16 * devices
    )
    swapped = np.stack([minus_x[:, :, :, 1], -minus_x[:, :, :, 0]], 3)
    x_turn = np.einsum("sxabk,hg,jl,p->hkjpbsglax", swapped, two, two, np.ones(2)).reshape(
        16 * MX, 16 * devices
    )
    plus_x = host_plus(MX, all_planes).reshape(MX, 2, 2, devices, 2)
    crossed = np.stack([-plus_x[:, :, 1], plus_x[:, :, 0]], 2)
    both = np.stack([plus_x, crossed], 0)
    x_out = np.einsum("rkabsx,pq,jl->prsjbxklqa", both, two, two).reshape(32 * devices, 8 * MX)
    x_back = np.einsum("kabsx,jl,q->sjbxklqa", plus_x, two, np.ones(2)).reshape(
        8 * devices, 8 * MX
    )
    plus_y = host_plus(MY, lines).reshape(devices, 2, 2, 2, lines)
    y_out = np.einsum("skaby,hg,xw->xbhysgkaw", plus_y, two, two).reshape(8 * lines, 16 * devices)
    tables = dict(
        z_in=z_in, z_out=z_in.T, y_in=y_in, order=order, unorder=order.T, x_in=x_in,
        x_turn=x_turn, x_out=x_out, x_back=x_back, y_out=y_out,
    )
    return {name: jnp.asarray(np.ascontiguousarray(t), BF16) for name, t in tables.items()}


def fdot(left, right):
    return jnp.dot(left, right, preferred_element_type=F32)


def greet(devices):
    me, group = lax.axis_index("gx"), lax.axis_index("grp")
    barrier = pltpu.get_barrier_semaphore()

    @pl.loop(1, devices)
    def _(step):
        pl.semaphore_signal(
            barrier, inc=1, device_id=(group, lax.rem(me + step, devices)), device_id_type=MESH
        )

    def arrived():
        pl.semaphore_wait(barrier, devices - 1)

    return arrived


def swap_start(devices, sent, got, send_sem, recv_sem, stage):
    me, group = lax.axis_index("gx"), lax.axis_index("grp")

    def copy(step):
        target = lax.rem(me + step, devices)
        return pltpu.make_async_remote_copy(
            src_ref=sent.at[target],
            dst_ref=got.at[me],
            send_sem=send_sem.at[stage, step],
            recv_sem=recv_sem.at[stage, step],
            device_id=(group, target),
            device_id_type=MESH,
        )

    @pl.loop(1, devices)
    def _(step):
        copy(step).start()

    got[me] = sent[me]

    def finish():
        @pl.loop(1, devices)
        def _(step):
            copy(step).wait_recv()

    def drained():
        @pl.loop(1, devices)
        def _(step):
            copy(step).wait_send()

    return finish, drained


def to_chunks(devices, lines_ref, y_in, order, sent):
    rows = fdot(y_in[...], lines_ref[...]).astype(BF16)
    rows = fdot(rows, order[...])
    lanes = rows.shape[1]
    halves = [
        rows[:, h * lanes // 2 : (h + 1) * lanes // 2].reshape(devices, 8, lanes // 2)
        for h in range(2)
    ]
    chunk = jnp.concatenate(halves, 1).astype(BF16)
    for u in range(2):
        sent[u] = chunk[:, :, u * lanes // 4 : (u + 1) * lanes // 4]


def mode_block(weights, k_pair, half, pair):
    def one(kx):
        return jnp.concatenate(
            [weights[k2, half * 8 + pair * 2 + parity, kx] for k2 in range(2) for parity in range(2)],
            0,
        )

    return jnp.concatenate([one(2 * k_pair), one(2 * k_pair + 1)], 1)


def iotas():
    row = lax.broadcasted_iota(jnp.int32, (8, 128), 0)
    lane = lax.broadcasted_iota(jnp.int32, (8, 128), 1)
    return row, lane


def weight_copies(weights_hbm, weights, sem):
    def copy(half, pair):
        kz = pl.ds(half * 8 + pair * 2, 2)
        return pltpu.make_async_copy(
            weights_hbm.at[:, kz], weights.at[:, kz], sem.at[half, pair]
        )

    return copy


def fill_kron(channel_weight, out, contract):
    size = out.shape[0]
    channels = channel_weight.shape[0]

    def spread(rows, first, axis):
        shape = (rows, channels) if axis == 0 else (channels, rows)
        long = lax.broadcasted_iota(jnp.int32, shape, axis)
        short = lax.broadcasted_iota(jnp.int32, shape, 1 - axis)
        return jnp.where(long // 16 + first == short, 1.0, 0.0).astype(BF16)

    columns = spread(size, 0, 1)
    line = lax.broadcasted_iota(jnp.int32, (128, size), 0) % 16
    same = line == lax.broadcasted_iota(jnp.int32, (128, size), 1) % 16

    @pl.loop(0, size // 128)
    def _(block):
        rows = lax.dot_general(
            spread(128, block * 8, 0),
            channel_weight[...],
            (((1,), (1 - contract,)), ((), ())),
            preferred_element_type=F32,
        ).astype(BF16)
        out[pl.ds(pl.multiple_of(block * 128, 128), 128), :] = jnp.where(
            same, fdot(rows, columns), 0.0
        ).astype(BF16)


TABLES = (
    "z_in", "y_in", "order", "x_in", "x_out", "y_out", "unorder", "z_out", "x_turn", "x_back",
)
EARLY = 3


def layer_kernel(
    devices, forward_scale, inverse_scale, weight_scale,
    feat_hbm, cot_hbm, weights_hbm, channel_weight, bias, *refs,
):
    number = len(TABLES)
    tables_hbm = dict(zip(TABLES, refs[:number]))
    act, grad, weights, lefts, pairs = refs[number : number + 5]
    tables = dict(zip(TABLES, refs[number + 5 : 2 * number + 5]))
    (
        feat, cot, kron, kron_back, pointwise, lines_part, blocks, spectral,
        up_wide, sent, got, coeffs, modes, turned, mixed,
        feat_sem, load_sem, weight_sem, send_sem, recv_sem,
    ) = refs[2 * number + 5 :]
    channels, planes, lines, depth_len = feat.shape
    groups = channels // 8
    rows = 16
    arrived = greet(devices)
    pieces = feat_sem.shape[0]
    share = channels // pieces

    def load_feat(piece):
        here = pl.ds(piece * share, share)
        return pltpu.make_async_copy(feat_hbm.at[here], feat.at[here], feat_sem.at[piece])

    loads = {
        name: pltpu.make_async_copy(tables_hbm[name], tables[name], load_sem.at[i])
        for i, name in enumerate(TABLES)
    }
    load_cot = pltpu.make_async_copy(cot_hbm, cot, load_sem.at[number])
    loads["z_in"].start()
    for piece in range(pieces):
        load_feat(piece).start()
    for name in TABLES[1:EARLY]:
        loads[name].start()
    weight_copy = weight_copies(weights_hbm, weights, weight_sem)
    loads["z_in"].wait()

    @pl.loop(0, pieces)
    def _(piece):
        load_feat(piece).wait()
        for local in range(share // 8):
            group = piece * (share // 8) + local
            for plane in range(planes):
                wide = jnp.concatenate([feat[group * 8 + i, plane] for i in range(8)], 1)
                part = fdot(wide, tables["z_in"][...]).astype(BF16)
                for a in range(2):
                    lines_part[
                        pl.ds((plane * 2 + a) * lines, lines),
                        pl.ds(pl.multiple_of(group * 128, 128), 128),
                    ] = part[:, a * 128 : (a + 1) * 128]

    loads["x_in"].start()
    for pair in range(2):
        for half in range(2):
            weight_copy(half, pair).start()
    for name in TABLES[EARLY + 1 :]:
        loads[name].start()
    for pair in range(2, 4):
        for half in range(2):
            weight_copy(half, pair).start()
    load_cot.start()
    for name in TABLES[1:EARLY]:
        loads[name].wait()
    to_chunks(devices, lines_part, tables["y_in"], tables["order"], sent.at[0])
    arrived()

    def swap(stage, u):
        return swap_start(
            devices, sent.at[stage, u], got.at[stage, u], send_sem, recv_sem, 2 * stage + u
        )

    ends = [swap(0, 0)]

    def point(block):
        here = pl.ds(pl.multiple_of(block * rows, rows), rows)
        both = jnp.concatenate(
            [feat[:, x, here].reshape(channels * rows, depth_len) for x in range(planes)], 1
        )
        total = fdot(kron[...], both)
        for o in range(channels):
            here = slice(o * rows, (o + 1) * rows)
            pointwise[block, here] = total[here] + bias[o]

    fill_kron(channel_weight, kron, 1)

    @pl.loop(0, 1)
    def _(block):
        point(block)

    ends[0][1]()
    ends.append(swap(0, 1))

    @pl.loop(1, 2)
    def _(block):
        point(block)

    for name in TABLES[EARLY:]:
        loads[name].wait()
    row, lane = iotas()
    own = [(row // 2) == (lane // 64 + 2 * k2) for k2 in range(2)]
    low_tall = lax.broadcasted_iota(jnp.int32, (8 * devices, 128), 1) < 64
    low = lane < 64
    direct = low == ((row // 2) % 2 == 0)
    first_line = row < 4
    zero = jnp.zeros((8, 128), F32)

    for u in range(2):
        ends[u][0]()
        source = got[0, u].reshape(16 * devices, 256)
        coeffs[u] = (fdot(tables["x_in"][...], source) * forward_scale).reshape(2, MX, 8, 256)

        @pl.loop(0, 4)
        def _(part):
            half, local = part // 2, part % 2
            weight_copy(half, 2 * u + local).wait()
            span = pl.ds(pl.multiple_of(local * 128, 128), 128)

            def step(k_pair, carry):
                left = []
                for i in range(2):
                    block = coeffs[u, half, 2 * k_pair + i, :, span]
                    left.append(
                        jnp.concatenate([jnp.where(own[k2], block, 0.0) for k2 in range(2)], 1)
                    )
                left = jnp.concatenate(left, 0).astype(BF16)
                out = fdot(left, mode_block(weights, k_pair, half, 2 * u + local))
                out = jnp.concatenate([out[:8, :128], out[8:, 128:]], 0).astype(BF16)
                mixed[half, pl.ds(pl.multiple_of(k_pair * 16, 16), 16), span] = out
                return carry

            lax.fori_loop(0, MX // 2, step, 0, unroll=16)

        halves = []
        for half in range(2):
            every = fdot(tables["x_out"][...], mixed[half]) * inverse_scale
            size = 8 * devices
            tiles = []
            for local in range(2):
                even, even_x, odd, odd_x = [
                    every[i * size : (i + 1) * size, local * 128 : (local + 1) * 128]
                    for i in range(4)
                ]
                tiles.append(
                    jnp.where(low_tall, even, odd_x)
                    + pltpu.roll(jnp.where(low_tall, odd, even_x), 64, 1)
                )
            halves.append(jnp.concatenate(tiles, 1).reshape(devices, 8, 256))
        sent[1, u] = jnp.concatenate(halves, 1).astype(BF16)
        ends.append(swap(1, u))

    @pl.loop(2, lines // rows)
    def _(block):
        point(block)

    fill_kron(channel_weight, kron_back, 0)

    @pl.loop(0, 2)
    def _(k_half):
        here = pl.ds(k_half * (MX // 2), MX // 2)
        for index in range(8):
            half, u, local = index // 4, (index % 4) // 2, index % 2
            values = coeffs[u, half, here, :, local * 128 : (local + 1) * 128]
            wide = jnp.concatenate(
                [jnp.where(own[k2][None], values, 0.0).reshape(128, 128) for k2 in range(2)], 1
            )
            lefts[index, k_half] = wide.T.astype(BF16)

    load_cot.wait()
    ends[2][0]()
    ends[3][0]()
    to_lines(devices, got.at[1], tables["y_out"], tables["unorder"], blocks)

    @pl.loop(0, lines // rows)
    def _(block):
        line = pl.ds(pl.multiple_of(block * rows, rows), rows)
        spectral[...] = fdot(blocks[block], tables["z_out"][...])

        @pl.loop(0, groups, unroll=True)
        def _(group):
            for plane in range(planes):
                here = pl.ds(pl.multiple_of((plane * groups + group) * rows, rows), rows)
                for i in range(8):
                    o = group * 8 + i
                    hidden = (
                        spectral[here, i * 128 : (i + 1) * 128]
                        + pointwise[
                            block,
                            pl.ds(pl.multiple_of(o * rows, rows), rows),
                            plane * 128 : (plane + 1) * 128,
                        ]
                    )
                    activated, derivative = gelu_parts(hidden)
                    act[o, plane, line] = activated.astype(BF16)
                    up_wide[block, here, i * 128 : (i + 1) * 128] = (
                        cot[o, plane, line].astype(F32) * derivative
                    ).astype(BF16)

        part = (fdot(up_wide[block], tables["z_in"][...]) * inverse_scale).astype(BF16)
        for plane in range(planes):
            for a in range(2):
                for group in range(groups):
                    first = (plane * groups + group) * rows
                    lines_part[
                        pl.ds(
                            pl.multiple_of((plane * 2 + a) * lines + block * rows, rows), rows
                        ),
                        group * 128 : (group + 1) * 128,
                    ] = part[first : first + rows, a * 128 : (a + 1) * 128]

    to_chunks(devices, lines_part, tables["y_in"], tables["order"], sent.at[2])
    ends.append(swap(2, 0))

    def point_back(block):
        both = []
        for plane in range(planes):
            tiles = []
            for o in range(channels):
                first = (plane * groups + o // 8) * rows
                tiles.append(
                    up_wide[block, first : first + rows, (o % 8) * 128 : (o % 8 + 1) * 128]
                )
            both.append(jnp.concatenate(tiles, 0))
        pointwise[block] = fdot(kron_back[...], jnp.concatenate(both, 1))

    pl.loop(0, 3)(point_back)
    ends[4][1]()
    ends.append(swap(2, 1))
    pl.loop(3, 4)(point_back)

    for u in range(2):
        ends[4 + u][0]()
        source = got[2, u].reshape(16 * devices, 256)
        modes[...] = fdot(tables["x_in"][...], source).reshape(2, MX, 8, 256)
        turned[...] = fdot(tables["x_turn"][...], source).reshape(2, MX, 8, 256)

        @pl.loop(0, 4)
        def _(part):
            half, local = part // 2, part % 2
            span = pl.ds(pl.multiple_of(local * 128, 128), 128)

            def step(k_pair, carry):
                here = pl.ds(pl.multiple_of(k_pair * 16, 16), 16)
                tiles = [
                    pair_tile(
                        modes[half, 2 * k_pair + i, :, span],
                        turned[half, 2 * k_pair + i, :, span],
                        low,
                        direct,
                    )
                    for i in range(2)
                ]
                pairs[half * 4 + 2 * u + local, here] = jnp.concatenate(tiles, 0).astype(BF16)
                left = jnp.concatenate(
                    [jnp.concatenate([tiles[0], zero], 1), jnp.concatenate([zero, tiles[1]], 1)], 0
                ).astype(BF16)
                out = lax.dot_general(
                    left,
                    mode_block(weights, k_pair, half, 2 * u + local),
                    (((1,), (1,)), ((), ())),
                    preferred_element_type=F32,
                )
                kept = []
                for i in range(2):
                    here_rows = out[8 * i : 8 * i + 8]
                    kept.append(
                        jnp.where(
                            direct,
                            jnp.where(first_line, here_rows[:, :128], here_rows[:, 128:]),
                            0.0,
                        )
                    )
                mixed[half, here, span] = (jnp.concatenate(kept, 0) * forward_scale).astype(BF16)
                return carry

            lax.fori_loop(0, MX // 2, step, 0, unroll=16)

        sent[3, u] = jnp.concatenate(
            [fdot(tables["x_back"][...], mixed[half]).reshape(devices, 8, 256) for half in range(2)],
            1,
        ).astype(BF16)
        ends.append(swap(3, u))

    for index in (0, 1, 4, 5):
        weight_grad_block(
            weight_scale, lefts.at[index], pairs.at[index], weights.at[:, 2 * index : 2 * index + 2]
        )
    ends[6][0]()
    ends[7][0]()
    to_lines(devices, got.at[3], tables["y_out"], tables["unorder"], blocks)

    @pl.loop(0, lines // rows)
    def _(block):
        line = pl.ds(pl.multiple_of(block * rows, rows), rows)
        spectral[...] = fdot(blocks[block], tables["z_out"][...])

        @pl.loop(0, groups, unroll=True)
        def _(group):
            for plane in range(planes):
                here = pl.ds(pl.multiple_of((plane * groups + group) * rows, rows), rows)
                for i in range(8):
                    o = group * 8 + i
                    total = (
                        spectral[here, i * 128 : (i + 1) * 128]
                        + pointwise[
                            block,
                            pl.ds(pl.multiple_of(o * rows, rows), rows),
                            plane * 128 : (plane + 1) * 128,
                        ]
                    )
                    grad[o, plane, line] = total.astype(BF16)

    for end in (ends[1], ends[2], ends[3], ends[5], ends[6], ends[7]):
        end[1]()


def to_lines(devices, back, y_out, unorder, blocks):
    lines_u = [fdot(y_out[...], back[u].reshape(16 * devices, 256)).astype(BF16) for u in range(2)]
    lines = lines_u[0].shape[0] // 8
    for plane in range(2):
        for part in range(2):
            pieces = []
            for half in range(2):
                first = ((plane * 2 + part) * 2 + half) * lines
                pieces += [lines_u[u][first : first + lines] for u in range(2)]
            rows = fdot(jnp.concatenate(pieces, 1), unorder[...]).astype(BF16)
            groups = rows.shape[1] // 128
            for block in range(lines // 16):
                for group in range(groups):
                    blocks[
                        block,
                        (plane * groups + group) * 16 : (plane * groups + group + 1) * 16,
                        part * 128 : (part + 1) * 128,
                    ] = rows[block * 16 : (block + 1) * 16, group * 128 : (group + 1) * 128]


def pair_tile(straight, other, low, direct):
    return jnp.where(
        direct,
        jnp.where(low, straight, other),
        pltpu.roll(jnp.where(low, other, straight), 64, 1),
    )


def weight_grad_block(weight_scale, left, pairs, out):
    block = lax.broadcasted_iota(jnp.int32, (128, 256), 0) // 8
    side = lax.broadcasted_iota(jnp.int32, (128, 256), 1) // 128

    @pl.loop(0, 2)
    def _(k_half):
        here = pl.ds(pl.multiple_of(k_half * 128, 128), 128)
        right = pairs[here].astype(F32) * weight_scale
        right = jnp.concatenate([right, right], 1)
        for i in range(MX // 4):
            kept = jnp.where(block == 2 * i + side, right, 0.0).astype(BF16)
            total = fdot(left[k_half], kept).astype(BF16)
            for s in range(2):
                for k2 in range(2):
                    for parity in range(2):
                        first = (k2 * 2 + parity) * 64
                        out[k2, parity, k_half * (MX // 2) + 2 * i + s] = total[
                            first : first + 64, s * 128 : (s + 1) * 128
                        ]


def weight_grad_kernel(
    weight_scale, act_in, grad_in, part_in, lefts, pairs, act_out, grad_out, out_hbm, buffer, sem,
    field_sem,
):
    def place(index):
        return out_hbm.at[:, 2 * index : 2 * index + 2]

    copies = [
        pltpu.make_async_copy(
            part_in.at[:, 2 * index : 2 * index + 2], place(index), sem.at[index]
        )
        for index in (0, 1, 4, 5)
    ]
    copies += [
        pltpu.make_async_copy(act_in, act_out, field_sem.at[0]),
        pltpu.make_async_copy(grad_in, grad_out, field_sem.at[1]),
    ]
    for copy in copies:
        copy.start()
    for slot, index in enumerate((2, 3, 6, 7)):
        weight_grad_block(weight_scale, lefts.at[index], pairs.at[index], buffer.at[slot])
        copy = pltpu.make_async_copy(buffer.at[slot], place(index), sem.at[index])
        copy.start()
        copies.append(copy)
    for copy in copies:
        copy.wait()


def vmem(*shape, dtype=BF16):
    return pltpu.VMEM(shape, dtype)


WHOLE = pl.BlockSpec(memory_space=pltpu.VMEM)
ANYWHERE = pl.BlockSpec(memory_space=pl.ANY)


def block_body(features, cotangent, spectral_weight, channel_weight, channel_bias):
    channels, planes, lines, depth_len = features.shape
    devices = lax.axis_size("gx")
    all_planes = planes * devices
    number = MX * MY * MZ
    forward_scale = 1.0 / math.sqrt(all_planes * lines * depth_len)
    inverse_scale = 1.0 / math.sqrt(number)
    weight_scale = math.sqrt(number / (all_planes * lines * depth_len))
    tables = host_tables(devices, lines, depth_len, channels)
    tables = [tables[name] for name in TABLES]
    weights = spectral_weight.reshape(2, MZ, MX, channels, 2 * channels)
    wide = MZ * channels
    rows = 16
    steps = lines // rows
    dma = pltpu.SemaphoreType.DMA
    like = jax.ShapeDtypeStruct(features.shape, BF16)
    lefts = (8, 2, 256, 128)
    pairs = (8, 8 * MX, 128)
    activated, feature_grad, weight_part, left, pair = pl.pallas_call(
        functools.partial(layer_kernel, devices, forward_scale, inverse_scale, weight_scale),
        out_shape=[
            vmem(*features.shape), vmem(*features.shape), vmem(*weights.shape), vmem(*lefts),
            vmem(*pairs),
        ],
        in_specs=[ANYWHERE] * 3
        + [WHOLE, pl.BlockSpec(memory_space=pltpu.SMEM)]
        + [ANYWHERE] * len(tables),
        out_specs=[WHOLE] * 5,
        scratch_shapes=[vmem(*table.shape) for table in tables]
        + [
            vmem(*features.shape),
            vmem(*features.shape),
            vmem(channels * rows, channels * rows),
            vmem(channels * rows, channels * rows),
            vmem(steps, channels * rows, planes * depth_len, dtype=F32),
            vmem(4 * lines, wide),
            vmem(steps, 2 * wide // 8, 256),
            vmem(planes * channels * 2, 8 * depth_len, dtype=F32),
            vmem(steps, planes * channels * 2, 8 * depth_len),
            vmem(4, 2, devices, 16, 256),
            vmem(4, 2, devices, 16, 256),
            vmem(2, 2, MX, 8, 256, dtype=F32),
            vmem(2, MX, 8, 256, dtype=F32),
            vmem(2, MX, 8, 256, dtype=F32),
            vmem(2, 8 * MX, 256),
            dma((4,)),
            dma((len(tables) + 1,)),
            dma((2, 4)),
            dma((8, devices)),
            dma((8, devices)),
        ],
        compiler_params=pltpu.CompilerParams(
            collective_id=0, has_side_effects=True, vmem_limit_bytes=40 * MB
        ),
        name="layer",
    )(features, cotangent, weights, channel_weight, channel_bias, *tables)
    activated, feature_grad, spectral_grad = pl.pallas_call(
        functools.partial(weight_grad_kernel, weight_scale),
        out_shape=[like, like, jax.ShapeDtypeStruct(weights.shape, BF16)],
        in_specs=[WHOLE] * 5,
        out_specs=[ANYWHERE] * 3,
        scratch_shapes=[
            vmem(4, 2, 2, MX, channels, 2 * channels),
            dma((8,)),
            dma((2,)),
        ],
        compiler_params=pltpu.CompilerParams(vmem_limit_bytes=14 * MB),
        name="weight_grad",
    )(activated, feature_grad, weight_part, left, pair)
    return (activated, feature_grad, spectral_grad.reshape(spectral_weight.shape))


def body(features, cotangent, spectral_weight, channel_weight, channel_bias):
    channels, planes, lines, depth_len = features.shape
    devices = lax.axis_size("gx")
    fits = (
        2 * devices == MY
        and planes == 2
        and channels == 64
        and lines == 64
        and depth_len == 128
        and spectral_weight.shape[0] == 2 * MZ * MX
    )
    chosen = block_body if fits else plain_body
    return chosen(features, cotangent, spectral_weight, channel_weight, channel_bias)


def solution(mesh):
    in_specs = (
        P("grp", "gx", None, None),
        P("grp", "gx", None, None),
        P("gx", None, None),
        P(),
        P(),
    )
    out_specs = (
        P("grp", "gx", None, None),
        P("grp", "gx", None, None),
        P(("grp", "gx"), None, None),
    )
    return jax.shard_map(body, mesh=mesh, in_specs=in_specs, out_specs=out_specs, check_vma=False)
```

```python
import functools
import math

import jax
import jax.numpy as jnp
import numpy as np
from jax import lax
from jax.experimental import pallas as pl
from jax.experimental.pallas import tpu as pltpu
from jax.sharding import PartitionSpec as P

MX = 32
MY = 32
MZ = 16


SQRT_TWO_PI = math.sqrt(2.0 / math.pi)
CUBIC_COEF = 0.044715


def freq_index(retained, length):
    ladder = jnp.arange(retained, dtype=jnp.int32)
    return jnp.where(ladder < retained // 2, ladder, length - retained + ladder)


def cos_sin(wavenum, length):
    points = jnp.arange(length, dtype=jnp.int32)
    angles = (wavenum[:, None] * points[None, :] % length).astype(jnp.float32) * (
        2.0 * math.pi / length
    )
    return (jnp.cos(angles), jnp.sin(angles))


def analysis_pair(wavenum, length):
    cosine, sine_wave = cos_sin(wavenum, length)
    cosine, sine_wave = (cosine.T, sine_wave.T)
    return jnp.stack(
        [jnp.stack([cosine, -sine_wave], 1), jnp.stack([sine_wave, cosine], 1)], 1
    ).astype(jnp.bfloat16)


def synthesis_pair(wavenum, length):
    cosine, sine_wave = cos_sin(wavenum, length)
    return jnp.stack(
        [jnp.stack([cosine, sine_wave], 1), jnp.stack([-sine_wave, cosine], 1)], 1
    ).astype(jnp.bfloat16)


def depth_table(retained, length):
    cosine, sine_wave = cos_sin(jnp.arange(retained, dtype=jnp.int32), length)
    return jnp.concatenate([cosine, -sine_wave], 0).astype(jnp.bfloat16)


def gelu_parts(inputs):
    squared = inputs * inputs
    slope = SQRT_TWO_PI * CUBIC_COEF
    tangent = jnp.tanh(inputs * (SQRT_TWO_PI + slope * squared))
    half = 0.5 + 0.5 * tangent
    output = inputs * half
    derivative = half + output * (1.0 - tangent) * (SQRT_TWO_PI + 3.0 * slope * squared)
    return (output, derivative)


def mode_product(coeffs, weights):
    channels = weights.shape[1]
    halves = jnp.einsum("mac,mcj->amj", coeffs, weights, preferred_element_type=jnp.float32)
    real_out = halves[0, :, :channels] - halves[1, :, channels:]
    imag_out = halves[0, :, channels:] + halves[1, :, :channels]
    return jnp.stack([real_out, imag_out], 1).astype(jnp.bfloat16)


def exchange(blocks):
    return lax.all_to_all(blocks, "gx", 0, 0, tiled=True)


def middle_kernel(
    scale, feat_ref, cot_ref, lines_ref, weight_ref, bias_ref, basis_ref, act_ref, up_ref, grad_ref
):
    channels, _, rows, depth_len = feat_ref.shape
    spectral = jnp.dot(
        lines_ref[0].reshape(rows * channels, lines_ref.shape[3]),
        basis_ref[...],
        preferred_element_type=jnp.float32,
    ).reshape(rows, channels, depth_len)
    feats = jnp.swapaxes(feat_ref[:, 0].astype(jnp.float32), 0, 1).astype(jnp.bfloat16)
    cots = jnp.swapaxes(cot_ref[:, 0].astype(jnp.float32), 0, 1)
    acts = []
    for row in range(rows):
        pointwise = jnp.dot(weight_ref[...], feats[row], preferred_element_type=jnp.float32)
        hidden = spectral[row] * scale + pointwise + bias_ref[...]
        activated, derivative = gelu_parts(hidden)
        acts.append(activated)
        up_ref[0, row] = (cots[row] * derivative).astype(jnp.bfloat16)
    act_ref[:, 0] = jnp.swapaxes(jnp.stack(acts, 0), 0, 1).astype(jnp.bfloat16)
    grad = lax.dot_general(
        up_ref[0].reshape(rows * channels, depth_len),
        basis_ref[...],
        (((1,), (1,)), ((), ())),
        preferred_element_type=jnp.float32,
    )
    grad_ref[0] = (grad * scale).astype(jnp.bfloat16).reshape(rows, channels, lines_ref.shape[3])


def final_kernel(up_ref, depth_ref, weight_ref, basis_ref, out_ref):
    _, rows, channels, depth_len = up_ref.shape
    spectral = jnp.dot(
        depth_ref[0].reshape(rows * channels, depth_ref.shape[3]),
        basis_ref[...],
        preferred_element_type=jnp.float32,
    ).reshape(rows, channels, depth_len)
    totals = []
    for row in range(rows):
        back = jnp.dot(weight_ref[...], up_ref[0, row], preferred_element_type=jnp.float32)
        totals.append(spectral[row] + back)
    out_ref[:, 0] = jnp.swapaxes(jnp.stack(totals, 0), 0, 1).astype(jnp.bfloat16)


ROWS = 16


def middle(features, cotangent, lines_back, channel_weight, channel_bias, depth_basis, scale):
    channels, planes, lines, depth_len = features.shape
    parts = lines_back.shape[3]
    field = pl.BlockSpec((channels, 1, ROWS, depth_len), lambda x, y: (0, x, y, 0))
    turned = pl.BlockSpec((1, ROWS, channels, depth_len), lambda x, y: (x, y, 0, 0))
    narrow = pl.BlockSpec((1, ROWS, channels, parts), lambda x, y: (x, y, 0, 0))
    count = features.size
    return pl.pallas_call(
        functools.partial(middle_kernel, scale),
        grid=(planes, lines // ROWS),
        in_specs=[
            field,
            field,
            narrow,
            pl.BlockSpec((channels, channels), lambda x, y: (0, 0)),
            pl.BlockSpec((channels, 1), lambda x, y: (0, 0)),
            pl.BlockSpec((parts, depth_len), lambda x, y: (0, 0)),
        ],
        out_specs=[field, turned, narrow],
        out_shape=[
            jax.ShapeDtypeStruct(features.shape, jnp.bfloat16),
            jax.ShapeDtypeStruct((planes, lines, channels, depth_len), jnp.bfloat16),
            jax.ShapeDtypeStruct((planes, lines, channels, parts), jnp.bfloat16),
        ],
        compiler_params=pltpu.CompilerParams(vmem_limit_bytes=56 * 1024 * 1024),
        cost_estimate=pl.CostEstimate(
            flops=count * 2 * (channels + 2 * parts), bytes_accessed=count * 8, transcendentals=count
        ),
    )(features, cotangent, lines_back, channel_weight, channel_bias[:, None], depth_basis)


def final(upstream, depth_grad, weight_back, depth_basis):
    planes, lines, channels, depth_len = upstream.shape
    parts = depth_grad.shape[3]
    count = upstream.size
    return pl.pallas_call(
        final_kernel,
        grid=(planes, lines // ROWS),
        in_specs=[
            pl.BlockSpec((1, ROWS, channels, depth_len), lambda x, y: (x, y, 0, 0)),
            pl.BlockSpec((1, ROWS, channels, parts), lambda x, y: (x, y, 0, 0)),
            pl.BlockSpec((channels, channels), lambda x, y: (0, 0)),
            pl.BlockSpec((parts, depth_len), lambda x, y: (0, 0)),
        ],
        out_specs=pl.BlockSpec((channels, 1, ROWS, depth_len), lambda x, y: (0, x, y, 0)),
        out_shape=jax.ShapeDtypeStruct((channels, planes, lines, depth_len), jnp.bfloat16),
        compiler_params=pltpu.CompilerParams(vmem_limit_bytes=32 * 1024 * 1024),
        cost_estimate=pl.CostEstimate(
            flops=count * 2 * (channels + parts), bytes_accessed=count * 4, transcendentals=0
        ),
    )(upstream, depth_grad, weight_back, depth_basis)


def plain_body(features, cotangent, spectral_weight, channel_weight, channel_bias):
    channels, planes, lines, depth_len = features.shape
    devices = lax.axis_size("gx")
    all_planes = planes * devices
    owned_modes = spectral_weight.shape[0]
    wave_pairs = MY * MZ
    owned_pairs = owned_modes // MX
    wide = 2 * channels
    forward_scale = 1.0 / math.sqrt(all_planes * lines * depth_len)
    inverse_scale = 1.0 / math.sqrt(MX * wave_pairs)
    weight_scale = math.sqrt(MX * wave_pairs / (all_planes * lines * depth_len))
    depth_basis = depth_table(MZ, depth_len)
    across_y = analysis_pair(freq_index(MY, lines), lines)
    back_y = synthesis_pair(freq_index(MY, lines), lines)
    across_x = analysis_pair(freq_index(MX, all_planes), all_planes)
    back_x = synthesis_pair(freq_index(MX, all_planes), all_planes)

    def to_owners(rows):
        blocks = rows.reshape(devices, owned_pairs * planes, wide)
        return exchange(blocks).reshape(devices, owned_pairs, planes, 2, channels)

    def to_planes(rows):
        blocks = rows.reshape(devices, planes * owned_pairs, wide)
        got = exchange(blocks).reshape(devices, planes, owned_pairs, 2, channels)
        return got.transpose(1, 0, 2, 3, 4).reshape(planes, MY, MZ, 2, channels)

    depth_part = jnp.dot(features, depth_basis.T, preferred_element_type=jnp.float32).astype(
        jnp.bfloat16
    )
    plane_part = jnp.einsum(
        "cxyaz,yabk->kzxbc",
        depth_part.reshape(channels, planes, lines, 2, MZ),
        across_y,
        preferred_element_type=jnp.float32,
    ).astype(jnp.bfloat16)
    gathered = to_owners(plane_part)
    mode_sums = jnp.einsum(
        "sqpac,spabk->qkbc",
        gathered,
        across_x.reshape(devices, planes, 2, 2, MX),
        preferred_element_type=jnp.float32,
    )
    coeffs = (mode_sums * forward_scale).astype(jnp.bfloat16).reshape(owned_modes, 2, channels)
    spectral = mode_product(coeffs, spectral_weight)
    planes_back = jnp.einsum(
        "qkao,kabx->xqbo",
        spectral.reshape(owned_pairs, MX, 2, channels),
        back_x,
        preferred_element_type=jnp.float32,
    ).astype(jnp.bfloat16)
    planes_here = to_planes(planes_back)
    lines_back = (
        jnp.einsum("xkzao,kaby->xyobz", planes_here, back_y, preferred_element_type=jnp.float32)
        .astype(jnp.bfloat16)
        .reshape(planes, lines, channels, 2 * MZ)
    )
    activated, upstream, lines_grad = middle(
        features, cotangent, lines_back, channel_weight, channel_bias, depth_basis, inverse_scale
    )
    rows_grad = jnp.einsum(
        "xyobz,kaby->kzxao",
        lines_grad.reshape(planes, lines, channels, 2, MZ),
        back_y,
        preferred_element_type=jnp.float32,
    ).astype(jnp.bfloat16)
    gathered_grad = to_owners(rows_grad)
    grad_modes = (
        jnp.einsum(
            "sqpbo,kabsp->qkao",
            gathered_grad,
            back_x.reshape(MX, 2, 2, devices, planes),
            preferred_element_type=jnp.float32,
        )
        .astype(jnp.bfloat16)
        .reshape(owned_modes, 2, channels)
    )
    straight = grad_modes.reshape(owned_modes, wide)
    rotated = jnp.concatenate([grad_modes[:, 1], -grad_modes[:, 0]], 1)
    pairs = jnp.stack([straight, rotated], 1)
    coeff_grad = (
        jnp.einsum("mcj,mbj->mbc", spectral_weight, pairs, preferred_element_type=jnp.float32)
        * forward_scale
    ).astype(jnp.bfloat16)
    plane_grad = jnp.einsum(
        "qkbc,xabk->xqac",
        coeff_grad.reshape(owned_pairs, MX, 2, channels),
        across_x,
        preferred_element_type=jnp.float32,
    ).astype(jnp.bfloat16)
    grad_here = to_planes(plane_grad)
    spectral_grad = (
        jnp.einsum("mac,maj->mcj", coeffs, pairs, preferred_element_type=jnp.float32)
        * weight_scale
    ).astype(jnp.bfloat16)
    depth_grad = (
        jnp.einsum("xkzbc,yabk->xycaz", grad_here, across_y, preferred_element_type=jnp.float32)
        .astype(jnp.bfloat16)
        .reshape(planes, lines, channels, 2 * MZ)
    )
    feature_grad = final(upstream, depth_grad, channel_weight.T, depth_basis)
    return (activated, feature_grad, spectral_grad)


MESH = pl.DeviceIdType.MESH
F32 = jnp.float32
BF16 = jnp.bfloat16
MB = 1024 * 1024


def host_cos_sin(wavenum, length):
    angles = (np.outer(wavenum, np.arange(length)) % length).astype(np.float32) * np.float32(
        2.0 * math.pi / length
    )
    return np.cos(angles), np.sin(angles)


def host_freq(retained, length):
    ladder = np.arange(retained)
    return np.where(ladder < retained // 2, ladder, length - retained + ladder)


def host_minus(retained, length):
    cosine, sine = host_cos_sin(host_freq(retained, length), length)
    cosine, sine = cosine.T, sine.T
    return np.stack([np.stack([cosine, -sine], 1), np.stack([sine, cosine], 1)], 1)


def host_plus(retained, length):
    cosine, sine = host_cos_sin(host_freq(retained, length), length)
    return np.stack([np.stack([cosine, sine], 1), np.stack([-sine, cosine], 1)], 1)


def host_tables(devices, lines, depth_len, channels):
    all_planes = 2 * devices
    two = np.eye(2)
    eight = np.eye(8)
    cosine, sine = host_cos_sin(np.arange(MZ), depth_len)
    depth = np.stack([cosine, -sine], 0)
    z_in = np.einsum("akz,cd->czakd", depth, eight).reshape(8 * depth_len, 16 * MZ)
    minus_y = host_minus(MY, lines).reshape(lines, 2, 2, devices, 2)
    y_in = np.einsum("yabdk,xw->dkbwxay", minus_y, two).reshape(8 * devices, 4 * lines)
    groups = channels // 8
    source = np.arange(MZ * channels).reshape(groups, MZ, 8)
    target = source.transpose(1, 0, 2).reshape(-1)
    order = np.zeros((MZ * channels, MZ * channels))
    order[target, np.arange(MZ * channels)] = 1.0
    minus_x = host_minus(MX, all_planes).reshape(devices, 2, 2, 2, MX)
    x_in = np.einsum("sxabk,hg,jl,p->hkjpbsglax", minus_x, two, two, np.ones(2)).reshape(
        16 * MX, 16 * devices
    )
    swapped = np.stack([minus_x[:, :, :, 1], -minus_x[:, :, :, 0]], 3)
    x_turn = np.einsum("sxabk,hg,jl,p->hkjpbsglax", swapped, two, two, np.ones(2)).reshape(
        16 * MX, 16 * devices
    )
    plus_x = host_plus(MX, all_planes).reshape(MX, 2, 2, devices, 2)
    crossed = np.stack([-plus_x[:, :, 1], plus_x[:, :, 0]], 2)
    both = np.stack([plus_x, crossed], 0)
    x_out = np.einsum("rkabsx,pq,jl->prsjbxklqa", both, two, two).reshape(32 * devices, 8 * MX)
    x_back = np.einsum("kabsx,jl,q->sjbxklqa", plus_x, two, np.ones(2)).reshape(
        8 * devices, 8 * MX
    )
    plus_y = host_plus(MY, lines).reshape(devices, 2, 2, 2, lines)
    y_out = np.einsum("skaby,hg,xw->xbhysgkaw", plus_y, two, two).reshape(8 * lines, 16 * devices)
    tables = dict(
        z_in=z_in, z_out=z_in.T, y_in=y_in, order=order, unorder=order.T, x_in=x_in,
        x_turn=x_turn, x_out=x_out, x_back=x_back, y_out=y_out,
    )
    return {name: jnp.asarray(np.ascontiguousarray(t), BF16) for name, t in tables.items()}


def fdot(left, right):
    return jnp.dot(left, right, preferred_element_type=F32)


def greet(devices):
    me, group = lax.axis_index("gx"), lax.axis_index("grp")
    barrier = pltpu.get_barrier_semaphore()

    @pl.loop(1, devices)
    def _(step):
        pl.semaphore_signal(
            barrier, inc=1, device_id=(group, lax.rem(me + step, devices)), device_id_type=MESH
        )

    def arrived():
        pl.semaphore_wait(barrier, devices - 1)

    return arrived


def swap_start(devices, sent, got, send_sem, recv_sem, stage):
    me, group = lax.axis_index("gx"), lax.axis_index("grp")

    def copy(step):
        target = lax.rem(me + step, devices)
        return pltpu.make_async_remote_copy(
            src_ref=sent.at[target],
            dst_ref=got.at[me],
            send_sem=send_sem.at[stage, step],
            recv_sem=recv_sem.at[stage, step],
            device_id=(group, target),
            device_id_type=MESH,
        )

    @pl.loop(1, devices)
    def _(step):
        copy(step).start()

    got[me] = sent[me]

    def finish():
        @pl.loop(1, devices)
        def _(step):
            copy(step).wait_recv()

    def drained():
        @pl.loop(1, devices)
        def _(step):
            copy(step).wait_send()

    return finish, drained


def to_chunks(devices, lines_ref, y_in, order, sent):
    rows = fdot(y_in[...], lines_ref[...]).astype(BF16)
    rows = fdot(rows, order[...])
    lanes = rows.shape[1]
    halves = [
        rows[:, h * lanes // 2 : (h + 1) * lanes // 2].reshape(devices, 8, lanes // 2)
        for h in range(2)
    ]
    chunk = jnp.concatenate(halves, 1).astype(BF16)
    for u in range(2):
        sent[u] = chunk[:, :, u * lanes // 4 : (u + 1) * lanes // 4]


def mode_block(weights, k_pair, half, pair):
    def one(kx):
        return jnp.concatenate(
            [weights[k2, half * 8 + pair * 2 + parity, kx] for k2 in range(2) for parity in range(2)],
            0,
        )

    return jnp.concatenate([one(2 * k_pair), one(2 * k_pair + 1)], 1)


def iotas():
    row = lax.broadcasted_iota(jnp.int32, (8, 128), 0)
    lane = lax.broadcasted_iota(jnp.int32, (8, 128), 1)
    return row, lane


def weight_copies(weights_hbm, weights, sem):
    def copy(half, pair):
        kz = pl.ds(half * 8 + pair * 2, 2)
        return pltpu.make_async_copy(
            weights_hbm.at[:, kz], weights.at[:, kz], sem.at[half, pair]
        )

    return copy


def fill_kron(channel_weight, out, contract):
    size = out.shape[0]
    channels = channel_weight.shape[0]

    def spread(rows, first, axis):
        shape = (rows, channels) if axis == 0 else (channels, rows)
        long = lax.broadcasted_iota(jnp.int32, shape, axis)
        short = lax.broadcasted_iota(jnp.int32, shape, 1 - axis)
        return jnp.where(long // 16 + first == short, 1.0, 0.0).astype(BF16)

    columns = spread(size, 0, 1)
    line = lax.broadcasted_iota(jnp.int32, (128, size), 0) % 16
    same = line == lax.broadcasted_iota(jnp.int32, (128, size), 1) % 16

    @pl.loop(0, size // 128)
    def _(block):
        rows = lax.dot_general(
            spread(128, block * 8, 0),
            channel_weight[...],
            (((1,), (1 - contract,)), ((), ())),
            preferred_element_type=F32,
        ).astype(BF16)
        out[pl.ds(pl.multiple_of(block * 128, 128), 128), :] = jnp.where(
            same, fdot(rows, columns), 0.0
        ).astype(BF16)


TABLES = (
    "z_in", "y_in", "order", "x_in", "x_out", "y_out", "unorder", "z_out", "x_turn", "x_back",
)
EARLY = 3
LATE = 5
PARTS = 2


def layer_kernel(
    devices, forward_scale, inverse_scale, weight_scale,
    feat_hbm, cot_hbm, weights_hbm, channel_weight, bias, *refs,
):
    number = len(TABLES)
    tables_hbm = dict(zip(TABLES, refs[:number]))
    act, grad, weights, lefts, pairs = refs[number : number + 5]
    tables = dict(zip(TABLES, refs[number + 5 : 2 * number + 5]))
    (
        feat, cot, kron, kron_back, pointwise, lines_part, blocks, spectral,
        up_wide, sent, got, coeffs, modes, turned, mixed,
        feat_sem, load_sem, weight_sem, send_sem, recv_sem,
    ) = refs[2 * number + 5 :]
    channels, planes, lines, depth_len = feat.shape
    groups = channels // 8
    rows = 16
    arrived = greet(devices)
    pieces = feat_sem.shape[0]
    share = channels // pieces

    def load_feat(piece):
        here = pl.ds(piece * share, share)
        return pltpu.make_async_copy(feat_hbm.at[here], feat.at[here], feat_sem.at[piece])

    loads = {
        name: pltpu.make_async_copy(tables_hbm[name], tables[name], load_sem.at[i])
        for i, name in enumerate(TABLES)
    }
    load_cot = pltpu.make_async_copy(cot_hbm, cot, load_sem.at[number])
    loads["z_in"].start()
    for piece in range(pieces):
        load_feat(piece).start()
    for name in TABLES[1:EARLY]:
        loads[name].start()
    weight_copy = weight_copies(weights_hbm, weights, weight_sem)
    loads["z_in"].wait()

    @pl.loop(0, pieces)
    def _(piece):
        load_feat(piece).wait()
        spots = [(local, plane) for local in range(share // 8) for plane in range(planes)]
        wide = [
            jnp.concatenate([feat[piece * share + local * 8 + i, plane] for i in range(8)], 1)
            for local, plane in spots
        ]
        part = fdot(jnp.concatenate(wide, 0), tables["z_in"][...]).astype(BF16)
        for spot, (local, plane) in enumerate(spots):
            group = piece * (share // 8) + local
            for a in range(2):
                lines_part[
                    pl.ds((plane * 2 + a) * lines, lines),
                    pl.ds(pl.multiple_of(group * 128, 128), 128),
                ] = part[spot * lines : (spot + 1) * lines, a * 128 : (a + 1) * 128]

    loads["x_in"].start()
    for pair in range(2):
        for half in range(2):
            weight_copy(half, pair).start()
    for name in TABLES[EARLY + 1 :]:
        loads[name].start()
    for pair in range(2, 4):
        for half in range(2):
            weight_copy(half, pair).start()
    load_cot.start()
    for name in TABLES[1:EARLY]:
        loads[name].wait()
    to_chunks(devices, lines_part, tables["y_in"], tables["order"], sent.at[0])
    arrived()

    def swap(stage, u):
        return swap_start(
            devices, sent.at[stage, u], got.at[stage, u], send_sem, recv_sem, 2 * stage + u
        )

    def lines_of(stage, arrivals):
        for u in range(2):
            arrivals[u][0]()
            to_lines(u, got.at[stage], tables["y_out"], tables["unorder"], spectral.at[0])
        to_blocks(spectral.at[0], blocks)

    ends = [swap(0, 0)]

    def point(block):
        here = pl.ds(pl.multiple_of(block * rows, rows), rows)
        both = jnp.concatenate(
            [feat[:, x, here].reshape(channels * rows, depth_len) for x in range(planes)], 1
        )
        total = fdot(kron[...], both)
        for o in range(channels):
            here = slice(o * rows, (o + 1) * rows)
            pointwise[block, here] = total[here] + bias[o]

    fill_kron(channel_weight, kron, 1)

    @pl.loop(0, 1)
    def _(block):
        point(block)

    ends[0][1]()
    ends.append(swap(0, 1))

    @pl.loop(1, 2)
    def _(block):
        point(block)

    for name in TABLES[EARLY:LATE]:
        loads[name].wait()
    row, lane = iotas()
    own = [(row // 2) == (lane // 64 + 2 * k2) for k2 in range(2)]
    low_tall = lax.broadcasted_iota(jnp.int32, (8 * devices, 128), 1) < 64
    low = lane < 64
    direct = low == ((row // 2) % 2 == 0)
    first_line = row < 4
    zero = jnp.zeros((8, 128), F32)

    for u in range(2):
        ends[u][0]()
        source = got[0, u].reshape(16 * devices, 256)
        coeffs[u] = (fdot(tables["x_in"][...], source) * forward_scale).reshape(2, MX, 8, 256)

        @pl.loop(0, 4, unroll=PARTS)
        def _(part):
            half, local = part // 2, part % 2
            weight_copy(half, 2 * u + local).wait()
            span = pl.ds(pl.multiple_of(local * 128, 128), 128)

            def step(k_pair, carry):
                left = []
                for i in range(2):
                    block = coeffs[u, half, 2 * k_pair + i, :, span]
                    left.append(
                        jnp.concatenate([jnp.where(own[k2], block, 0.0) for k2 in range(2)], 1)
                    )
                left = jnp.concatenate(left, 0).astype(BF16)
                out = fdot(left, mode_block(weights, k_pair, half, 2 * u + local))
                out = jnp.concatenate([out[:8, :128], out[8:, 128:]], 0).astype(BF16)
                mixed[half, pl.ds(pl.multiple_of(k_pair * 16, 16), 16), span] = out
                return carry

            lax.fori_loop(0, MX // 2, step, 0, unroll=16)

        halves = []
        for half in range(2):
            every = fdot(tables["x_out"][...], mixed[half]) * inverse_scale
            size = 8 * devices
            tiles = []
            for local in range(2):
                even, even_x, odd, odd_x = [
                    every[i * size : (i + 1) * size, local * 128 : (local + 1) * 128]
                    for i in range(4)
                ]
                tiles.append(
                    jnp.where(low_tall, even, odd_x)
                    + pltpu.roll(jnp.where(low_tall, odd, even_x), 64, 1)
                )
            halves.append(jnp.concatenate(tiles, 1).reshape(devices, 8, 256))
        sent[1, u] = jnp.concatenate(halves, 1).astype(BF16)
        ends.append(swap(1, u))

    @pl.loop(2, lines // rows)
    def _(block):
        point(block)

    fill_kron(channel_weight, kron_back, 0)

    @pl.loop(0, 2)
    def _(k_half):
        here = pl.ds(k_half * (MX // 2), MX // 2)
        for index in range(8):
            half, u, local = index // 4, (index % 4) // 2, index % 2
            values = coeffs[u, half, here, :, local * 128 : (local + 1) * 128]
            wide = jnp.concatenate(
                [jnp.where(own[k2][None], values, 0.0).reshape(128, 128) for k2 in range(2)], 1
            )
            lefts[index, k_half] = wide.T.astype(BF16)

    load_cot.wait()
    for name in TABLES[LATE:]:
        loads[name].wait()
    lines_of(1, ends[2:4])

    @pl.loop(0, lines // rows, unroll=True)
    def _(block):
        line = pl.ds(pl.multiple_of(block * rows, rows), rows)
        slot = block % 2
        spectral[slot] = fdot(blocks[block], tables["z_out"][...])

        @pl.loop(0, groups, unroll=True)
        def _(group):
            for plane in range(planes):
                here = pl.ds(pl.multiple_of((plane * groups + group) * rows, rows), rows)
                for i in range(8):
                    o = group * 8 + i
                    hidden = (
                        spectral[slot, here, i * 128 : (i + 1) * 128]
                        + pointwise[
                            block,
                            pl.ds(pl.multiple_of(o * rows, rows), rows),
                            plane * 128 : (plane + 1) * 128,
                        ]
                    )
                    activated, derivative = gelu_parts(hidden)
                    act[o, plane, line] = activated.astype(BF16)
                    up_wide[block, here, i * 128 : (i + 1) * 128] = (
                        cot[o, plane, line].astype(F32) * derivative
                    ).astype(BF16)

        part = (fdot(up_wide[block], tables["z_in"][...]) * inverse_scale).astype(BF16)
        for plane in range(planes):
            for a in range(2):
                for group in range(groups):
                    first = (plane * groups + group) * rows
                    lines_part[
                        pl.ds(
                            pl.multiple_of((plane * 2 + a) * lines + block * rows, rows), rows
                        ),
                        group * 128 : (group + 1) * 128,
                    ] = part[first : first + rows, a * 128 : (a + 1) * 128]

    to_chunks(devices, lines_part, tables["y_in"], tables["order"], sent.at[2])
    ends.append(swap(2, 0))

    def point_back(block):
        both = []
        for plane in range(planes):
            tiles = []
            for o in range(channels):
                first = (plane * groups + o // 8) * rows
                tiles.append(
                    up_wide[block, first : first + rows, (o % 8) * 128 : (o % 8 + 1) * 128]
                )
            both.append(jnp.concatenate(tiles, 0))
        pointwise[block] = fdot(kron_back[...], jnp.concatenate(both, 1))

    pl.loop(0, 3)(point_back)
    ends[4][1]()
    ends.append(swap(2, 1))
    pl.loop(3, 4)(point_back)

    for u in range(2):
        ends[4 + u][0]()
        source = got[2, u].reshape(16 * devices, 256)
        modes[...] = fdot(tables["x_in"][...], source).reshape(2, MX, 8, 256)
        turned[...] = fdot(tables["x_turn"][...], source).reshape(2, MX, 8, 256)

        @pl.loop(0, 4, unroll=PARTS)
        def _(part):
            half, local = part // 2, part % 2
            span = pl.ds(pl.multiple_of(local * 128, 128), 128)

            def step(k_pair, carry):
                here = pl.ds(pl.multiple_of(k_pair * 16, 16), 16)
                tiles = [
                    pair_tile(
                        modes[half, 2 * k_pair + i, :, span],
                        turned[half, 2 * k_pair + i, :, span],
                        low,
                        direct,
                    )
                    for i in range(2)
                ]
                pairs[half * 4 + 2 * u + local, here] = jnp.concatenate(tiles, 0).astype(BF16)
                left = jnp.concatenate(
                    [jnp.concatenate([tiles[0], zero], 1), jnp.concatenate([zero, tiles[1]], 1)], 0
                ).astype(BF16)
                out = lax.dot_general(
                    left,
                    mode_block(weights, k_pair, half, 2 * u + local),
                    (((1,), (1,)), ((), ())),
                    preferred_element_type=F32,
                )
                kept = []
                for i in range(2):
                    here_rows = out[8 * i : 8 * i + 8]
                    kept.append(
                        jnp.where(
                            direct,
                            jnp.where(first_line, here_rows[:, :128], here_rows[:, 128:]),
                            0.0,
                        )
                    )
                mixed[half, here, span] = (jnp.concatenate(kept, 0) * forward_scale).astype(BF16)
                return carry

            lax.fori_loop(0, MX // 2, step, 0, unroll=16)

        sent[3, u] = jnp.concatenate(
            [fdot(tables["x_back"][...], mixed[half]).reshape(devices, 8, 256) for half in range(2)],
            1,
        ).astype(BF16)
        ends.append(swap(3, u))

    for index in (0, 1, 4, 5):
        weight_grad_block(
            weight_scale, lefts.at[index], pairs.at[index], weights.at[:, 2 * index : 2 * index + 2]
        )
    lines_of(3, ends[6:8])

    @pl.loop(0, lines // rows, unroll=True)
    def _(block):
        line = pl.ds(pl.multiple_of(block * rows, rows), rows)
        slot = block % 2
        spectral[slot] = fdot(blocks[block], tables["z_out"][...])

        @pl.loop(0, groups, unroll=True)
        def _(group):
            for plane in range(planes):
                here = pl.ds(pl.multiple_of((plane * groups + group) * rows, rows), rows)
                for i in range(8):
                    o = group * 8 + i
                    total = (
                        spectral[slot, here, i * 128 : (i + 1) * 128]
                        + pointwise[
                            block,
                            pl.ds(pl.multiple_of(o * rows, rows), rows),
                            plane * 128 : (plane + 1) * 128,
                        ]
                    )
                    grad[o, plane, line] = total.astype(BF16)

    for end in (ends[1], ends[2], ends[3], ends[5], ends[6], ends[7]):
        end[1]()


def to_lines(u, back, y_out, unorder, total):
    values = fdot(y_out[...], back[u].reshape(-1, 256)).astype(BF16)
    lines = values.shape[0] // 8
    part = 0.0
    for half in range(2):
        rows = jnp.concatenate(
            [values[(2 * i + half) * lines : (2 * i + half + 1) * lines] for i in range(4)], 0
        )
        first = (2 * half + u) * 256
        part = part + fdot(rows, unorder[first : first + 256, :])
    total[...] = part if u == 0 else total[...] + part


def to_blocks(total, blocks):
    size, wide = total.shape
    lines, groups = size // 4, wide // 128
    for plane in range(2):
        for part in range(2):
            for block in range(lines // 16):
                first = (plane * 2 + part) * lines + block * 16
                for group in range(groups):
                    blocks[
                        block,
                        (plane * groups + group) * 16 : (plane * groups + group + 1) * 16,
                        part * 128 : (part + 1) * 128,
                    ] = total[first : first + 16, group * 128 : (group + 1) * 128].astype(BF16)


def pair_tile(straight, other, low, direct):
    return jnp.where(
        direct,
        jnp.where(low, straight, other),
        pltpu.roll(jnp.where(low, other, straight), 64, 1),
    )


def weight_grad_block(weight_scale, left, pairs, out):
    block = lax.broadcasted_iota(jnp.int32, (128, 256), 0) // 8
    side = lax.broadcasted_iota(jnp.int32, (128, 256), 1) // 128

    @pl.loop(0, 2)
    def _(k_half):
        here = pl.ds(pl.multiple_of(k_half * 128, 128), 128)
        right = pairs[here].astype(F32) * weight_scale
        right = jnp.concatenate([right, right], 1)
        for i in range(MX // 4):
            kept = jnp.where(block == 2 * i + side, right, 0.0).astype(BF16)
            total = fdot(left[k_half], kept).astype(BF16)
            for s in range(2):
                for k2 in range(2):
                    for parity in range(2):
                        first = (k2 * 2 + parity) * 64
                        out[k2, parity, k_half * (MX // 2) + 2 * i + s] = total[
                            first : first + 64, s * 128 : (s + 1) * 128
                        ]


def weight_grad_kernel(
    weight_scale, act_in, grad_in, part_in, lefts, pairs, act_out, grad_out, out_hbm, buffer, sem,
    field_sem,
):
    def place(index):
        return out_hbm.at[:, 2 * index : 2 * index + 2]

    copies = [
        pltpu.make_async_copy(
            part_in.at[:, 2 * index : 2 * index + 2], place(index), sem.at[index]
        )
        for index in (0, 1, 4, 5)
    ]
    copies += [
        pltpu.make_async_copy(act_in, act_out, field_sem.at[0]),
        pltpu.make_async_copy(grad_in, grad_out, field_sem.at[1]),
    ]
    for copy in copies:
        copy.start()
    for slot, index in enumerate((2, 3, 6, 7)):
        weight_grad_block(weight_scale, lefts.at[index], pairs.at[index], buffer.at[slot])
        copy = pltpu.make_async_copy(buffer.at[slot], place(index), sem.at[index])
        copy.start()
        copies.append(copy)
    for copy in copies:
        copy.wait()


def vmem(*shape, dtype=BF16):
    return pltpu.VMEM(shape, dtype)


WHOLE = pl.BlockSpec(memory_space=pltpu.VMEM)
ANYWHERE = pl.BlockSpec(memory_space=pl.ANY)


def block_body(features, cotangent, spectral_weight, channel_weight, channel_bias):
    channels, planes, lines, depth_len = features.shape
    devices = lax.axis_size("gx")
    all_planes = planes * devices
    number = MX * MY * MZ
    forward_scale = 1.0 / math.sqrt(all_planes * lines * depth_len)
    inverse_scale = 1.0 / math.sqrt(number)
    weight_scale = math.sqrt(number / (all_planes * lines * depth_len))
    tables = host_tables(devices, lines, depth_len, channels)
    tables = [tables[name] for name in TABLES]
    weights = spectral_weight.reshape(2, MZ, MX, channels, 2 * channels)
    wide = MZ * channels
    rows = 16
    steps = lines // rows
    dma = pltpu.SemaphoreType.DMA
    like = jax.ShapeDtypeStruct(features.shape, BF16)
    lefts = (8, 2, 256, 128)
    pairs = (8, 8 * MX, 128)
    activated, feature_grad, weight_part, left, pair = pl.pallas_call(
        functools.partial(layer_kernel, devices, forward_scale, inverse_scale, weight_scale),
        out_shape=[
            vmem(*features.shape), vmem(*features.shape), vmem(*weights.shape), vmem(*lefts),
            vmem(*pairs),
        ],
        in_specs=[ANYWHERE] * 3
        + [WHOLE, pl.BlockSpec(memory_space=pltpu.SMEM)]
        + [ANYWHERE] * len(tables),
        out_specs=[WHOLE] * 5,
        scratch_shapes=[vmem(*table.shape) for table in tables]
        + [
            vmem(*features.shape),
            vmem(*features.shape),
            vmem(channels * rows, channels * rows),
            vmem(channels * rows, channels * rows),
            vmem(steps, channels * rows, planes * depth_len, dtype=F32),
            vmem(4 * lines, wide),
            vmem(steps, 2 * wide // 8, 256),
            vmem(2, planes * channels * 2, 8 * depth_len, dtype=F32),
            vmem(steps, planes * channels * 2, 8 * depth_len),
            vmem(4, 2, devices, 16, 256),
            vmem(4, 2, devices, 16, 256),
            vmem(2, 2, MX, 8, 256, dtype=F32),
            vmem(2, MX, 8, 256, dtype=F32),
            vmem(2, MX, 8, 256, dtype=F32),
            vmem(2, 8 * MX, 256),
            dma((4,)),
            dma((len(tables) + 1,)),
            dma((2, 4)),
            dma((8, devices)),
            dma((8, devices)),
        ],
        compiler_params=pltpu.CompilerParams(
            collective_id=0, has_side_effects=True, vmem_limit_bytes=40 * MB
        ),
        name="layer",
    )(features, cotangent, weights, channel_weight, channel_bias, *tables)
    activated, feature_grad, spectral_grad = pl.pallas_call(
        functools.partial(weight_grad_kernel, weight_scale),
        out_shape=[like, like, jax.ShapeDtypeStruct(weights.shape, BF16)],
        in_specs=[WHOLE] * 5,
        out_specs=[ANYWHERE] * 3,
        scratch_shapes=[
            vmem(4, 2, 2, MX, channels, 2 * channels),
            dma((8,)),
            dma((2,)),
        ],
        compiler_params=pltpu.CompilerParams(vmem_limit_bytes=14 * MB),
        name="weight_grad",
    )(activated, feature_grad, weight_part, left, pair)
    return (activated, feature_grad, spectral_grad.reshape(spectral_weight.shape))


def body(features, cotangent, spectral_weight, channel_weight, channel_bias):
    channels, planes, lines, depth_len = features.shape
    devices = lax.axis_size("gx")
    fits = (
        2 * devices == MY
        and planes == 2
        and channels == 64
        and lines == 64
        and depth_len == 128
        and spectral_weight.shape[0] == 2 * MZ * MX
    )
    chosen = block_body if fits else plain_body
    return chosen(features, cotangent, spectral_weight, channel_weight, channel_bias)


def solution(mesh):
    in_specs = (
        P("grp", "gx", None, None),
        P("grp", "gx", None, None),
        P("gx", None, None),
        P(),
        P(),
    )
    out_specs = (
        P("grp", "gx", None, None),
        P("grp", "gx", None, None),
        P(("grp", "gx"), None, None),
    )
    return jax.shard_map(body, mesh=mesh, in_specs=in_specs, out_specs=out_specs, check_vma=False)
```

```python
import functools
import math

import jax
import jax.numpy as jnp
import numpy as np
from jax import lax
from jax.experimental import pallas as pl
from jax.experimental.pallas import tpu as pltpu
from jax.sharding import PartitionSpec as P

MX = 32
MY = 32
MZ = 16


SQRT_TWO_PI = math.sqrt(2.0 / math.pi)
CUBIC_COEF = 0.044715


def freq_index(retained, length):
    ladder = jnp.arange(retained, dtype=jnp.int32)
    return jnp.where(ladder < retained // 2, ladder, length - retained + ladder)


def cos_sin(wavenum, length):
    points = jnp.arange(length, dtype=jnp.int32)
    angles = (wavenum[:, None] * points[None, :] % length).astype(jnp.float32) * (
        2.0 * math.pi / length
    )
    return (jnp.cos(angles), jnp.sin(angles))


def analysis_pair(wavenum, length):
    cosine, sine_wave = cos_sin(wavenum, length)
    cosine, sine_wave = (cosine.T, sine_wave.T)
    return jnp.stack(
        [jnp.stack([cosine, -sine_wave], 1), jnp.stack([sine_wave, cosine], 1)], 1
    ).astype(jnp.bfloat16)


def synthesis_pair(wavenum, length):
    cosine, sine_wave = cos_sin(wavenum, length)
    return jnp.stack(
        [jnp.stack([cosine, sine_wave], 1), jnp.stack([-sine_wave, cosine], 1)], 1
    ).astype(jnp.bfloat16)


def depth_table(retained, length):
    cosine, sine_wave = cos_sin(jnp.arange(retained, dtype=jnp.int32), length)
    return jnp.concatenate([cosine, -sine_wave], 0).astype(jnp.bfloat16)


def gelu_parts(inputs):
    squared = inputs * inputs
    slope = SQRT_TWO_PI * CUBIC_COEF
    tangent = jnp.tanh(inputs * (SQRT_TWO_PI + slope * squared))
    half = 0.5 + 0.5 * tangent
    output = inputs * half
    derivative = half + output * (1.0 - tangent) * (SQRT_TWO_PI + 3.0 * slope * squared)
    return (output, derivative)


def mode_product(coeffs, weights):
    channels = weights.shape[1]
    halves = jnp.einsum("mac,mcj->amj", coeffs, weights, preferred_element_type=jnp.float32)
    real_out = halves[0, :, :channels] - halves[1, :, channels:]
    imag_out = halves[0, :, channels:] + halves[1, :, :channels]
    return jnp.stack([real_out, imag_out], 1).astype(jnp.bfloat16)


def exchange(blocks):
    return lax.all_to_all(blocks, "gx", 0, 0, tiled=True)


def middle_kernel(
    scale, feat_ref, cot_ref, lines_ref, weight_ref, bias_ref, basis_ref, act_ref, up_ref, grad_ref
):
    channels, _, rows, depth_len = feat_ref.shape
    spectral = jnp.dot(
        lines_ref[0].reshape(rows * channels, lines_ref.shape[3]),
        basis_ref[...],
        preferred_element_type=jnp.float32,
    ).reshape(rows, channels, depth_len)
    feats = jnp.swapaxes(feat_ref[:, 0].astype(jnp.float32), 0, 1).astype(jnp.bfloat16)
    cots = jnp.swapaxes(cot_ref[:, 0].astype(jnp.float32), 0, 1)
    acts = []
    for row in range(rows):
        pointwise = jnp.dot(weight_ref[...], feats[row], preferred_element_type=jnp.float32)
        hidden = spectral[row] * scale + pointwise + bias_ref[...]
        activated, derivative = gelu_parts(hidden)
        acts.append(activated)
        up_ref[0, row] = (cots[row] * derivative).astype(jnp.bfloat16)
    act_ref[:, 0] = jnp.swapaxes(jnp.stack(acts, 0), 0, 1).astype(jnp.bfloat16)
    grad = lax.dot_general(
        up_ref[0].reshape(rows * channels, depth_len),
        basis_ref[...],
        (((1,), (1,)), ((), ())),
        preferred_element_type=jnp.float32,
    )
    grad_ref[0] = (grad * scale).astype(jnp.bfloat16).reshape(rows, channels, lines_ref.shape[3])


def final_kernel(up_ref, depth_ref, weight_ref, basis_ref, out_ref):
    _, rows, channels, depth_len = up_ref.shape
    spectral = jnp.dot(
        depth_ref[0].reshape(rows * channels, depth_ref.shape[3]),
        basis_ref[...],
        preferred_element_type=jnp.float32,
    ).reshape(rows, channels, depth_len)
    totals = []
    for row in range(rows):
        back = jnp.dot(weight_ref[...], up_ref[0, row], preferred_element_type=jnp.float32)
        totals.append(spectral[row] + back)
    out_ref[:, 0] = jnp.swapaxes(jnp.stack(totals, 0), 0, 1).astype(jnp.bfloat16)


ROWS = 16


def middle(features, cotangent, lines_back, channel_weight, channel_bias, depth_basis, scale):
    channels, planes, lines, depth_len = features.shape
    parts = lines_back.shape[3]
    field = pl.BlockSpec((channels, 1, ROWS, depth_len), lambda x, y: (0, x, y, 0))
    turned = pl.BlockSpec((1, ROWS, channels, depth_len), lambda x, y: (x, y, 0, 0))
    narrow = pl.BlockSpec((1, ROWS, channels, parts), lambda x, y: (x, y, 0, 0))
    count = features.size
    return pl.pallas_call(
        functools.partial(middle_kernel, scale),
        grid=(planes, lines // ROWS),
        in_specs=[
            field,
            field,
            narrow,
            pl.BlockSpec((channels, channels), lambda x, y: (0, 0)),
            pl.BlockSpec((channels, 1), lambda x, y: (0, 0)),
            pl.BlockSpec((parts, depth_len), lambda x, y: (0, 0)),
        ],
        out_specs=[field, turned, narrow],
        out_shape=[
            jax.ShapeDtypeStruct(features.shape, jnp.bfloat16),
            jax.ShapeDtypeStruct((planes, lines, channels, depth_len), jnp.bfloat16),
            jax.ShapeDtypeStruct((planes, lines, channels, parts), jnp.bfloat16),
        ],
        compiler_params=pltpu.CompilerParams(vmem_limit_bytes=56 * 1024 * 1024),
        cost_estimate=pl.CostEstimate(
            flops=count * 2 * (channels + 2 * parts), bytes_accessed=count * 8, transcendentals=count
        ),
    )(features, cotangent, lines_back, channel_weight, channel_bias[:, None], depth_basis)


def final(upstream, depth_grad, weight_back, depth_basis):
    planes, lines, channels, depth_len = upstream.shape
    parts = depth_grad.shape[3]
    count = upstream.size
    return pl.pallas_call(
        final_kernel,
        grid=(planes, lines // ROWS),
        in_specs=[
            pl.BlockSpec((1, ROWS, channels, depth_len), lambda x, y: (x, y, 0, 0)),
            pl.BlockSpec((1, ROWS, channels, parts), lambda x, y: (x, y, 0, 0)),
            pl.BlockSpec((channels, channels), lambda x, y: (0, 0)),
            pl.BlockSpec((parts, depth_len), lambda x, y: (0, 0)),
        ],
        out_specs=pl.BlockSpec((channels, 1, ROWS, depth_len), lambda x, y: (0, x, y, 0)),
        out_shape=jax.ShapeDtypeStruct((channels, planes, lines, depth_len), jnp.bfloat16),
        compiler_params=pltpu.CompilerParams(vmem_limit_bytes=32 * 1024 * 1024),
        cost_estimate=pl.CostEstimate(
            flops=count * 2 * (channels + parts), bytes_accessed=count * 4, transcendentals=0
        ),
    )(upstream, depth_grad, weight_back, depth_basis)


def plain_body(features, cotangent, spectral_weight, channel_weight, channel_bias):
    channels, planes, lines, depth_len = features.shape
    devices = lax.axis_size("gx")
    all_planes = planes * devices
    owned_modes = spectral_weight.shape[0]
    wave_pairs = MY * MZ
    owned_pairs = owned_modes // MX
    wide = 2 * channels
    forward_scale = 1.0 / math.sqrt(all_planes * lines * depth_len)
    inverse_scale = 1.0 / math.sqrt(MX * wave_pairs)
    weight_scale = math.sqrt(MX * wave_pairs / (all_planes * lines * depth_len))
    depth_basis = depth_table(MZ, depth_len)
    across_y = analysis_pair(freq_index(MY, lines), lines)
    back_y = synthesis_pair(freq_index(MY, lines), lines)
    across_x = analysis_pair(freq_index(MX, all_planes), all_planes)
    back_x = synthesis_pair(freq_index(MX, all_planes), all_planes)

    def to_owners(rows):
        blocks = rows.reshape(devices, owned_pairs * planes, wide)
        return exchange(blocks).reshape(devices, owned_pairs, planes, 2, channels)

    def to_planes(rows):
        blocks = rows.reshape(devices, planes * owned_pairs, wide)
        got = exchange(blocks).reshape(devices, planes, owned_pairs, 2, channels)
        return got.transpose(1, 0, 2, 3, 4).reshape(planes, MY, MZ, 2, channels)

    depth_part = jnp.dot(features, depth_basis.T, preferred_element_type=jnp.float32).astype(
        jnp.bfloat16
    )
    plane_part = jnp.einsum(
        "cxyaz,yabk->kzxbc",
        depth_part.reshape(channels, planes, lines, 2, MZ),
        across_y,
        preferred_element_type=jnp.float32,
    ).astype(jnp.bfloat16)
    gathered = to_owners(plane_part)
    mode_sums = jnp.einsum(
        "sqpac,spabk->qkbc",
        gathered,
        across_x.reshape(devices, planes, 2, 2, MX),
        preferred_element_type=jnp.float32,
    )
    coeffs = (mode_sums * forward_scale).astype(jnp.bfloat16).reshape(owned_modes, 2, channels)
    spectral = mode_product(coeffs, spectral_weight)
    planes_back = jnp.einsum(
        "qkao,kabx->xqbo",
        spectral.reshape(owned_pairs, MX, 2, channels),
        back_x,
        preferred_element_type=jnp.float32,
    ).astype(jnp.bfloat16)
    planes_here = to_planes(planes_back)
    lines_back = (
        jnp.einsum("xkzao,kaby->xyobz", planes_here, back_y, preferred_element_type=jnp.float32)
        .astype(jnp.bfloat16)
        .reshape(planes, lines, channels, 2 * MZ)
    )
    activated, upstream, lines_grad = middle(
        features, cotangent, lines_back, channel_weight, channel_bias, depth_basis, inverse_scale
    )
    rows_grad = jnp.einsum(
        "xyobz,kaby->kzxao",
        lines_grad.reshape(planes, lines, channels, 2, MZ),
        back_y,
        preferred_element_type=jnp.float32,
    ).astype(jnp.bfloat16)
    gathered_grad = to_owners(rows_grad)
    grad_modes = (
        jnp.einsum(
            "sqpbo,kabsp->qkao",
            gathered_grad,
            back_x.reshape(MX, 2, 2, devices, planes),
            preferred_element_type=jnp.float32,
        )
        .astype(jnp.bfloat16)
        .reshape(owned_modes, 2, channels)
    )
    straight = grad_modes.reshape(owned_modes, wide)
    rotated = jnp.concatenate([grad_modes[:, 1], -grad_modes[:, 0]], 1)
    pairs = jnp.stack([straight, rotated], 1)
    coeff_grad = (
        jnp.einsum("mcj,mbj->mbc", spectral_weight, pairs, preferred_element_type=jnp.float32)
        * forward_scale
    ).astype(jnp.bfloat16)
    plane_grad = jnp.einsum(
        "qkbc,xabk->xqac",
        coeff_grad.reshape(owned_pairs, MX, 2, channels),
        across_x,
        preferred_element_type=jnp.float32,
    ).astype(jnp.bfloat16)
    grad_here = to_planes(plane_grad)
    spectral_grad = (
        jnp.einsum("mac,maj->mcj", coeffs, pairs, preferred_element_type=jnp.float32)
        * weight_scale
    ).astype(jnp.bfloat16)
    depth_grad = (
        jnp.einsum("xkzbc,yabk->xycaz", grad_here, across_y, preferred_element_type=jnp.float32)
        .astype(jnp.bfloat16)
        .reshape(planes, lines, channels, 2 * MZ)
    )
    feature_grad = final(upstream, depth_grad, channel_weight.T, depth_basis)
    return (activated, feature_grad, spectral_grad)


MESH = pl.DeviceIdType.MESH
F32 = jnp.float32
BF16 = jnp.bfloat16
MB = 1024 * 1024


def host_cos_sin(wavenum, length):
    angles = (np.outer(wavenum, np.arange(length)) % length).astype(np.float32) * np.float32(
        2.0 * math.pi / length
    )
    return np.cos(angles), np.sin(angles)


def host_freq(retained, length):
    ladder = np.arange(retained)
    return np.where(ladder < retained // 2, ladder, length - retained + ladder)


def host_minus(retained, length):
    cosine, sine = host_cos_sin(host_freq(retained, length), length)
    cosine, sine = cosine.T, sine.T
    return np.stack([np.stack([cosine, -sine], 1), np.stack([sine, cosine], 1)], 1)


def host_plus(retained, length):
    cosine, sine = host_cos_sin(host_freq(retained, length), length)
    return np.stack([np.stack([cosine, sine], 1), np.stack([-sine, cosine], 1)], 1)


def host_tables(devices, lines, depth_len, channels):
    all_planes = 2 * devices
    two = np.eye(2)
    eight = np.eye(8)
    cosine, sine = host_cos_sin(np.arange(MZ), depth_len)
    depth = np.stack([cosine, -sine], 0)
    z_in = np.einsum("akz,cd->czakd", depth, eight).reshape(8 * depth_len, 16 * MZ)
    minus_y = host_minus(MY, lines).reshape(lines, 2, 2, devices, 2)
    y_in = np.einsum("yabdk,xw->dkbwxay", minus_y, two).reshape(8 * devices, 4 * lines)
    groups = channels // 8
    source = np.arange(MZ * channels).reshape(groups, MZ, 8)
    target = source.transpose(1, 0, 2).reshape(-1)
    order = np.zeros((MZ * channels, MZ * channels))
    order[target, np.arange(MZ * channels)] = 1.0
    minus_x = host_minus(MX, all_planes).reshape(devices, 2, 2, 2, MX)
    x_in = np.einsum("sxabk,hg,jl,p->hkjpbsglax", minus_x, two, two, np.ones(2)).reshape(
        16 * MX, 16 * devices
    )
    swapped = np.stack([minus_x[:, :, :, 1], -minus_x[:, :, :, 0]], 3)
    x_turn = np.einsum("sxabk,hg,jl,p->hkjpbsglax", swapped, two, two, np.ones(2)).reshape(
        16 * MX, 16 * devices
    )
    plus_x = host_plus(MX, all_planes).reshape(MX, 2, 2, devices, 2)
    crossed = np.stack([-plus_x[:, :, 1], plus_x[:, :, 0]], 2)
    both = np.stack([plus_x, crossed], 0)
    x_out = np.einsum("rkabsx,pq,jl->prsjbxklqa", both, two, two).reshape(32 * devices, 8 * MX)
    x_back = np.einsum("kabsx,jl,q->sjbxklqa", plus_x, two, np.ones(2)).reshape(
        8 * devices, 8 * MX
    )
    plus_y = host_plus(MY, lines).reshape(devices, 2, 2, 2, lines)
    y_out = np.einsum("skaby,hg,xw->xbhysgkaw", plus_y, two, two).reshape(8 * lines, 16 * devices)
    tables = dict(
        z_in=z_in, z_out=z_in.T, y_in=y_in, order=order, unorder=order.T, x_in=x_in,
        x_turn=x_turn, x_out=x_out, x_back=x_back, y_out=y_out,
    )
    return {name: jnp.asarray(np.ascontiguousarray(t), BF16) for name, t in tables.items()}


def fdot(left, right):
    return jnp.dot(left, right, preferred_element_type=F32)


def greet(devices):
    me, group = lax.axis_index("gx"), lax.axis_index("grp")
    barrier = pltpu.get_barrier_semaphore()

    @pl.loop(1, devices)
    def _(step):
        pl.semaphore_signal(
            barrier, inc=1, device_id=(group, lax.rem(me + step, devices)), device_id_type=MESH
        )

    def arrived():
        pl.semaphore_wait(barrier, devices - 1)

    return arrived


def swap_start(devices, sent, got, send_sem, recv_sem, stage):
    me, group = lax.axis_index("gx"), lax.axis_index("grp")

    def copy(source, landing, target):
        return pltpu.make_async_remote_copy(
            src_ref=source,
            dst_ref=landing,
            send_sem=send_sem.at[stage],
            recv_sem=recv_sem.at[stage],
            device_id=(group, target),
            device_id_type=MESH,
        )

    @pl.loop(1, devices, unroll=True)
    def _(step):
        target = lax.rem(me + step, devices)
        copy(sent.at[target], got.at[me], target).start()

    got[me] = sent[me]
    others = pl.ds(0, devices - 1)
    every = copy(sent.at[others], got.at[others], lax.rem(me + 1, devices))

    def finish():
        every.wait_recv()

    def drained():
        every.wait_send()

    return finish, drained


def to_chunks(devices, lines_ref, y_in, order, sent):
    rows = fdot(y_in[...], lines_ref[...]).astype(BF16)
    rows = fdot(rows, order[...])
    lanes = rows.shape[1]
    halves = [
        rows[:, h * lanes // 2 : (h + 1) * lanes // 2].reshape(devices, 8, lanes // 2)
        for h in range(2)
    ]
    chunk = jnp.concatenate(halves, 1).astype(BF16)
    for u in range(2):
        sent[u] = chunk[:, :, u * lanes // 4 : (u + 1) * lanes // 4]


def mode_block(weights, k_pair, half, pair):
    def one(kx):
        return jnp.concatenate(
            [weights[k2, half * 8 + pair * 2 + parity, kx] for k2 in range(2) for parity in range(2)],
            0,
        )

    return jnp.concatenate([one(2 * k_pair), one(2 * k_pair + 1)], 1)


def iotas():
    row = lax.broadcasted_iota(jnp.int32, (8, 128), 0)
    lane = lax.broadcasted_iota(jnp.int32, (8, 128), 1)
    return row, lane


def weight_copies(weights_hbm, weights, sem):
    def copy(half, pair):
        kz = pl.ds(half * 8 + pair * 2, 2)
        return pltpu.make_async_copy(
            weights_hbm.at[:, kz], weights.at[:, kz], sem.at[half, pair]
        )

    return copy


def fill_kron(channel_weight, out, contract):
    size = out.shape[0]
    channels = channel_weight.shape[0]

    def spread(rows, first, axis):
        shape = (rows, channels) if axis == 0 else (channels, rows)
        long = lax.broadcasted_iota(jnp.int32, shape, axis)
        short = lax.broadcasted_iota(jnp.int32, shape, 1 - axis)
        return jnp.where(long // 16 + first == short, 1.0, 0.0).astype(BF16)

    columns = spread(size, 0, 1)
    line = lax.broadcasted_iota(jnp.int32, (128, size), 0) % 16
    same = line == lax.broadcasted_iota(jnp.int32, (128, size), 1) % 16

    @pl.loop(0, size // 128)
    def _(block):
        rows = lax.dot_general(
            spread(128, block * 8, 0),
            channel_weight[...],
            (((1,), (1 - contract,)), ((), ())),
            preferred_element_type=F32,
        ).astype(BF16)
        out[pl.ds(pl.multiple_of(block * 128, 128), 128), :] = jnp.where(
            same, fdot(rows, columns), 0.0
        ).astype(BF16)


TABLES = (
    "z_in", "y_in", "order", "x_in", "x_out", "y_out", "unorder", "z_out", "x_turn", "x_back",
)
EARLY = 3
LATE = 5
PARTS = 2


def layer_kernel(
    devices, forward_scale, inverse_scale, weight_scale,
    feat_hbm, cot_hbm, weights_hbm, channel_weight, bias, *refs,
):
    number = len(TABLES)
    tables_hbm = dict(zip(TABLES, refs[:number]))
    act, grad, weights, lefts, pairs = refs[number : number + 5]
    tables = dict(zip(TABLES, refs[number + 5 : 2 * number + 5]))
    (
        feat, cot, kron, kron_back, pointwise, lines_part, blocks, spectral,
        up_wide, sent, got, coeffs, modes, turned, mixed,
        feat_sem, load_sem, weight_sem, send_sem, recv_sem,
    ) = refs[2 * number + 5 :]
    channels, planes, lines, depth_len = feat.shape
    groups = channels // 8
    rows = 16
    arrived = greet(devices)
    pieces = feat_sem.shape[0]
    share = channels // pieces

    def load_feat(piece):
        here = pl.ds(piece * share, share)
        return pltpu.make_async_copy(feat_hbm.at[here], feat.at[here], feat_sem.at[piece])

    loads = {
        name: pltpu.make_async_copy(tables_hbm[name], tables[name], load_sem.at[i])
        for i, name in enumerate(TABLES)
    }
    load_cot = pltpu.make_async_copy(cot_hbm, cot, load_sem.at[number])
    loads["z_in"].start()
    for piece in range(pieces):
        load_feat(piece).start()
    for name in TABLES[1:EARLY]:
        loads[name].start()
    weight_copy = weight_copies(weights_hbm, weights, weight_sem)
    loads["z_in"].wait()

    @pl.loop(0, pieces)
    def _(piece):
        load_feat(piece).wait()
        spots = [(local, plane) for local in range(share // 8) for plane in range(planes)]
        wide = [
            jnp.concatenate([feat[piece * share + local * 8 + i, plane] for i in range(8)], 1)
            for local, plane in spots
        ]
        part = fdot(jnp.concatenate(wide, 0), tables["z_in"][...]).astype(BF16)
        for spot, (local, plane) in enumerate(spots):
            group = piece * (share // 8) + local
            for a in range(2):
                lines_part[
                    pl.ds((plane * 2 + a) * lines, lines),
                    pl.ds(pl.multiple_of(group * 128, 128), 128),
                ] = part[spot * lines : (spot + 1) * lines, a * 128 : (a + 1) * 128]

    loads["x_in"].start()
    for pair in range(2):
        for half in range(2):
            weight_copy(half, pair).start()
    for name in TABLES[EARLY + 1 :]:
        loads[name].start()
    for pair in range(2, 4):
        for half in range(2):
            weight_copy(half, pair).start()
    load_cot.start()
    for name in TABLES[1:EARLY]:
        loads[name].wait()
    to_chunks(devices, lines_part, tables["y_in"], tables["order"], sent.at[0])
    arrived()

    def swap(stage, u):
        return swap_start(
            devices, sent.at[stage, u], got.at[stage, u], send_sem, recv_sem, 2 * stage + u
        )

    def lines_of(stage, arrivals):
        for u in range(2):
            arrivals[u][0]()
            to_lines(u, got.at[stage], tables["y_out"], tables["unorder"], spectral.at[0])
        to_blocks(spectral.at[0], blocks)

    ends = [swap(0, 0)]

    def point(block):
        here = pl.ds(pl.multiple_of(block * rows, rows), rows)
        both = jnp.concatenate(
            [feat[:, x, here].reshape(channels * rows, depth_len) for x in range(planes)], 1
        )
        total = fdot(kron[...], both)
        for o in range(channels):
            here = slice(o * rows, (o + 1) * rows)
            pointwise[block, here] = total[here] + bias[o]

    fill_kron(channel_weight, kron, 1)

    @pl.loop(0, 1)
    def _(block):
        point(block)

    ends[0][1]()
    ends.append(swap(0, 1))

    @pl.loop(1, 2)
    def _(block):
        point(block)

    for name in TABLES[EARLY:LATE]:
        loads[name].wait()
    row, lane = iotas()
    own = [(row // 2) == (lane // 64 + 2 * k2) for k2 in range(2)]
    low_tall = lax.broadcasted_iota(jnp.int32, (8 * devices, 128), 1) < 64
    low = lane < 64
    direct = low == ((row // 2) % 2 == 0)
    first_line = row < 4
    zero = jnp.zeros((8, 128), F32)

    for u in range(2):
        ends[u][0]()
        source = got[0, u].reshape(16 * devices, 256)
        coeffs[u] = (fdot(tables["x_in"][...], source) * forward_scale).reshape(2, MX, 8, 256)

        @pl.loop(0, 4, unroll=PARTS)
        def _(part):
            half, local = part // 2, part % 2
            weight_copy(half, 2 * u + local).wait()
            span = pl.ds(pl.multiple_of(local * 128, 128), 128)

            def step(k_pair, carry):
                left = []
                for i in range(2):
                    block = coeffs[u, half, 2 * k_pair + i, :, span]
                    left.append(
                        jnp.concatenate([jnp.where(own[k2], block, 0.0) for k2 in range(2)], 1)
                    )
                left = jnp.concatenate(left, 0).astype(BF16)
                out = fdot(left, mode_block(weights, k_pair, half, 2 * u + local))
                out = jnp.concatenate([out[:8, :128], out[8:, 128:]], 0).astype(BF16)
                mixed[half, pl.ds(pl.multiple_of(k_pair * 16, 16), 16), span] = out
                return carry

            lax.fori_loop(0, MX // 2, step, 0, unroll=16)

        halves = []
        for half in range(2):
            every = fdot(tables["x_out"][...], mixed[half]) * inverse_scale
            size = 8 * devices
            tiles = []
            for local in range(2):
                even, even_x, odd, odd_x = [
                    every[i * size : (i + 1) * size, local * 128 : (local + 1) * 128]
                    for i in range(4)
                ]
                tiles.append(
                    jnp.where(low_tall, even, odd_x)
                    + pltpu.roll(jnp.where(low_tall, odd, even_x), 64, 1)
                )
            halves.append(jnp.concatenate(tiles, 1).reshape(devices, 8, 256))
        sent[1, u] = jnp.concatenate(halves, 1).astype(BF16)
        ends.append(swap(1, u))

    @pl.loop(2, lines // rows)
    def _(block):
        point(block)

    fill_kron(channel_weight, kron_back, 0)

    @pl.loop(0, 2)
    def _(k_half):
        here = pl.ds(k_half * (MX // 2), MX // 2)
        for index in range(8):
            half, u, local = index // 4, (index % 4) // 2, index % 2
            values = coeffs[u, half, here, :, local * 128 : (local + 1) * 128]
            wide = jnp.concatenate(
                [jnp.where(own[k2][None], values, 0.0).reshape(128, 128) for k2 in range(2)], 1
            )
            lefts[index, k_half] = wide.T.astype(BF16)

    load_cot.wait()
    for name in TABLES[LATE:]:
        loads[name].wait()
    lines_of(1, ends[2:4])

    @pl.loop(0, lines // rows, unroll=True)
    def _(block):
        line = pl.ds(pl.multiple_of(block * rows, rows), rows)
        slot = block % 2
        spectral[slot] = fdot(blocks[block], tables["z_out"][...])

        @pl.loop(0, groups, unroll=True)
        def _(group):
            for plane in range(planes):
                here = pl.ds(pl.multiple_of((plane * groups + group) * rows, rows), rows)
                for i in range(8):
                    o = group * 8 + i
                    hidden = (
                        spectral[slot, here, i * 128 : (i + 1) * 128]
                        + pointwise[
                            block,
                            pl.ds(pl.multiple_of(o * rows, rows), rows),
                            plane * 128 : (plane + 1) * 128,
                        ]
                    )
                    activated, derivative = gelu_parts(hidden)
                    act[o, plane, line] = activated.astype(BF16)
                    up_wide[block, here, i * 128 : (i + 1) * 128] = (
                        cot[o, plane, line].astype(F32) * derivative
                    ).astype(BF16)

        part = (fdot(up_wide[block], tables["z_in"][...]) * inverse_scale).astype(BF16)
        for plane in range(planes):
            for a in range(2):
                for group in range(groups):
                    first = (plane * groups + group) * rows
                    lines_part[
                        pl.ds(
                            pl.multiple_of((plane * 2 + a) * lines + block * rows, rows), rows
                        ),
                        group * 128 : (group + 1) * 128,
                    ] = part[first : first + rows, a * 128 : (a + 1) * 128]

    to_chunks(devices, lines_part, tables["y_in"], tables["order"], sent.at[2])
    ends.append(swap(2, 0))

    def point_back(block):
        both = []
        for plane in range(planes):
            tiles = []
            for o in range(channels):
                first = (plane * groups + o // 8) * rows
                tiles.append(
                    up_wide[block, first : first + rows, (o % 8) * 128 : (o % 8 + 1) * 128]
                )
            both.append(jnp.concatenate(tiles, 0))
        pointwise[block] = fdot(kron_back[...], jnp.concatenate(both, 1))

    pl.loop(0, 3)(point_back)
    ends[4][1]()
    ends.append(swap(2, 1))
    pl.loop(3, 4)(point_back)

    for u in range(2):
        ends[4 + u][0]()
        source = got[2, u].reshape(16 * devices, 256)
        modes[...] = fdot(tables["x_in"][...], source).reshape(2, MX, 8, 256)
        turned[...] = fdot(tables["x_turn"][...], source).reshape(2, MX, 8, 256)

        @pl.loop(0, 4, unroll=PARTS)
        def _(part):
            half, local = part // 2, part % 2
            span = pl.ds(pl.multiple_of(local * 128, 128), 128)

            def step(k_pair, carry):
                here = pl.ds(pl.multiple_of(k_pair * 16, 16), 16)
                tiles = [
                    pair_tile(
                        modes[half, 2 * k_pair + i, :, span],
                        turned[half, 2 * k_pair + i, :, span],
                        low,
                        direct,
                    )
                    for i in range(2)
                ]
                pairs[half * 4 + 2 * u + local, here] = jnp.concatenate(tiles, 0).astype(BF16)
                left = jnp.concatenate(
                    [jnp.concatenate([tiles[0], zero], 1), jnp.concatenate([zero, tiles[1]], 1)], 0
                ).astype(BF16)
                out = lax.dot_general(
                    left,
                    mode_block(weights, k_pair, half, 2 * u + local),
                    (((1,), (1,)), ((), ())),
                    preferred_element_type=F32,
                )
                kept = []
                for i in range(2):
                    here_rows = out[8 * i : 8 * i + 8]
                    kept.append(
                        jnp.where(
                            direct,
                            jnp.where(first_line, here_rows[:, :128], here_rows[:, 128:]),
                            0.0,
                        )
                    )
                mixed[half, here, span] = (jnp.concatenate(kept, 0) * forward_scale).astype(BF16)
                return carry

            lax.fori_loop(0, MX // 2, step, 0, unroll=16)

        sent[3, u] = jnp.concatenate(
            [fdot(tables["x_back"][...], mixed[half]).reshape(devices, 8, 256) for half in range(2)],
            1,
        ).astype(BF16)
        ends.append(swap(3, u))

    for index in (0, 1, 4, 5):
        weight_grad_block(
            weight_scale, lefts.at[index], pairs.at[index], weights.at[:, 2 * index : 2 * index + 2]
        )
    lines_of(3, ends[6:8])

    @pl.loop(0, lines // rows, unroll=True)
    def _(block):
        line = pl.ds(pl.multiple_of(block * rows, rows), rows)
        slot = block % 2
        spectral[slot] = fdot(blocks[block], tables["z_out"][...])

        @pl.loop(0, groups, unroll=True)
        def _(group):
            for plane in range(planes):
                here = pl.ds(pl.multiple_of((plane * groups + group) * rows, rows), rows)
                for i in range(8):
                    o = group * 8 + i
                    total = (
                        spectral[slot, here, i * 128 : (i + 1) * 128]
                        + pointwise[
                            block,
                            pl.ds(pl.multiple_of(o * rows, rows), rows),
                            plane * 128 : (plane + 1) * 128,
                        ]
                    )
                    grad[o, plane, line] = total.astype(BF16)

    for end in (ends[1], ends[2], ends[3], ends[5], ends[6], ends[7]):
        end[1]()


def to_lines(u, back, y_out, unorder, total):
    values = fdot(y_out[...], back[u].reshape(-1, 256)).astype(BF16)
    lines = values.shape[0] // 8
    part = 0.0
    for half in range(2):
        rows = jnp.concatenate(
            [values[(2 * i + half) * lines : (2 * i + half + 1) * lines] for i in range(4)], 0
        )
        first = (2 * half + u) * 256
        part = part + fdot(rows, unorder[first : first + 256, :])
    total[...] = part if u == 0 else total[...] + part


def to_blocks(total, blocks):
    size, wide = total.shape
    lines, groups = size // 4, wide // 128
    for plane in range(2):
        for part in range(2):
            for block in range(lines // 16):
                first = (plane * 2 + part) * lines + block * 16
                for group in range(groups):
                    blocks[
                        block,
                        (plane * groups + group) * 16 : (plane * groups + group + 1) * 16,
                        part * 128 : (part + 1) * 128,
                    ] = total[first : first + 16, group * 128 : (group + 1) * 128].astype(BF16)


def pair_tile(straight, other, low, direct):
    return jnp.where(
        direct,
        jnp.where(low, straight, other),
        pltpu.roll(jnp.where(low, other, straight), 64, 1),
    )


def weight_grad_block(weight_scale, left, pairs, out):
    block = lax.broadcasted_iota(jnp.int32, (128, 256), 0) // 8
    side = lax.broadcasted_iota(jnp.int32, (128, 256), 1) // 128

    @pl.loop(0, 2)
    def _(k_half):
        here = pl.ds(pl.multiple_of(k_half * 128, 128), 128)
        right = pairs[here].astype(F32) * weight_scale
        right = jnp.concatenate([right, right], 1)
        for i in range(MX // 4):
            kept = jnp.where(block == 2 * i + side, right, 0.0).astype(BF16)
            total = fdot(left[k_half], kept).astype(BF16)
            for s in range(2):
                for k2 in range(2):
                    for parity in range(2):
                        first = (k2 * 2 + parity) * 64
                        out[k2, parity, k_half * (MX // 2) + 2 * i + s] = total[
                            first : first + 64, s * 128 : (s + 1) * 128
                        ]


def weight_grad_kernel(
    weight_scale, act_in, grad_in, part_in, lefts, pairs, act_out, grad_out, out_hbm, buffer, sem,
    field_sem,
):
    def place(index):
        return out_hbm.at[:, 2 * index : 2 * index + 2]

    copies = [
        pltpu.make_async_copy(
            part_in.at[:, 2 * index : 2 * index + 2], place(index), sem.at[index]
        )
        for index in (0, 1, 4, 5)
    ]
    copies += [
        pltpu.make_async_copy(act_in, act_out, field_sem.at[0]),
        pltpu.make_async_copy(grad_in, grad_out, field_sem.at[1]),
    ]
    for copy in copies:
        copy.start()
    for slot, index in enumerate((2, 3, 6, 7)):
        weight_grad_block(weight_scale, lefts.at[index], pairs.at[index], buffer.at[slot])
        copy = pltpu.make_async_copy(buffer.at[slot], place(index), sem.at[index])
        copy.start()
        copies.append(copy)
    for copy in copies:
        copy.wait()


def vmem(*shape, dtype=BF16):
    return pltpu.VMEM(shape, dtype)


WHOLE = pl.BlockSpec(memory_space=pltpu.VMEM)
ANYWHERE = pl.BlockSpec(memory_space=pl.ANY)


def block_body(features, cotangent, spectral_weight, channel_weight, channel_bias):
    channels, planes, lines, depth_len = features.shape
    devices = lax.axis_size("gx")
    all_planes = planes * devices
    number = MX * MY * MZ
    forward_scale = 1.0 / math.sqrt(all_planes * lines * depth_len)
    inverse_scale = 1.0 / math.sqrt(number)
    weight_scale = math.sqrt(number / (all_planes * lines * depth_len))
    tables = host_tables(devices, lines, depth_len, channels)
    tables = [tables[name] for name in TABLES]
    weights = spectral_weight.reshape(2, MZ, MX, channels, 2 * channels)
    wide = MZ * channels
    rows = 16
    steps = lines // rows
    dma = pltpu.SemaphoreType.DMA
    like = jax.ShapeDtypeStruct(features.shape, BF16)
    lefts = (8, 2, 256, 128)
    pairs = (8, 8 * MX, 128)
    activated, feature_grad, weight_part, left, pair = pl.pallas_call(
        functools.partial(layer_kernel, devices, forward_scale, inverse_scale, weight_scale),
        out_shape=[
            vmem(*features.shape), vmem(*features.shape), vmem(*weights.shape), vmem(*lefts),
            vmem(*pairs),
        ],
        in_specs=[ANYWHERE] * 3
        + [WHOLE, pl.BlockSpec(memory_space=pltpu.SMEM)]
        + [ANYWHERE] * len(tables),
        out_specs=[WHOLE] * 5,
        scratch_shapes=[vmem(*table.shape) for table in tables]
        + [
            vmem(*features.shape),
            vmem(*features.shape),
            vmem(channels * rows, channels * rows),
            vmem(channels * rows, channels * rows),
            vmem(steps, channels * rows, planes * depth_len, dtype=F32),
            vmem(4 * lines, wide),
            vmem(steps, 2 * wide // 8, 256),
            vmem(2, planes * channels * 2, 8 * depth_len, dtype=F32),
            vmem(steps, planes * channels * 2, 8 * depth_len),
            vmem(4, 2, devices, 16, 256),
            vmem(4, 2, devices, 16, 256),
            vmem(2, 2, MX, 8, 256, dtype=F32),
            vmem(2, MX, 8, 256, dtype=F32),
            vmem(2, MX, 8, 256, dtype=F32),
            vmem(2, 8 * MX, 256),
            dma((4,)),
            dma((len(tables) + 1,)),
            dma((2, 4)),
            dma((8,)),
            dma((8,)),
        ],
        compiler_params=pltpu.CompilerParams(
            collective_id=0, has_side_effects=True, vmem_limit_bytes=40 * MB
        ),
        name="layer",
    )(features, cotangent, weights, channel_weight, channel_bias, *tables)
    activated, feature_grad, spectral_grad = pl.pallas_call(
        functools.partial(weight_grad_kernel, weight_scale),
        out_shape=[like, like, jax.ShapeDtypeStruct(weights.shape, BF16)],
        in_specs=[WHOLE] * 5,
        out_specs=[ANYWHERE] * 3,
        scratch_shapes=[
            vmem(4, 2, 2, MX, channels, 2 * channels),
            dma((8,)),
            dma((2,)),
        ],
        compiler_params=pltpu.CompilerParams(vmem_limit_bytes=14 * MB),
        name="weight_grad",
    )(activated, feature_grad, weight_part, left, pair)
    return (activated, feature_grad, spectral_grad.reshape(spectral_weight.shape))


def body(features, cotangent, spectral_weight, channel_weight, channel_bias):
    channels, planes, lines, depth_len = features.shape
    devices = lax.axis_size("gx")
    fits = (
        2 * devices == MY
        and planes == 2
        and channels == 64
        and lines == 64
        and depth_len == 128
        and spectral_weight.shape[0] == 2 * MZ * MX
    )
    chosen = block_body if fits else plain_body
    return chosen(features, cotangent, spectral_weight, channel_weight, channel_bias)


def solution(mesh):
    in_specs = (
        P("grp", "gx", None, None),
        P("grp", "gx", None, None),
        P("gx", None, None),
        P(),
        P(),
    )
    out_specs = (
        P("grp", "gx", None, None),
        P("grp", "gx", None, None),
        P(("grp", "gx"), None, None),
    )
    return jax.shard_map(body, mesh=mesh, in_specs=in_specs, out_specs=out_specs, check_vma=False)
```

```python
import functools
import math

import jax
import jax.numpy as jnp
import numpy as np
from jax import lax
from jax.experimental import pallas as pl
from jax.experimental.pallas import tpu as pltpu
from jax.sharding import PartitionSpec as P

MX = 32
MY = 32
MZ = 16


SQRT_TWO_PI = math.sqrt(2.0 / math.pi)
CUBIC_COEF = 0.044715


def freq_index(retained, length):
    ladder = jnp.arange(retained, dtype=jnp.int32)
    return jnp.where(ladder < retained // 2, ladder, length - retained + ladder)


def cos_sin(wavenum, length):
    points = jnp.arange(length, dtype=jnp.int32)
    angles = (wavenum[:, None] * points[None, :] % length).astype(jnp.float32) * (
        2.0 * math.pi / length
    )
    return (jnp.cos(angles), jnp.sin(angles))


def analysis_pair(wavenum, length):
    cosine, sine_wave = cos_sin(wavenum, length)
    cosine, sine_wave = (cosine.T, sine_wave.T)
    return jnp.stack(
        [jnp.stack([cosine, -sine_wave], 1), jnp.stack([sine_wave, cosine], 1)], 1
    ).astype(jnp.bfloat16)


def synthesis_pair(wavenum, length):
    cosine, sine_wave = cos_sin(wavenum, length)
    return jnp.stack(
        [jnp.stack([cosine, sine_wave], 1), jnp.stack([-sine_wave, cosine], 1)], 1
    ).astype(jnp.bfloat16)


def depth_table(retained, length):
    cosine, sine_wave = cos_sin(jnp.arange(retained, dtype=jnp.int32), length)
    return jnp.concatenate([cosine, -sine_wave], 0).astype(jnp.bfloat16)


def gelu_parts(inputs):
    squared = inputs * inputs
    slope = SQRT_TWO_PI * CUBIC_COEF
    tangent = jnp.tanh(inputs * (SQRT_TWO_PI + slope * squared))
    half = 0.5 + 0.5 * tangent
    output = inputs * half
    derivative = half + output * (1.0 - tangent) * (SQRT_TWO_PI + 3.0 * slope * squared)
    return (output, derivative)


def mode_product(coeffs, weights):
    channels = weights.shape[1]
    halves = jnp.einsum("mac,mcj->amj", coeffs, weights, preferred_element_type=jnp.float32)
    real_out = halves[0, :, :channels] - halves[1, :, channels:]
    imag_out = halves[0, :, channels:] + halves[1, :, :channels]
    return jnp.stack([real_out, imag_out], 1).astype(jnp.bfloat16)


def exchange(blocks):
    return lax.all_to_all(blocks, "gx", 0, 0, tiled=True)


def middle_kernel(
    scale, feat_ref, cot_ref, lines_ref, weight_ref, bias_ref, basis_ref, act_ref, up_ref, grad_ref
):
    channels, _, rows, depth_len = feat_ref.shape
    spectral = jnp.dot(
        lines_ref[0].reshape(rows * channels, lines_ref.shape[3]),
        basis_ref[...],
        preferred_element_type=jnp.float32,
    ).reshape(rows, channels, depth_len)
    feats = jnp.swapaxes(feat_ref[:, 0].astype(jnp.float32), 0, 1).astype(jnp.bfloat16)
    cots = jnp.swapaxes(cot_ref[:, 0].astype(jnp.float32), 0, 1)
    acts = []
    for row in range(rows):
        pointwise = jnp.dot(weight_ref[...], feats[row], preferred_element_type=jnp.float32)
        hidden = spectral[row] * scale + pointwise + bias_ref[...]
        activated, derivative = gelu_parts(hidden)
        acts.append(activated)
        up_ref[0, row] = (cots[row] * derivative).astype(jnp.bfloat16)
    act_ref[:, 0] = jnp.swapaxes(jnp.stack(acts, 0), 0, 1).astype(jnp.bfloat16)
    grad = lax.dot_general(
        up_ref[0].reshape(rows * channels, depth_len),
        basis_ref[...],
        (((1,), (1,)), ((), ())),
        preferred_element_type=jnp.float32,
    )
    grad_ref[0] = (grad * scale).astype(jnp.bfloat16).reshape(rows, channels, lines_ref.shape[3])


def final_kernel(up_ref, depth_ref, weight_ref, basis_ref, out_ref):
    _, rows, channels, depth_len = up_ref.shape
    spectral = jnp.dot(
        depth_ref[0].reshape(rows * channels, depth_ref.shape[3]),
        basis_ref[...],
        preferred_element_type=jnp.float32,
    ).reshape(rows, channels, depth_len)
    totals = []
    for row in range(rows):
        back = jnp.dot(weight_ref[...], up_ref[0, row], preferred_element_type=jnp.float32)
        totals.append(spectral[row] + back)
    out_ref[:, 0] = jnp.swapaxes(jnp.stack(totals, 0), 0, 1).astype(jnp.bfloat16)


ROWS = 16


def middle(features, cotangent, lines_back, channel_weight, channel_bias, depth_basis, scale):
    channels, planes, lines, depth_len = features.shape
    parts = lines_back.shape[3]
    field = pl.BlockSpec((channels, 1, ROWS, depth_len), lambda x, y: (0, x, y, 0))
    turned = pl.BlockSpec((1, ROWS, channels, depth_len), lambda x, y: (x, y, 0, 0))
    narrow = pl.BlockSpec((1, ROWS, channels, parts), lambda x, y: (x, y, 0, 0))
    count = features.size
    return pl.pallas_call(
        functools.partial(middle_kernel, scale),
        grid=(planes, lines // ROWS),
        in_specs=[
            field,
            field,
            narrow,
            pl.BlockSpec((channels, channels), lambda x, y: (0, 0)),
            pl.BlockSpec((channels, 1), lambda x, y: (0, 0)),
            pl.BlockSpec((parts, depth_len), lambda x, y: (0, 0)),
        ],
        out_specs=[field, turned, narrow],
        out_shape=[
            jax.ShapeDtypeStruct(features.shape, jnp.bfloat16),
            jax.ShapeDtypeStruct((planes, lines, channels, depth_len), jnp.bfloat16),
            jax.ShapeDtypeStruct((planes, lines, channels, parts), jnp.bfloat16),
        ],
        compiler_params=pltpu.CompilerParams(vmem_limit_bytes=56 * 1024 * 1024),
        cost_estimate=pl.CostEstimate(
            flops=count * 2 * (channels + 2 * parts), bytes_accessed=count * 8, transcendentals=count
        ),
    )(features, cotangent, lines_back, channel_weight, channel_bias[:, None], depth_basis)


def final(upstream, depth_grad, weight_back, depth_basis):
    planes, lines, channels, depth_len = upstream.shape
    parts = depth_grad.shape[3]
    count = upstream.size
    return pl.pallas_call(
        final_kernel,
        grid=(planes, lines // ROWS),
        in_specs=[
            pl.BlockSpec((1, ROWS, channels, depth_len), lambda x, y: (x, y, 0, 0)),
            pl.BlockSpec((1, ROWS, channels, parts), lambda x, y: (x, y, 0, 0)),
            pl.BlockSpec((channels, channels), lambda x, y: (0, 0)),
            pl.BlockSpec((parts, depth_len), lambda x, y: (0, 0)),
        ],
        out_specs=pl.BlockSpec((channels, 1, ROWS, depth_len), lambda x, y: (0, x, y, 0)),
        out_shape=jax.ShapeDtypeStruct((channels, planes, lines, depth_len), jnp.bfloat16),
        compiler_params=pltpu.CompilerParams(vmem_limit_bytes=32 * 1024 * 1024),
        cost_estimate=pl.CostEstimate(
            flops=count * 2 * (channels + parts), bytes_accessed=count * 4, transcendentals=0
        ),
    )(upstream, depth_grad, weight_back, depth_basis)


def plain_body(features, cotangent, spectral_weight, channel_weight, channel_bias):
    channels, planes, lines, depth_len = features.shape
    devices = lax.axis_size("gx")
    all_planes = planes * devices
    owned_modes = spectral_weight.shape[0]
    wave_pairs = MY * MZ
    owned_pairs = owned_modes // MX
    wide = 2 * channels
    forward_scale = 1.0 / math.sqrt(all_planes * lines * depth_len)
    inverse_scale = 1.0 / math.sqrt(MX * wave_pairs)
    weight_scale = math.sqrt(MX * wave_pairs / (all_planes * lines * depth_len))
    depth_basis = depth_table(MZ, depth_len)
    across_y = analysis_pair(freq_index(MY, lines), lines)
    back_y = synthesis_pair(freq_index(MY, lines), lines)
    across_x = analysis_pair(freq_index(MX, all_planes), all_planes)
    back_x = synthesis_pair(freq_index(MX, all_planes), all_planes)

    def to_owners(rows):
        blocks = rows.reshape(devices, owned_pairs * planes, wide)
        return exchange(blocks).reshape(devices, owned_pairs, planes, 2, channels)

    def to_planes(rows):
        blocks = rows.reshape(devices, planes * owned_pairs, wide)
        got = exchange(blocks).reshape(devices, planes, owned_pairs, 2, channels)
        return got.transpose(1, 0, 2, 3, 4).reshape(planes, MY, MZ, 2, channels)

    depth_part = jnp.dot(features, depth_basis.T, preferred_element_type=jnp.float32).astype(
        jnp.bfloat16
    )
    plane_part = jnp.einsum(
        "cxyaz,yabk->kzxbc",
        depth_part.reshape(channels, planes, lines, 2, MZ),
        across_y,
        preferred_element_type=jnp.float32,
    ).astype(jnp.bfloat16)
    gathered = to_owners(plane_part)
    mode_sums = jnp.einsum(
        "sqpac,spabk->qkbc",
        gathered,
        across_x.reshape(devices, planes, 2, 2, MX),
        preferred_element_type=jnp.float32,
    )
    coeffs = (mode_sums * forward_scale).astype(jnp.bfloat16).reshape(owned_modes, 2, channels)
    spectral = mode_product(coeffs, spectral_weight)
    planes_back = jnp.einsum(
        "qkao,kabx->xqbo",
        spectral.reshape(owned_pairs, MX, 2, channels),
        back_x,
        preferred_element_type=jnp.float32,
    ).astype(jnp.bfloat16)
    planes_here = to_planes(planes_back)
    lines_back = (
        jnp.einsum("xkzao,kaby->xyobz", planes_here, back_y, preferred_element_type=jnp.float32)
        .astype(jnp.bfloat16)
        .reshape(planes, lines, channels, 2 * MZ)
    )
    activated, upstream, lines_grad = middle(
        features, cotangent, lines_back, channel_weight, channel_bias, depth_basis, inverse_scale
    )
    rows_grad = jnp.einsum(
        "xyobz,kaby->kzxao",
        lines_grad.reshape(planes, lines, channels, 2, MZ),
        back_y,
        preferred_element_type=jnp.float32,
    ).astype(jnp.bfloat16)
    gathered_grad = to_owners(rows_grad)
    grad_modes = (
        jnp.einsum(
            "sqpbo,kabsp->qkao",
            gathered_grad,
            back_x.reshape(MX, 2, 2, devices, planes),
            preferred_element_type=jnp.float32,
        )
        .astype(jnp.bfloat16)
        .reshape(owned_modes, 2, channels)
    )
    straight = grad_modes.reshape(owned_modes, wide)
    rotated = jnp.concatenate([grad_modes[:, 1], -grad_modes[:, 0]], 1)
    pairs = jnp.stack([straight, rotated], 1)
    coeff_grad = (
        jnp.einsum("mcj,mbj->mbc", spectral_weight, pairs, preferred_element_type=jnp.float32)
        * forward_scale
    ).astype(jnp.bfloat16)
    plane_grad = jnp.einsum(
        "qkbc,xabk->xqac",
        coeff_grad.reshape(owned_pairs, MX, 2, channels),
        across_x,
        preferred_element_type=jnp.float32,
    ).astype(jnp.bfloat16)
    grad_here = to_planes(plane_grad)
    spectral_grad = (
        jnp.einsum("mac,maj->mcj", coeffs, pairs, preferred_element_type=jnp.float32)
        * weight_scale
    ).astype(jnp.bfloat16)
    depth_grad = (
        jnp.einsum("xkzbc,yabk->xycaz", grad_here, across_y, preferred_element_type=jnp.float32)
        .astype(jnp.bfloat16)
        .reshape(planes, lines, channels, 2 * MZ)
    )
    feature_grad = final(upstream, depth_grad, channel_weight.T, depth_basis)
    return (activated, feature_grad, spectral_grad)


MESH = pl.DeviceIdType.MESH
F32 = jnp.float32
BF16 = jnp.bfloat16
MB = 1024 * 1024


def host_cos_sin(wavenum, length):
    angles = (np.outer(wavenum, np.arange(length)) % length).astype(np.float32) * np.float32(
        2.0 * math.pi / length
    )
    return np.cos(angles), np.sin(angles)


def host_freq(retained, length):
    ladder = np.arange(retained)
    return np.where(ladder < retained // 2, ladder, length - retained + ladder)


def host_minus(retained, length):
    cosine, sine = host_cos_sin(host_freq(retained, length), length)
    cosine, sine = cosine.T, sine.T
    return np.stack([np.stack([cosine, -sine], 1), np.stack([sine, cosine], 1)], 1)


def host_plus(retained, length):
    cosine, sine = host_cos_sin(host_freq(retained, length), length)
    return np.stack([np.stack([cosine, sine], 1), np.stack([-sine, cosine], 1)], 1)


def host_tables(devices, lines, depth_len, channels):
    all_planes = 2 * devices
    two = np.eye(2)
    eight = np.eye(8)
    cosine, sine = host_cos_sin(np.arange(MZ), depth_len)
    depth = np.stack([cosine, -sine], 0)
    z_in = np.einsum("akz,cd->czakd", depth, eight).reshape(8 * depth_len, 16 * MZ)
    minus_y = host_minus(MY, lines).reshape(lines, 2, 2, devices, 2)
    y_in = np.einsum("yabdk,xw->dkbwxay", minus_y, two).reshape(8 * devices, 4 * lines)
    groups = channels // 8
    source = np.arange(MZ * channels).reshape(groups, MZ, 8)
    target = source.transpose(1, 0, 2).reshape(-1)
    order = np.zeros((MZ * channels, MZ * channels))
    order[target, np.arange(MZ * channels)] = 1.0
    minus_x = host_minus(MX, all_planes).reshape(devices, 2, 2, 2, MX)
    x_in = np.einsum("sxabk,hg,jl,p->hkjpbsglax", minus_x, two, two, np.ones(2)).reshape(
        16 * MX, 16 * devices
    )
    swapped = np.stack([minus_x[:, :, :, 1], -minus_x[:, :, :, 0]], 3)
    x_turn = np.einsum("sxabk,hg,jl,p->hkjpbsglax", swapped, two, two, np.ones(2)).reshape(
        16 * MX, 16 * devices
    )
    plus_x = host_plus(MX, all_planes).reshape(MX, 2, 2, devices, 2)
    crossed = np.stack([-plus_x[:, :, 1], plus_x[:, :, 0]], 2)
    both = np.stack([plus_x, crossed], 0)
    x_out = np.einsum("rkabsx,pq,jl->prsjbxklqa", both, two, two).reshape(32 * devices, 8 * MX)
    x_back = np.einsum("kabsx,jl,q->sjbxklqa", plus_x, two, np.ones(2)).reshape(
        8 * devices, 8 * MX
    )
    plus_y = host_plus(MY, lines).reshape(devices, 2, 2, 2, lines)
    y_out = np.einsum("skaby,hg,xw->xbhysgkaw", plus_y, two, two).reshape(8 * lines, 16 * devices)
    tables = dict(
        z_in=z_in, z_out=z_in.T, y_in=y_in, order=order, unorder=order.T, x_in=x_in,
        x_turn=x_turn, x_out=x_out, x_back=x_back, y_out=y_out,
    )
    return {name: jnp.asarray(np.ascontiguousarray(t), BF16) for name, t in tables.items()}


def fdot(left, right):
    return jnp.dot(left, right, preferred_element_type=F32)


def greet(devices):
    me, group = lax.axis_index("gx"), lax.axis_index("grp")
    barrier = pltpu.get_barrier_semaphore()

    @pl.loop(1, devices, unroll=True)
    def _(step):
        pl.semaphore_signal(
            barrier, inc=1, device_id=(group, lax.rem(me + step, devices)), device_id_type=MESH
        )

    def arrived():
        pl.semaphore_wait(barrier, devices - 1)

    return arrived


def swap_start(devices, sent, got, send_sem, recv_sem, stage):
    me, group = lax.axis_index("gx"), lax.axis_index("grp")

    def copy(source, landing, target):
        return pltpu.make_async_remote_copy(
            src_ref=source,
            dst_ref=landing,
            send_sem=send_sem.at[stage],
            recv_sem=recv_sem.at[stage],
            device_id=(group, target),
            device_id_type=MESH,
        )

    @pl.loop(1, devices, unroll=True)
    def _(step):
        target = lax.rem(me + step, devices)
        copy(sent.at[target], got.at[me], target).start()

    got[me] = sent[me]
    others = pl.ds(0, devices - 1)
    every = copy(sent.at[others], got.at[others], lax.rem(me + 1, devices))

    def finish():
        every.wait_recv()

    def drained():
        every.wait_send()

    return finish, drained


def to_chunks(devices, lines_ref, y_in, order, sent):
    rows = fdot(y_in[...], lines_ref[...]).astype(BF16)
    rows = fdot(rows, order[...])
    lanes = rows.shape[1]
    halves = [
        rows[:, h * lanes // 2 : (h + 1) * lanes // 2].reshape(devices, 8, lanes // 2)
        for h in range(2)
    ]
    chunk = jnp.concatenate(halves, 1).astype(BF16)
    for u in range(2):
        sent[u] = chunk[:, :, u * lanes // 4 : (u + 1) * lanes // 4]


def mode_block(weights, k_pair, half, pair):
    def one(kx):
        return jnp.concatenate(
            [weights[k2, half * 8 + pair * 2 + parity, kx] for k2 in range(2) for parity in range(2)],
            0,
        )

    return jnp.concatenate([one(2 * k_pair), one(2 * k_pair + 1)], 1)


def iotas():
    row = lax.broadcasted_iota(jnp.int32, (8, 128), 0)
    lane = lax.broadcasted_iota(jnp.int32, (8, 128), 1)
    return row, lane


def weight_copies(weights_hbm, weights, sem):
    def copy(half, pair):
        kz = pl.ds(half * 8 + pair * 2, 2)
        return pltpu.make_async_copy(
            weights_hbm.at[:, kz], weights.at[:, kz], sem.at[half, pair]
        )

    return copy


def fill_kron(channel_weight, out, contract):
    size = out.shape[0]
    channels = channel_weight.shape[0]

    def spread(rows, first, axis):
        shape = (rows, channels) if axis == 0 else (channels, rows)
        long = lax.broadcasted_iota(jnp.int32, shape, axis)
        short = lax.broadcasted_iota(jnp.int32, shape, 1 - axis)
        return jnp.where(long // 16 + first == short, 1.0, 0.0).astype(BF16)

    columns = spread(size, 0, 1)
    line = lax.broadcasted_iota(jnp.int32, (128, size), 0) % 16
    same = line == lax.broadcasted_iota(jnp.int32, (128, size), 1) % 16

    @pl.loop(0, size // 128)
    def _(block):
        rows = lax.dot_general(
            spread(128, block * 8, 0),
            channel_weight[...],
            (((1,), (1 - contract,)), ((), ())),
            preferred_element_type=F32,
        ).astype(BF16)
        out[pl.ds(pl.multiple_of(block * 128, 128), 128), :] = jnp.where(
            same, fdot(rows, columns), 0.0
        ).astype(BF16)


TABLES = (
    "z_in", "y_in", "order", "x_in", "x_out", "y_out", "unorder", "z_out", "x_turn", "x_back",
)
EARLY = 3
LATE = 5
PARTS = 4


def layer_kernel(
    devices, forward_scale, inverse_scale, weight_scale,
    feat_hbm, cot_hbm, weights_hbm, channel_weight, bias, *refs,
):
    number = len(TABLES)
    tables_hbm = dict(zip(TABLES, refs[:number]))
    act, grad, weights, lefts, pairs = refs[number : number + 5]
    tables = dict(zip(TABLES, refs[number + 5 : 2 * number + 5]))
    (
        feat, cot, kron, kron_back, pointwise, lines_part, blocks, spectral,
        up_wide, sent, got, coeffs, modes, turned, mixed,
        feat_sem, load_sem, weight_sem, send_sem, recv_sem,
    ) = refs[2 * number + 5 :]
    channels, planes, lines, depth_len = feat.shape
    groups = channels // 8
    rows = 16
    pieces = feat_sem.shape[0]
    share = channels // pieces

    def load_feat(piece):
        here = pl.ds(piece * share, share)
        return pltpu.make_async_copy(feat_hbm.at[here], feat.at[here], feat_sem.at[piece])

    loads = {
        name: pltpu.make_async_copy(tables_hbm[name], tables[name], load_sem.at[i])
        for i, name in enumerate(TABLES)
    }
    load_cot = pltpu.make_async_copy(cot_hbm, cot, load_sem.at[number])
    loads["z_in"].start()
    for piece in range(pieces):
        load_feat(piece).start()
    for name in TABLES[1:EARLY]:
        loads[name].start()
    arrived = greet(devices)
    weight_copy = weight_copies(weights_hbm, weights, weight_sem)
    loads["z_in"].wait()

    @pl.loop(0, pieces)
    def _(piece):
        load_feat(piece).wait()
        spots = [(local, plane) for local in range(share // 8) for plane in range(planes)]
        wide = [
            jnp.concatenate([feat[piece * share + local * 8 + i, plane] for i in range(8)], 1)
            for local, plane in spots
        ]
        part = fdot(jnp.concatenate(wide, 0), tables["z_in"][...]).astype(BF16)
        for spot, (local, plane) in enumerate(spots):
            group = piece * (share // 8) + local
            for a in range(2):
                lines_part[
                    pl.ds((plane * 2 + a) * lines, lines),
                    pl.ds(pl.multiple_of(group * 128, 128), 128),
                ] = part[spot * lines : (spot + 1) * lines, a * 128 : (a + 1) * 128]

    loads["x_in"].start()
    for pair in range(2):
        for half in range(2):
            weight_copy(half, pair).start()
    for name in TABLES[EARLY + 1 :]:
        loads[name].start()
    for pair in range(2, 4):
        for half in range(2):
            weight_copy(half, pair).start()
    load_cot.start()
    for name in TABLES[1:EARLY]:
        loads[name].wait()
    to_chunks(devices, lines_part, tables["y_in"], tables["order"], sent.at[0])
    arrived()

    def swap(stage, u):
        return swap_start(
            devices, sent.at[stage, u], got.at[stage, u], send_sem, recv_sem, 2 * stage + u
        )

    def lines_of(stage, arrivals):
        for u in range(2):
            arrivals[u][0]()
            to_lines(u, got.at[stage], tables["y_out"], tables["unorder"], spectral.at[0])
        to_blocks(spectral.at[0], blocks)

    ends = [swap(0, 0)]

    def point(block):
        here = pl.ds(pl.multiple_of(block * rows, rows), rows)
        both = jnp.concatenate(
            [feat[:, x, here].reshape(channels * rows, depth_len) for x in range(planes)], 1
        )
        total = fdot(kron[...], both)
        for o in range(channels):
            here = slice(o * rows, (o + 1) * rows)
            pointwise[block, here] = total[here] + bias[o]

    fill_kron(channel_weight, kron, 1)

    @pl.loop(0, 1)
    def _(block):
        point(block)

    ends[0][1]()
    ends.append(swap(0, 1))

    @pl.loop(1, 2)
    def _(block):
        point(block)

    for name in TABLES[EARLY:LATE]:
        loads[name].wait()
    row, lane = iotas()
    own = [(row // 2) == (lane // 64 + 2 * k2) for k2 in range(2)]
    low_tall = lax.broadcasted_iota(jnp.int32, (8 * devices, 128), 1) < 64
    low = lane < 64
    direct = low == ((row // 2) % 2 == 0)
    first_line = row < 4
    zero = jnp.zeros((8, 128), F32)

    for u in range(2):
        ends[u][0]()
        source = got[0, u].reshape(16 * devices, 256)
        coeffs[u] = (fdot(tables["x_in"][...], source) * forward_scale).reshape(2, MX, 8, 256)

        @pl.loop(0, 4, unroll=PARTS)
        def _(part):
            half, local = part // 2, part % 2
            weight_copy(half, 2 * u + local).wait()
            span = pl.ds(pl.multiple_of(local * 128, 128), 128)

            def step(k_pair, carry):
                left = []
                for i in range(2):
                    block = coeffs[u, half, 2 * k_pair + i, :, span]
                    left.append(
                        jnp.concatenate([jnp.where(own[k2], block, 0.0) for k2 in range(2)], 1)
                    )
                left = jnp.concatenate(left, 0).astype(BF16)
                out = fdot(left, mode_block(weights, k_pair, half, 2 * u + local))
                out = jnp.concatenate([out[:8, :128], out[8:, 128:]], 0).astype(BF16)
                mixed[half, pl.ds(pl.multiple_of(k_pair * 16, 16), 16), span] = out
                return carry

            lax.fori_loop(0, MX // 2, step, 0, unroll=16)

        halves = []
        for half in range(2):
            every = fdot(tables["x_out"][...], mixed[half]) * inverse_scale
            size = 8 * devices
            tiles = []
            for local in range(2):
                even, even_x, odd, odd_x = [
                    every[i * size : (i + 1) * size, local * 128 : (local + 1) * 128]
                    for i in range(4)
                ]
                tiles.append(
                    jnp.where(low_tall, even, odd_x)
                    + pltpu.roll(jnp.where(low_tall, odd, even_x), 64, 1)
                )
            halves.append(jnp.concatenate(tiles, 1).reshape(devices, 8, 256))
        sent[1, u] = jnp.concatenate(halves, 1).astype(BF16)
        ends.append(swap(1, u))

    @pl.loop(2, lines // rows)
    def _(block):
        point(block)

    fill_kron(channel_weight, kron_back, 0)

    @pl.loop(0, 2)
    def _(k_half):
        here = pl.ds(k_half * (MX // 2), MX // 2)
        for index in range(8):
            half, u, local = index // 4, (index % 4) // 2, index % 2
            values = coeffs[u, half, here, :, local * 128 : (local + 1) * 128]
            wide = jnp.concatenate(
                [jnp.where(own[k2][None], values, 0.0).reshape(128, 128) for k2 in range(2)], 1
            )
            lefts[index, k_half] = wide.T.astype(BF16)

    load_cot.wait()
    for name in TABLES[LATE:]:
        loads[name].wait()
    lines_of(1, ends[2:4])

    @pl.loop(0, lines // rows, unroll=True)
    def _(block):
        line = pl.ds(pl.multiple_of(block * rows, rows), rows)
        slot = block % 2
        spectral[slot] = fdot(blocks[block], tables["z_out"][...])

        @pl.loop(0, groups, unroll=True)
        def _(group):
            for plane in range(planes):
                here = pl.ds(pl.multiple_of((plane * groups + group) * rows, rows), rows)
                for i in range(8):
                    o = group * 8 + i
                    hidden = (
                        spectral[slot, here, i * 128 : (i + 1) * 128]
                        + pointwise[
                            block,
                            pl.ds(pl.multiple_of(o * rows, rows), rows),
                            plane * 128 : (plane + 1) * 128,
                        ]
                    )
                    activated, derivative = gelu_parts(hidden)
                    act[o, plane, line] = activated.astype(BF16)
                    up_wide[block, here, i * 128 : (i + 1) * 128] = (
                        cot[o, plane, line].astype(F32) * derivative
                    ).astype(BF16)

        part = (fdot(up_wide[block], tables["z_in"][...]) * inverse_scale).astype(BF16)
        for plane in range(planes):
            for a in range(2):
                for group in range(groups):
                    first = (plane * groups + group) * rows
                    lines_part[
                        pl.ds(
                            pl.multiple_of((plane * 2 + a) * lines + block * rows, rows), rows
                        ),
                        group * 128 : (group + 1) * 128,
                    ] = part[first : first + rows, a * 128 : (a + 1) * 128]

    to_chunks(devices, lines_part, tables["y_in"], tables["order"], sent.at[2])
    ends.append(swap(2, 0))

    def point_back(block):
        both = []
        for plane in range(planes):
            tiles = []
            for o in range(channels):
                first = (plane * groups + o // 8) * rows
                tiles.append(
                    up_wide[block, first : first + rows, (o % 8) * 128 : (o % 8 + 1) * 128]
                )
            both.append(jnp.concatenate(tiles, 0))
        pointwise[block] = fdot(kron_back[...], jnp.concatenate(both, 1))

    pl.loop(0, 3)(point_back)
    ends[4][1]()
    ends.append(swap(2, 1))
    pl.loop(3, 4)(point_back)

    for u in range(2):
        ends[4 + u][0]()
        source = got[2, u].reshape(16 * devices, 256)
        modes[...] = fdot(tables["x_in"][...], source).reshape(2, MX, 8, 256)
        turned[...] = fdot(tables["x_turn"][...], source).reshape(2, MX, 8, 256)

        @pl.loop(0, 4, unroll=PARTS)
        def _(part):
            half, local = part // 2, part % 2
            span = pl.ds(pl.multiple_of(local * 128, 128), 128)

            def step(k_pair, carry):
                here = pl.ds(pl.multiple_of(k_pair * 16, 16), 16)
                tiles = [
                    pair_tile(
                        modes[half, 2 * k_pair + i, :, span],
                        turned[half, 2 * k_pair + i, :, span],
                        low,
                        direct,
                    )
                    for i in range(2)
                ]
                pairs[half * 4 + 2 * u + local, here] = jnp.concatenate(tiles, 0).astype(BF16)
                left = jnp.concatenate(
                    [jnp.concatenate([tiles[0], zero], 1), jnp.concatenate([zero, tiles[1]], 1)], 0
                ).astype(BF16)
                out = lax.dot_general(
                    left,
                    mode_block(weights, k_pair, half, 2 * u + local),
                    (((1,), (1,)), ((), ())),
                    preferred_element_type=F32,
                )
                kept = []
                for i in range(2):
                    here_rows = out[8 * i : 8 * i + 8]
                    kept.append(
                        jnp.where(
                            direct,
                            jnp.where(first_line, here_rows[:, :128], here_rows[:, 128:]),
                            0.0,
                        )
                    )
                mixed[half, here, span] = (jnp.concatenate(kept, 0) * forward_scale).astype(BF16)
                return carry

            lax.fori_loop(0, MX // 2, step, 0, unroll=16)

        sent[3, u] = jnp.concatenate(
            [fdot(tables["x_back"][...], mixed[half]).reshape(devices, 8, 256) for half in range(2)],
            1,
        ).astype(BF16)
        ends.append(swap(3, u))

    for index in (0, 1, 4, 5):
        weight_grad_block(
            weight_scale, lefts.at[index], pairs.at[index], weights.at[:, 2 * index : 2 * index + 2]
        )
    lines_of(3, ends[6:8])

    @pl.loop(0, lines // rows, unroll=True)
    def _(block):
        line = pl.ds(pl.multiple_of(block * rows, rows), rows)
        slot = block % 2
        spectral[slot] = fdot(blocks[block], tables["z_out"][...])

        @pl.loop(0, groups, unroll=True)
        def _(group):
            for plane in range(planes):
                here = pl.ds(pl.multiple_of((plane * groups + group) * rows, rows), rows)
                for i in range(8):
                    o = group * 8 + i
                    total = (
                        spectral[slot, here, i * 128 : (i + 1) * 128]
                        + pointwise[
                            block,
                            pl.ds(pl.multiple_of(o * rows, rows), rows),
                            plane * 128 : (plane + 1) * 128,
                        ]
                    )
                    grad[o, plane, line] = total.astype(BF16)

    for end in (ends[1], ends[2], ends[3], ends[5], ends[6], ends[7]):
        end[1]()


def to_lines(u, back, y_out, unorder, total):
    values = fdot(y_out[...], back[u].reshape(-1, 256)).astype(BF16)
    lines = values.shape[0] // 8
    part = 0.0
    for half in range(2):
        rows = jnp.concatenate(
            [values[(2 * i + half) * lines : (2 * i + half + 1) * lines] for i in range(4)], 0
        )
        first = (2 * half + u) * 256
        part = part + fdot(rows, unorder[first : first + 256, :])
    total[...] = part if u == 0 else total[...] + part


def to_blocks(total, blocks):
    size, wide = total.shape
    lines, groups = size // 4, wide // 128
    for plane in range(2):
        for part in range(2):
            for block in range(lines // 16):
                first = (plane * 2 + part) * lines + block * 16
                for group in range(groups):
                    blocks[
                        block,
                        (plane * groups + group) * 16 : (plane * groups + group + 1) * 16,
                        part * 128 : (part + 1) * 128,
                    ] = total[first : first + 16, group * 128 : (group + 1) * 128].astype(BF16)


def pair_tile(straight, other, low, direct):
    return jnp.where(
        direct,
        jnp.where(low, straight, other),
        pltpu.roll(jnp.where(low, other, straight), 64, 1),
    )


def weight_grad_block(weight_scale, left, pairs, out):
    block = lax.broadcasted_iota(jnp.int32, (128, 256), 0) // 8
    side = lax.broadcasted_iota(jnp.int32, (128, 256), 1) // 128

    @pl.loop(0, 2)
    def _(k_half):
        here = pl.ds(pl.multiple_of(k_half * 128, 128), 128)
        right = pairs[here].astype(F32) * weight_scale
        right = jnp.concatenate([right, right], 1)
        for i in range(MX // 4):
            kept = jnp.where(block == 2 * i + side, right, 0.0).astype(BF16)
            total = fdot(left[k_half], kept).astype(BF16)
            for s in range(2):
                for k2 in range(2):
                    for parity in range(2):
                        first = (k2 * 2 + parity) * 64
                        out[k2, parity, k_half * (MX // 2) + 2 * i + s] = total[
                            first : first + 64, s * 128 : (s + 1) * 128
                        ]


def weight_grad_kernel(
    weight_scale, act_in, grad_in, part_in, lefts, pairs, act_out, grad_out, out_hbm, buffer, sem,
    field_sem,
):
    def place(index):
        return out_hbm.at[:, 2 * index : 2 * index + 2]

    copies = [
        pltpu.make_async_copy(
            part_in.at[:, 2 * index : 2 * index + 2], place(index), sem.at[index]
        )
        for index in (0, 1, 4, 5)
    ]
    copies += [
        pltpu.make_async_copy(act_in, act_out, field_sem.at[0]),
        pltpu.make_async_copy(grad_in, grad_out, field_sem.at[1]),
    ]
    for copy in copies:
        copy.start()
    for slot, index in enumerate((2, 3, 6, 7)):
        weight_grad_block(weight_scale, lefts.at[index], pairs.at[index], buffer.at[slot])
        copy = pltpu.make_async_copy(buffer.at[slot], place(index), sem.at[index])
        copy.start()
        copies.append(copy)
    for copy in copies:
        copy.wait()


def vmem(*shape, dtype=BF16):
    return pltpu.VMEM(shape, dtype)


WHOLE = pl.BlockSpec(memory_space=pltpu.VMEM)
ANYWHERE = pl.BlockSpec(memory_space=pl.ANY)


def block_body(features, cotangent, spectral_weight, channel_weight, channel_bias):
    channels, planes, lines, depth_len = features.shape
    devices = lax.axis_size("gx")
    all_planes = planes * devices
    number = MX * MY * MZ
    forward_scale = 1.0 / math.sqrt(all_planes * lines * depth_len)
    inverse_scale = 1.0 / math.sqrt(number)
    weight_scale = math.sqrt(number / (all_planes * lines * depth_len))
    tables = host_tables(devices, lines, depth_len, channels)
    tables = [tables[name] for name in TABLES]
    weights = spectral_weight.reshape(2, MZ, MX, channels, 2 * channels)
    wide = MZ * channels
    rows = 16
    steps = lines // rows
    dma = pltpu.SemaphoreType.DMA
    like = jax.ShapeDtypeStruct(features.shape, BF16)
    lefts = (8, 2, 256, 128)
    pairs = (8, 8 * MX, 128)
    activated, feature_grad, weight_part, left, pair = pl.pallas_call(
        functools.partial(layer_kernel, devices, forward_scale, inverse_scale, weight_scale),
        out_shape=[
            vmem(*features.shape), vmem(*features.shape), vmem(*weights.shape), vmem(*lefts),
            vmem(*pairs),
        ],
        in_specs=[ANYWHERE] * 3
        + [WHOLE, pl.BlockSpec(memory_space=pltpu.SMEM)]
        + [ANYWHERE] * len(tables),
        out_specs=[WHOLE] * 5,
        scratch_shapes=[vmem(*table.shape) for table in tables]
        + [
            vmem(*features.shape),
            vmem(*features.shape),
            vmem(channels * rows, channels * rows),
            vmem(channels * rows, channels * rows),
            vmem(steps, channels * rows, planes * depth_len, dtype=F32),
            vmem(4 * lines, wide),
            vmem(steps, 2 * wide // 8, 256),
            vmem(2, planes * channels * 2, 8 * depth_len, dtype=F32),
            vmem(steps, planes * channels * 2, 8 * depth_len),
            vmem(4, 2, devices, 16, 256),
            vmem(4, 2, devices, 16, 256),
            vmem(2, 2, MX, 8, 256, dtype=F32),
            vmem(2, MX, 8, 256, dtype=F32),
            vmem(2, MX, 8, 256, dtype=F32),
            vmem(2, 8 * MX, 256),
            dma((4,)),
            dma((len(tables) + 1,)),
            dma((2, 4)),
            dma((8,)),
            dma((8,)),
        ],
        compiler_params=pltpu.CompilerParams(
            collective_id=0, has_side_effects=True, vmem_limit_bytes=40 * MB
        ),
        name="layer",
    )(features, cotangent, weights, channel_weight, channel_bias, *tables)
    activated, feature_grad, spectral_grad = pl.pallas_call(
        functools.partial(weight_grad_kernel, weight_scale),
        out_shape=[like, like, jax.ShapeDtypeStruct(weights.shape, BF16)],
        in_specs=[WHOLE] * 5,
        out_specs=[ANYWHERE] * 3,
        scratch_shapes=[
            vmem(4, 2, 2, MX, channels, 2 * channels),
            dma((8,)),
            dma((2,)),
        ],
        compiler_params=pltpu.CompilerParams(vmem_limit_bytes=14 * MB),
        name="weight_grad",
    )(activated, feature_grad, weight_part, left, pair)
    return (activated, feature_grad, spectral_grad.reshape(spectral_weight.shape))


def body(features, cotangent, spectral_weight, channel_weight, channel_bias):
    channels, planes, lines, depth_len = features.shape
    devices = lax.axis_size("gx")
    fits = (
        2 * devices == MY
        and planes == 2
        and channels == 64
        and lines == 64
        and depth_len == 128
        and spectral_weight.shape[0] == 2 * MZ * MX
    )
    chosen = block_body if fits else plain_body
    return chosen(features, cotangent, spectral_weight, channel_weight, channel_bias)


def solution(mesh):
    in_specs = (
        P("grp", "gx", None, None),
        P("grp", "gx", None, None),
        P("gx", None, None),
        P(),
        P(),
    )
    out_specs = (
        P("grp", "gx", None, None),
        P("grp", "gx", None, None),
        P(("grp", "gx"), None, None),
    )
    return jax.shard_map(body, mesh=mesh, in_specs=in_specs, out_specs=out_specs, check_vma=False)
```
